32 devices in a mesh: section: 2 (over x), fsdp: 16 (over z, y, core).
Axes of the slice: x: 2, y: 2, z: 4, core: 2. Of those that a mesh axis runs over, the one named last changes fastest.
Arguments:
- section_inputs: bfloat16 [2, 4, 32, 128, 768], P('section', None, 'fsdp'), may hold values from -6 to 6
- norm_gains: bfloat16 [2, 2, 768], P('section', None, 'fsdp'), may hold values from 0.5 to 1.5
- offsets: bfloat16 [2, 6, 768], P('section', None, 'fsdp'), may hold values from -2 to 2
- attend_weight: bfloat16 [2, 768, 2304], P('section', 'fsdp'), may hold values from -0.21875 to 0.21875
- merge_weight: bfloat16 [2, 768, 768], P('section', 'fsdp'), may hold values from -0.875 to 0.875
- up_weight: bfloat16 [2, 768, 3072], P('section', 'fsdp'), may hold values from -0.21875 to 0.21875
- up_bias: bfloat16 [2, 3072], P('section', 'fsdp'), may hold values from -2 to 2
- down_weight: bfloat16 [2, 3072, 768], P('section', 'fsdp'), may hold values from -0.109375 to 0.109375
Outputs:
- section_outputs: bfloat16 [2, 4, 32, 128, 768], P('section', None, 'fsdp')
- gains_grad: float32 [2, 2, 768], P('section', None, 'fsdp')
- offsets_grad: float32 [2, 6, 768], P('section', None, 'fsdp')
- attend_grad: float32 [2, 768, 2304], P('section', 'fsdp')
- merge_grad: float32 [2, 768, 768], P('section', 'fsdp')
- up_grad: float32 [2, 768, 3072], P('section', 'fsdp')
- bias_grad: float32 [2, 3072], P('section', 'fsdp')
- down_grad: float32 [2, 3072, 768], P('section', 'fsdp')
The draws below stay inside these ranges and needn't reach their ends.
All inputs are finite; a program needn't handle non-finite values.
Results may differ from the reference program's by a relative error of at most 0.009.
Values may be sent and summed in bfloat16 or wider, within the bound.
A program may use at most 256 MiB of HBM per device.

```python
import math
import jax
import jax.numpy as jnp
from jax import lax

D = 768
HEADS = 12
HEAD_DIM = 64
FF = 3072
LEN = 128
MICRO = 4
CLIPS = 32
LAYERS = 2


def spiked(array, stream_key, source, target, blocks, factor):
    owner, partner = [(jnp.arange(array.shape[position]) // (array.shape[position] // blocks)).reshape([-1 if axis == position else 1 for axis in range(array.ndim)]) for position in (source, target)]
    chosen = jax.random.permutation(stream_key, blocks)[partner]
    strong = (owner == chosen) | (owner == (partner + blocks // 2) % blocks)
    return jnp.where(strong, factor * array, array)


def block_scale(rng, dims, shards, least, high):
    gain, own = 1.0, jax.random.fold_in(rng, 6)
    for position, blocks in shards:
        steps = jnp.exp(jax.random.uniform(jax.random.fold_in(own, position), (blocks,), jnp.float32, least / len(shards), high / len(shards)))
        gain = gain * jnp.repeat(steps, dims[position] // blocks).reshape([-1 if axis == position else 1 for axis in range(len(dims))])
    return gain


def bell_draw(stream_key, dims, width, reach, split=(), held_as=jnp.bfloat16):
    entries = jax.random.normal(stream_key, dims, jnp.float32) * width
    if len(split) > 0:
        entries = block_scale(stream_key, dims, split, -0.22, 0.18) * entries
    return jnp.clip(entries, min=-reach, max=reach).astype(held_as)


def noise_with(stream_key, shape, width, reach, split, heavy, held_as=jnp.bfloat16):
    result = width * jax.random.normal(stream_key, shape, jnp.float32)
    if split:
        result = result * block_scale(stream_key, shape, split, -0.22, 0.18)
    return jnp.clip(spiked(result, jax.random.fold_in(stream_key, 3), *heavy), -reach, reach).astype(held_as)


def setup_inputs(seed: int = 0) -> dict:
    streams_of = jax.random.split(jax.random.key(seed), 9)
    section_inputs = noise_with(streams_of[0], (2, MICRO, CLIPS, LEN, D), 1.0, 6.0, ((0, 2), (2, 16)), (2, 4, 16, 2.0))
    norm_gains = jnp.clip(1.0 + 0.1 * jax.random.normal(streams_of[1], (LAYERS, 2, D), jnp.float32), 0.5, 1.5).astype(jnp.bfloat16)
    offsets = bell_draw(streams_of[2], (LAYERS, 6, D), 0.3, 2.0, ((0, 2), (2, 16)))
    attend_weight = bell_draw(streams_of[3], (LAYERS, D, 3 * D), D ** -0.5, 0.21875, ((0, 2), (1, 16)))
    merge_weight = bell_draw(streams_of[4], (LAYERS, D, D), (D // 16) ** -0.5, 0.875, ((0, 2), (1, 16)))
    up_weight = bell_draw(streams_of[5], (LAYERS, D, FF), D ** -0.5, 0.21875, ((0, 2), (1, 16)))
    up_bias = bell_draw(streams_of[6], (LAYERS, FF), 0.3, 2.0, ((0, 2), (1, 16)))
    down_weight = bell_draw(streams_of[7], (LAYERS, FF, D), FF ** -0.5, 0.109375, ((0, 2), (1, 16)))
    return dict(section_inputs=section_inputs, norm_gains=norm_gains, offsets=offsets, attend_weight=attend_weight, merge_weight=merge_weight, up_weight=up_weight, up_bias=up_bias, down_weight=down_weight)


@jax.custom_vjp
def low(v):
    return lax.optimization_barrier(v.astype(jnp.bfloat16)).astype(jnp.float32)

@jax.custom_vjp
def low_back(v):
    return v

def low_keep(v):
    return (low(v), None)

def low_pass(kept, grad):
    return (grad,)

def back_keep(v):
    return (v, None)

def back_low(kept, grad):
    return (low(grad),)
low.defvjp(low_keep, low_pass)
low_back.defvjp(back_keep, back_low)
epsilon = 1e-05
HIGHEST = lax.Precision.HIGHEST

def product(spec, left, right):
    return jnp.einsum(spec, left, right, precision=HIGHEST)

def normalize(features, gain_row, offset):
    centred = features - lax.optimization_barrier(jnp.mean(features, axis=-1, keepdims=True))
    spread = lax.optimization_barrier(jnp.mean(centred * centred, axis=-1, keepdims=True))
    return centred * lax.rsqrt(spread + epsilon) * gain_row + offset

def encoder_layer(hidden, gain_rows, offset_rows, attend_weight, merge_weight, up_weight, up_bias, down_weight):
    clip_count = hidden.shape[0]
    normed = low(normalize(hidden, gain_rows[0], offset_rows[0]))
    projected = low_back(product('gld,de->gle', normed, attend_weight))
    query_heads = low(projected[..., :D] + offset_rows[2]).reshape(clip_count, LEN, HEADS, HEAD_DIM)
    key_heads = low(projected[..., D:2 * D]).reshape(clip_count, LEN, HEADS, HEAD_DIM)
    value_heads = low(projected[..., 2 * D:] + offset_rows[3]).reshape(clip_count, LEN, HEADS, HEAD_DIM)
    scores = low_back(float(HEAD_DIM) ** (-0.5) * product('glhe,gmhe->ghlm', query_heads, key_heads))
    row_peak = lax.optimization_barrier(jnp.max(scores, axis=-1, keepdims=True))
    exponent = jnp.exp(scores - row_peak)
    probability = low(exponent / lax.optimization_barrier(jnp.sum(exponent, axis=-1, keepdims=True)))
    attended = low(low_back(product('ghlm,gmhe->glhe', probability, value_heads))).reshape(clip_count, LEN, D)
    middle = hidden + low_back(product('gld,de->gle', attended, merge_weight)) + offset_rows[4]
    normed_two = low(normalize(middle, gain_rows[1], offset_rows[1]))
    raised = low_back(product('gld,df->glf', normed_two, up_weight)) + up_bias
    activated = low(jax.nn.gelu(raised, approximate=False))
    return middle + low_back(product('glf,fd->gld', activated, down_weight)) + offset_rows[5]

def network(block, params):
    first_layer = encoder_layer(block, *[tensor[0] for tensor in params])
    between = low(low_back(first_layer))
    return encoder_layer(between, *[tensor[1] for tensor in params])

def reference(section_inputs, norm_gains, offsets, attend_weight, merge_weight, up_weight, up_bias, down_weight):
    params = tuple((tensor.astype(jnp.float32) for tensor in (norm_gains, offsets, attend_weight, merge_weight, up_weight, up_bias, down_weight)))
    clips_all = MICRO * CLIPS
    group_size = math.gcd(clips_all, max(1, 4096 // LEN))
    inputs = section_inputs[0].astype(jnp.float32).reshape(clips_all // group_size, group_size, LEN, D)
    cotangent = section_inputs[1].astype(jnp.float32).reshape(clips_all // group_size, group_size, LEN, D)
    checked = jax.checkpoint(network)

    def forward(blocks, weights):
        return lax.map(lambda block: checked(block, weights), blocks)
    outputs, pullback = jax.vjp(forward, inputs, params)
    in_grad, grads = pullback(cotangent)
    input_grad_rows = in_grad.reshape(MICRO, CLIPS, LEN, D)
    output_rows = outputs.reshape(MICRO, CLIPS, LEN, D)
    section_outputs = jnp.stack([input_grad_rows, output_rows]).astype(jnp.bfloat16)
    return (section_outputs, grads[0], grads[1], grads[2], grads[3], grads[4], grads[5], grads[6])
```

```python
import functools

import jax
import jax.numpy as jnp
from jax import lax
from jax.experimental import pallas as pl
from jax.experimental.pallas import tpu as pltpu
from jax.sharding import PartitionSpec as P

MESH = pl.DeviceIdType.MESH


SIDE, ACROSS, UP, DOWN = range(4)


class Sends:
    def __init__(self):
        self.items = []

    def start(self, copy, when):
        if when is None:
            copy.start()
        else:
            pl.when(when)(copy.start)
        self.items.append((copy, when))

    def drain(self):
        for copy, when in self.items:
            if when is None:
                copy.wait_send()
            else:
                pl.when(when)(copy.wait_send)


def place():
    section, mine = lax.axis_index("section"), lax.axis_index("fsdp")
    return section, mine, lax.div(mine, 4), lax.rem(lax.div(mine, 2), 2), lax.rem(mine, 2)


def greet(section, mine, level, levels):
    barrier = pltpu.get_barrier_semaphore()

    def hello(target):
        pl.semaphore_signal(barrier, inc=1, device_id=(section, target), device_id_type=MESH)

    hello(mine ^ 1)
    hello(mine ^ 2)
    pl.when(level > 0)(lambda: hello(mine - 4))
    pl.when(level < levels - 1)(lambda: hello(mine + 4))
    ends = (level == 0).astype(jnp.int32) + (level == levels - 1).astype(jnp.int32)
    pl.semaphore_wait(barrier, 4 - ends)


def gather_kernel(levels, kinds, *refs):
    count = len(kinds)
    shards, wholes = refs[:count], refs[count : 2 * count]
    send_sem, recv_sem, local_sem = refs[2 * count :]
    section, mine, level, row, core = place()
    greet(section, mine, level, levels)
    has_up, has_down = level < levels - 1, level > 0
    targets = {SIDE: mine ^ 1, ACROSS: mine ^ 2, UP: mine + 4, DOWN: mine - 4}
    sends = Sends()

    def send(chunk, block, way, own=False, when=None):
        copy = pltpu.make_async_remote_copy(
            src_ref=shards[chunk] if own else wholes[chunk].at[block],
            dst_ref=wholes[chunk].at[block],
            send_sem=send_sem.at[chunk, block, way],
            recv_sem=recv_sem.at[chunk, block],
            device_id=(section, targets[way]),
            device_id_type=MESH,
        )
        sends.start(copy, when)

    def arrived(chunk, block):
        pltpu.make_async_remote_copy(
            src_ref=wholes[chunk].at[block],
            dst_ref=wholes[chunk].at[block],
            send_sem=send_sem.at[chunk, block, 0],
            recv_sem=recv_sem.at[chunk, block],
            device_id=(section, mine),
            device_id_type=MESH,
        ).wait_recv()

    def both(one, two):
        return jnp.logical_and(one, two)

    def guarded(when, action):
        pl.when(when)(action)

    local = []
    for chunk in range(count):
        copy = pltpu.make_async_copy(shards[chunk], wholes[chunk].at[mine], local_sem.at[chunk])
        copy.start()
        local.append(copy)
    for chunk in range(count):
        send(chunk, mine, ACROSS, own=True)
        send(chunk, mine, UP, own=True, when=has_up)
        send(chunk, mine, DOWN, own=True, when=has_down)
        send(chunk, mine, SIDE, own=True)

    def block_of(block_level, block_row, block_core):
        return block_level * 4 + block_row * 2 + block_core

    for chunk in range(count):
        if kinds[chunk] == "across":
            block = mine ^ 2
            arrived(chunk, block)
            send(chunk, block, UP, when=has_up)
            send(chunk, block, DOWN, when=has_down)
            send(chunk, block, SIDE)

    def across_arrivals(distance, chunk):
        if kinds[chunk] == "across":
            return
        if distance == 0:
            arrived(chunk, mine ^ 2)
            send(chunk, mine ^ 2, SIDE)
            return
        for sign in (-1, 1):
            other = level + sign * distance
            here = other >= 0 if sign < 0 else other < levels
            block = block_of(other, 1 - row, core)
            pl.when(here)(functools.partial(arrived, chunk, block))
            send(chunk, block, SIDE, when=here)

    for distance in range(1, levels):
        for chunk in range(count):
            rows = (row,) if kinds[chunk] == "level" else (row, 1 - row)
            for block_row in rows:
                for sign in (-1, 1):
                    other = level + sign * distance
                    here = other >= 0 if sign < 0 else other < levels
                    onward = has_up if sign < 0 else has_down
                    block = block_of(other, block_row, core)
                    pl.when(here)(functools.partial(arrived, chunk, block))
                    if distance < levels - 1:
                        send(chunk, block, UP if sign < 0 else DOWN, when=both(here, onward))
                    if kinds[chunk] == "level":
                        send(chunk, block, ACROSS, when=here)
                    send(chunk, block, SIDE, when=here)
            across_arrivals(distance - 1, chunk)
    for chunk in range(count):
        across_arrivals(levels - 1, chunk)
    for chunk in range(count):
        for block_level in range(levels):
            for block_row in range(2):
                arrived(chunk, block_of(block_level, block_row, 1 - core))
    for copy in local:
        copy.wait()
    sends.drain()


def gather_all(shards, kinds, ways, collective_id):
    levels = ways // 4
    count = len(shards)
    return pl.pallas_call(
        functools.partial(gather_kernel, levels, kinds),
        out_shape=[jax.ShapeDtypeStruct((ways,) + s.shape, s.dtype) for s in shards],
        in_specs=[pl.BlockSpec(memory_space=pl.ANY)] * count,
        out_specs=[pl.BlockSpec(memory_space=pl.ANY)] * count,
        scratch_shapes=[
            pltpu.SemaphoreType.DMA((count, ways, 4)),
            pltpu.SemaphoreType.DMA((count, ways)),
            pltpu.SemaphoreType.DMA((count,)),
        ],
        compiler_params=pltpu.CompilerParams(collective_id=collective_id, has_side_effects=True),
    )(*shards)


LEVELS_FIRST, ACROSS_FIRST = 0, 1


class Chunk:
    def __init__(self, levels, order, refs, sems, where):
        self.levels, self.order = levels, order
        self.part, self.from_side, self.from_across, self.from_below, self.from_above = refs
        (
            self.side_out,
            self.side_in,
            self.across_out,
            self.across_in,
            self.up_out,
            self.up_in,
            self.down_out,
            self.down_in,
        ) = sems
        self.section, self.mine, self.level, self.row, self.core = where

    def copy(self, source, target, out_sem, in_sem, device):
        return pltpu.make_async_remote_copy(
            src_ref=source,
            dst_ref=target,
            send_sem=out_sem,
            recv_sem=in_sem,
            device_id=(self.section, device),
            device_id_type=MESH,
        )

    def block(self, level, row, core):
        return level * 4 + row * 2 + core

    def side(self, pair):
        return self.copy(
            self.part.at[pair * 2 + 1 - self.core],
            self.from_side.at[pair],
            self.side_out.at[pair],
            self.side_in.at[pair],
            self.mine ^ 1,
        )

    def across(self, level, slot):
        return self.copy(
            self.part.at[self.block(level, 1 - self.row, self.core)],
            self.from_across.at[slot],
            self.across_out.at[slot],
            self.across_in.at[slot],
            self.mine ^ 2,
        )

    def up(self, row, slot, level):
        return self.copy(
            self.part.at[self.block(level, row, self.core)],
            self.from_below.at[slot, level],
            self.up_out.at[slot, level],
            self.up_in.at[slot, level],
            self.mine + 4,
        )

    def down(self, row, slot, level):
        return self.copy(
            self.part.at[self.block(level, row, self.core)],
            self.from_above.at[slot, level],
            self.down_out.at[slot, level],
            self.down_in.at[slot, level],
            self.mine - 4,
        )

    def add(self, block, term):
        total = self.part[block].astype(jnp.float32) + term.astype(jnp.float32)
        self.part[block] = total.astype(self.part.dtype)

    def send_side(self):
        @pl.loop(0, self.levels * 2)
        def _(pair):
            self.side(pair).start()

    def join_side(self):
        for other in (True, False):
            row = 1 - self.row if other else self.row

            @pl.loop(0, self.levels)
            def _(level):
                pair = level * 2 + row
                self.side(pair).wait_recv()
                self.add(pair * 2 + self.core, self.from_side[pair])
                if other and self.order == ACROSS_FIRST:
                    self.across(level, level).start()

    def join_across(self):
        @pl.loop(0, self.levels)
        def _(level):
            self.across(level, level).wait_recv()
            self.add(self.block(level, self.row, self.core), self.from_across[level])

    def rows(self):
        return ((0, self.row), (1, 1 - self.row)) if self.order == LEVELS_FIRST else ((0, self.row),)

    def chain_start(self):
        for slot, row in self.rows():
            for target in range(self.levels):
                if target:
                    pl.when(self.level == 0)(self.up(row, slot, self.levels - target).start)
                    pl.when(self.level == self.levels - 1)(self.down(row, slot, target - 1).start)

    def chain_pass(self, distance):
        last = self.levels - 1
        for slot, row in self.rows():
            for target in range(last, 0, -1):
                if target > distance:

                    @pl.when(self.level == distance)
                    def _():
                        self.up(row, slot, target).wait_recv()
                        self.add(self.block(target, row, self.core), self.from_below[slot, target])
                        self.up(row, slot, target).start()

            for target in range(last):
                if target < last - distance:

                    @pl.when(self.level == last - distance)
                    def _():
                        self.down(row, slot, target).wait_recv()
                        self.add(self.block(target, row, self.core), self.from_above[slot, target])
                        self.down(row, slot, target).start()

    def chain_end(self, out):
        last = self.levels - 1
        for slot, row in reversed(self.rows()):
            block = self.block(self.level, row, self.core)

            @pl.when(self.level > 0)
            def _():
                self.up(row, slot, self.level).wait_recv()
                self.add(block, self.from_below[slot, self.level])

            @pl.when(self.level < last)
            def _():
                self.down(row, slot, self.level).wait_recv()
                self.add(block, self.from_above[slot, self.level])

            if slot == 1:
                self.across(self.level, 0).start()
        if self.order == ACROSS_FIRST:
            out[...] = self.part[self.mine].astype(jnp.float32)

    def finish(self, out):
        if self.order == LEVELS_FIRST:
            self.across(self.level, 0).wait_recv()
            out[...] = self.part[self.mine].astype(jnp.float32) + self.from_across[0].astype(jnp.float32)

    def drain(self):
        @pl.loop(0, self.levels * 2)
        def _(pair):
            self.side(pair).wait_send()

        if self.order == ACROSS_FIRST:

            @pl.loop(0, self.levels)
            def _(level):
                self.across(level, level).wait_send()

        else:
            self.across(self.level, 0).wait_send()
        for slot, row in self.rows():
            for target in range(self.levels):
                pl.when(self.level < target)(self.up(row, slot, target).wait_send)
                pl.when(self.level > target)(self.down(row, slot, target).wait_send)


def chunk_scratch(levels, order, rows, cols, dtype):
    block = (rows, cols)
    slots = 2 if order == LEVELS_FIRST else 1
    crossing = 1 if order == LEVELS_FIRST else levels
    buffers = [
        pltpu.VMEM((levels * 4,) + block, dtype),
        pltpu.VMEM((levels * 2,) + block, dtype),
        pltpu.VMEM((crossing,) + block, dtype),
        pltpu.VMEM((slots, levels) + block, dtype),
        pltpu.VMEM((slots, levels) + block, dtype),
    ]
    dma = pltpu.SemaphoreType.DMA
    sems = [dma((levels * 2,))] * 2 + [dma((crossing,))] * 2 + [dma((slots, levels))] * 4
    return buffers + sems


CHUNK_REFS = 13


def weights_kernel(levels, plan, *refs):
    inputs, refs = refs[:9], refs[9:]
    outs, refs = refs[:6], refs[6:]
    wide_one, narrow_one, wide_two, narrow_two, turned, load_sem = refs[:6]
    refs = refs[6:]
    where = place()
    section, mine, level, row, core = where
    normed, attended, normed_two, activated, joined, middle, raised, low, vectors = inputs
    attend_out, merge_out, up_out, down_out, vector_out = outs[0], outs[1], outs[2], outs[3], outs[4]
    chunks = []
    for index, (name, order, rows, cols, dtype) in enumerate(plan):
        held = refs[index * CHUNK_REFS : (index + 1) * CHUNK_REFS]
        chunks.append(Chunk(levels, order, held[:5], held[5:], where))
    down_a, down_b, up_a, up_b, attend_a, attend_b, merge, vector = chunks
    width = normed.shape[1]

    def load(source, target, index):
        copy = pltpu.make_async_copy(source, target, load_sem.at[index])
        copy.start()
        return copy

    loads_down = [load(activated, wide_one, 0), load(low, narrow_one, 1)]
    loads_up = [load(normed_two, narrow_two, 2), load(raised, wide_two, 3)]
    load_vector = load(vectors, vector.part, 4)
    greet(section, mine, level, levels)

    for copy in loads_down:
        copy.wait()
    pair_cols = 2 * down_a.part.shape[1]
    half = down_a.part.shape[2]
    shard = down_a.part.shape[1]

    @pl.loop(0, levels * 2)
    def _(pair):
        tile = wide_one[:, pl.ds(pl.multiple_of(pair * pair_cols, 128), pair_cols)]
        for which, chunk in enumerate((down_a, down_b)):
            product = lax.dot_general(
                tile,
                narrow_one[:, which * half : (which + 1) * half],
                (((0,), (0,)), ((), ())),
                preferred_element_type=jnp.float32,
            ).astype(chunk.part.dtype)
            chunk.part[pair * 2] = product[:shard]
            chunk.part[pair * 2 + 1] = product[shard:]
            chunk.side(pair).start()

    load_vector.wait()
    vector.send_side()
    down_a.join_side()
    down_a.chain_start()
    down_b.join_side()
    vector.join_side()

    def turn(source):
        turned[...] = source[...].T

    def columns(source, start, chunk):
        cols = chunk.part.shape[2]
        step = 128 * max(d for d in (1, 2, 3) if cols % (128 * d) == 0)

        @pl.loop(0, cols // step)
        def _(index):
            at = pl.multiple_of(index * step, 128)
            product = jnp.dot(
                turned[...],
                source[:, pl.ds(pl.multiple_of(start + at, 128), step)],
                preferred_element_type=jnp.float32,
            )
            blocks = chunk.part.shape[0]
            chunk.part[:, :, pl.ds(at, step)] = product.astype(chunk.part.dtype).reshape(
                blocks, width // blocks, step
            )

        chunk.send_side()

    for copy in loads_up:
        copy.wait()
    turn(narrow_two)
    columns(wide_two, 0, up_a)
    loads_attend = [load(normed, narrow_one, 0), load(joined, wide_one.at[:, : joined.shape[1]], 1)]
    columns(wide_two, up_a.part.shape[2], up_b)
    loads_merge = [load(attended, narrow_two, 2), load(middle, wide_two.at[:, :width], 3)]
    up_a.join_side()
    down_a.chain_pass(1)
    up_b.join_side()
    for copy in loads_attend:
        copy.wait()
    turn(narrow_one)
    columns(wide_one, 0, attend_a)
    down_a.chain_pass(2)
    down_b.join_across()
    down_b.chain_start()
    vector.join_across()
    vector.chain_start()
    columns(wide_one, attend_a.part.shape[2], attend_b)
    attend_a.join_side()
    for copy in loads_merge:
        copy.wait()
    turn(narrow_two)
    columns(wide_two, 0, merge)
    attend_b.join_side()
    down_b.chain_pass(1)
    merge.join_side()
    down_a.chain_end(None)
    up_a.join_across()
    up_a.chain_start()
    down_b.chain_pass(2)
    vector.chain_pass(1)
    up_a.chain_pass(1)
    up_b.join_across()
    up_b.chain_start()
    vector.chain_pass(2)
    down_b.chain_end(down_out.at[:, half:])
    up_a.chain_pass(2)
    up_b.chain_pass(1)
    attend_a.join_across()
    attend_a.chain_start()
    vector.chain_end(vector_out)
    up_a.chain_end(up_out.at[:, : up_a.part.shape[2]])
    up_b.chain_pass(2)
    attend_a.chain_pass(1)
    attend_b.join_across()
    attend_b.chain_start()
    up_b.chain_end(up_out.at[:, up_a.part.shape[2] :])
    attend_a.chain_pass(2)
    attend_b.chain_pass(1)
    merge.join_across()
    merge.chain_start()
    attend_a.chain_end(attend_out.at[:, : attend_a.part.shape[2]])
    attend_b.chain_pass(2)
    merge.chain_pass(1)
    attend_b.chain_end(attend_out.at[:, attend_a.part.shape[2] :])
    merge.chain_pass(2)
    down_a.finish(down_out.at[:, :half])
    merge.chain_end(merge_out)
    for chunk in chunks:
        chunk.drain()


def reduce_weights(states, vectors, ways, collective_id):
    normed, attended, normed_two, activated, joined, middle, raised, low = states
    levels = ways // 4
    total_rows, width = normed.shape
    wide = activated.shape[1]
    rows, shard = width // ways, wide // ways
    low_type = jnp.bfloat16
    plan = [
        ("down_a", LEVELS_FIRST, shard, width // 2, low_type),
        ("down_b", ACROSS_FIRST, shard, width // 2, low_type),
        ("up_a", ACROSS_FIRST, rows, wide // 2, low_type),
        ("up_b", ACROSS_FIRST, rows, wide // 2, low_type),
        ("attend_a", ACROSS_FIRST, rows, 3 * width // 2, low_type),
        ("attend_b", ACROSS_FIRST, rows, 3 * width // 2, low_type),
        ("merge", ACROSS_FIRST, rows, width, low_type),
        ("vector", ACROSS_FIRST, vectors.shape[1], vectors.shape[2], jnp.float32),
    ]
    scratch = [
        pltpu.VMEM((total_rows, wide), low_type),
        pltpu.VMEM((total_rows, width), low_type),
        pltpu.VMEM((total_rows, wide), low_type),
        pltpu.VMEM((total_rows, width), low_type),
        pltpu.VMEM((width, total_rows), low_type),
        pltpu.SemaphoreType.DMA((5,)),
    ]
    for name, order, r, c, dtype in plan:
        scratch += chunk_scratch(levels, order, r, c, dtype)
    f32 = jnp.float32
    vmem = pl.BlockSpec(memory_space=pltpu.VMEM)
    return pl.pallas_call(
        functools.partial(weights_kernel, levels, plan),
        out_shape=[
            jax.ShapeDtypeStruct((rows, 3 * width), f32),
            jax.ShapeDtypeStruct((rows, width), f32),
            jax.ShapeDtypeStruct((rows, wide), f32),
            jax.ShapeDtypeStruct((shard, width), f32),
            jax.ShapeDtypeStruct(vectors.shape[1:], f32),
            jax.ShapeDtypeStruct((8, 128), f32),
        ],
        in_specs=[pl.BlockSpec(memory_space=pl.ANY)] * 9,
        out_specs=[vmem] * 6,
        scratch_shapes=scratch,
        compiler_params=pltpu.CompilerParams(
            collective_id=collective_id, has_side_effects=True, vmem_limit_bytes=62 * 2**20
        ),
    )(*states, vectors)


HEADS = 12
HEAD_DIM = 64


epsilon = 1e-05


def from_behind(block, axis, distance):
    devices = range(lax.axis_size(axis))
    route = [(i - distance, i) for i in devices if i - distance in devices]
    return lax.ppermute(block, axis, route)


def normalize(features, gain_row, offset):
    centred = features - jnp.mean(features, axis=-1, keepdims=True)
    spread = jnp.mean(centred * centred, axis=-1, keepdims=True)
    return centred * lax.rsqrt(spread + epsilon) * gain_row + offset


def gelu_exact(features):
    return jax.nn.gelu(features, approximate=False)


def split_heads(matrix, clip_count):
    return matrix.reshape(clip_count, matrix.shape[0] // clip_count, HEADS, HEAD_DIM)


def layer_forward(hidden, weights, clip_count):
    attend_weight, merge_weight, up_weight, down_weight, gain_rows, offset_rows, up_bias = weights
    gain_rows = gain_rows.astype(jnp.float32)
    offset_rows = offset_rows.astype(jnp.float32)
    row_count, model_width = hidden.shape
    score_scale = HEAD_DIM ** (-0.5)
    normed = normalize(hidden, gain_rows[0], offset_rows[0]).astype(jnp.bfloat16)
    projected = jnp.dot(normed, attend_weight, preferred_element_type=jnp.float32)
    query_heads = split_heads(
        (projected[:, :model_width] + offset_rows[2]).astype(jnp.bfloat16), clip_count
    )
    key_heads = split_heads(
        projected[:, model_width : 2 * model_width].astype(jnp.bfloat16), clip_count
    )
    value_heads = split_heads(
        (projected[:, 2 * model_width :] + offset_rows[3]).astype(jnp.bfloat16), clip_count
    )
    scores = (
        jnp.einsum("clhe,cmhe->chlm", query_heads, key_heads, preferred_element_type=jnp.float32)
        * score_scale
    )
    row_peak = jnp.max(scores, axis=-1, keepdims=True)
    exponent = jnp.exp(scores - row_peak)
    row_total = jnp.sum(exponent, axis=-1, keepdims=True)
    probability = (exponent / row_total).astype(jnp.bfloat16)
    log_total = (row_peak + jnp.log(row_total))[..., 0]
    attended = jnp.einsum(
        "chlm,cmhe->clhe", probability, value_heads, preferred_element_type=jnp.float32
    )
    attended = attended.reshape(row_count, model_width).astype(jnp.bfloat16)
    middle = (
        hidden
        + jnp.dot(attended, merge_weight, preferred_element_type=jnp.float32)
        + offset_rows[4]
    )
    normed_two = normalize(middle, gain_rows[1], offset_rows[1]).astype(jnp.bfloat16)
    raised = jnp.dot(normed_two, up_weight, preferred_element_type=jnp.float32) + up_bias.astype(
        jnp.float32
    )
    activated = gelu_exact(raised).astype(jnp.bfloat16)
    result = (
        middle
        + jnp.dot(activated, down_weight, preferred_element_type=jnp.float32)
        + offset_rows[5]
    )
    saved_state = (
        hidden,
        normed,
        query_heads,
        key_heads,
        value_heads,
        log_total,
        attended,
        middle,
        normed_two,
        raised,
        activated,
    )
    return (result, saved_state)


def layer_backward(out_grad, saved_state, weights, clip_count):
    attend_weight, merge_weight, up_weight, down_weight, gain_rows, offset_rows, up_bias = weights
    gain_rows = gain_rows.astype(jnp.float32)
    offset_rows = offset_rows.astype(jnp.float32)
    (
        hidden,
        normed,
        query_heads,
        key_heads,
        value_heads,
        log_total,
        attended,
        middle,
        normed_two,
        raised,
        activated,
    ) = saved_state
    row_count, model_width = hidden.shape
    score_scale = HEAD_DIM ** (-0.5)
    low_grad = out_grad.astype(jnp.bfloat16)
    last_bias = jnp.sum(out_grad, axis=0)
    act_grad = jnp.einsum("td,fd->tf", low_grad, down_weight, preferred_element_type=jnp.float32)
    raised_grad = jax.vjp(gelu_exact, raised)[1](act_grad)[0]
    up_bias_term = jnp.sum(raised_grad, axis=0)
    raised_low = raised_grad.astype(jnp.bfloat16)
    normed_two_grad = jnp.einsum(
        "tf,df->td", raised_low, up_weight, preferred_element_type=jnp.float32
    )
    second_back = jax.vjp(normalize, middle, gain_rows[1], offset_rows[1])[1]
    middle_part, gain_two, offset_two = second_back(normed_two_grad)
    middle_grad = out_grad + middle_part
    merge_bias = jnp.sum(middle_grad, axis=0)
    middle_low = middle_grad.astype(jnp.bfloat16)
    attended_grad = jnp.einsum(
        "te,de->td", middle_low, merge_weight, preferred_element_type=jnp.float32
    )
    attended_grad = split_heads(attended_grad.astype(jnp.bfloat16), clip_count)
    scores = (
        jnp.einsum("clhe,cmhe->chlm", query_heads, key_heads, preferred_element_type=jnp.float32)
        * score_scale
    )
    probability = jnp.exp(scores - log_total[..., None])
    prob_grad = jnp.einsum(
        "clhe,cmhe->chlm", attended_grad, value_heads, preferred_element_type=jnp.float32
    )
    value_grad = jnp.einsum(
        "chlm,clhe->cmhe",
        probability.astype(jnp.bfloat16),
        attended_grad,
        preferred_element_type=jnp.float32,
    )
    score_grad = probability * (
        prob_grad - jnp.sum(prob_grad * probability, axis=-1, keepdims=True)
    )
    score_grad = score_grad.astype(jnp.bfloat16)
    query_grad = (
        jnp.einsum("chlm,cmhe->clhe", score_grad, key_heads, preferred_element_type=jnp.float32)
        * score_scale
    )
    key_grad = (
        jnp.einsum("chlm,clhe->cmhe", score_grad, query_heads, preferred_element_type=jnp.float32)
        * score_scale
    )
    query_grad = query_grad.reshape(row_count, model_width)
    key_grad = key_grad.reshape(row_count, model_width)
    value_grad = value_grad.reshape(row_count, model_width)
    query_bias = jnp.sum(query_grad, axis=0)
    value_bias = jnp.sum(value_grad, axis=0)
    joined_low = jnp.concatenate([query_grad, key_grad, value_grad], axis=1).astype(jnp.bfloat16)
    normed_grad = jnp.einsum(
        "te,de->td", joined_low, attend_weight, preferred_element_type=jnp.float32
    )
    first_back = jax.vjp(normalize, hidden, gain_rows[0], offset_rows[0])[1]
    hidden_part, gain_one, offset_one = first_back(normed_grad)
    hidden_grad = middle_grad + hidden_part
    gain_term = jnp.stack([gain_one, gain_two])
    offset_term = jnp.stack([offset_one, offset_two, query_bias, value_bias, merge_bias, last_bias])
    factors = (normed, attended, normed_two, activated, joined_low, middle_low, raised_low, low_grad)
    return (hidden_grad, factors, (gain_term, offset_term, up_bias_term))


def pack_vectors(gains, shifts, bias, tile):
    flat = jnp.concatenate([gains.reshape(-1), shifts.reshape(-1), bias.reshape(-1)])
    rows = tile * (-(-flat.shape[0] // (tile * 128)))
    return jnp.pad(flat, (0, rows * 128 - flat.shape[0])).reshape(rows, 128)


def unpack_vectors(packed, width, wide):
    ways = packed.shape[0]
    flat = packed.reshape(ways, -1)
    own = width // ways
    gains = flat[:, : 2 * own].reshape(ways, 2, own).swapaxes(0, 1).reshape(2, width)
    shifts = flat[:, 2 * own : 8 * own].reshape(ways, 6, own).swapaxes(0, 1).reshape(6, width)
    bias = flat[:, 8 * own : 8 * own + wide // ways].reshape(wide)
    return gains, shifts, bias


def gather_weights(shards, gains, shifts, bias):
    ways = lax.axis_size("fsdp")
    width, wide = shards[0].shape[0] * ways, shards[2].shape[1]
    if shards[0].shape[0] % 16 or ways % 4:
        wholes = [lax.all_gather(shard, "fsdp", axis=0, tiled=True) for shard in shards]
        packed = lax.all_gather(pack_vectors(gains, shifts, bias, 16), "fsdp", axis=0)
        return (*wholes, *unpack_vectors(packed, width, wide))
    attend, merge, up, down = shards
    half = down.shape[0] // 2
    pieces = [attend, pack_vectors(gains, shifts, bias, 16), up, merge, down[:half], down[half:]]
    kinds = ["level", "level", "level", "level", "level", "across"]
    wholes = gather_all(pieces, kinds, ways, 1)
    attend, packed, up, merge, low_half, high_half = wholes
    down = jnp.concatenate([low_half, high_half], axis=1)
    return (
        attend.reshape(width, -1),
        merge.reshape(width, -1),
        up.reshape(width, -1),
        down.reshape(wide, -1),
        *unpack_vectors(packed, width, wide),
    )


def reduce_gradients(factors, gain_total, shift_total, bias_total):
    ways = lax.axis_size("fsdp")
    normed, attended, normed_two, activated, joined, middle, raised, low = factors
    width, wide = normed.shape[1], activated.shape[1]
    own = width // ways
    if own % 16 or ways % 4:

        def product(left, right):
            term = jnp.einsum("td,te->de", left, right, preferred_element_type=jnp.float32)
            return lax.psum_scatter(term, "fsdp", scatter_dimension=0, tiled=True)

        return (
            product(normed, joined),
            product(attended, middle),
            product(normed_two, raised),
            product(activated, low),
            lax.psum_scatter(gain_total, "fsdp", scatter_dimension=1, tiled=True),
            lax.psum_scatter(shift_total, "fsdp", scatter_dimension=1, tiled=True),
            lax.psum_scatter(bias_total, "fsdp", scatter_dimension=0, tiled=True),
        )
    flat = jnp.concatenate(
        [
            gain_total.reshape(2, ways, own).swapaxes(0, 1).reshape(ways, -1),
            shift_total.reshape(6, ways, own).swapaxes(0, 1).reshape(ways, -1),
            bias_total.reshape(ways, -1),
        ],
        axis=1,
    )
    rows = 8 * (-(-flat.shape[1] // 1024))
    vectors = jnp.pad(flat, ((0, 0), (0, rows * 128 - flat.shape[1]))).reshape(ways, rows, 128)
    attend, merge, up, down, vector, _ = reduce_weights(factors, vectors, ways, 2)
    vector = vector.reshape(-1)
    gains = vector[: 2 * own].reshape(2, own)
    shifts = vector[2 * own : 8 * own].reshape(6, own)
    return attend, merge, up, down, gains, shifts, vector[8 * own : 8 * own + wide // ways]


def body(
    section_inputs,
    norm_gains,
    offsets,
    attend_weight,
    merge_weight,
    up_weight,
    up_bias,
    down_weight,
):
    shards = (attend_weight[0], merge_weight[0], up_weight[0], down_weight[0])
    gathered = gather_weights(shards, norm_gains[0], offsets[0], up_bias[0])
    weights = gathered
    is_first = lax.axis_index("section") == 0
    own_data = section_inputs[0]
    batches, clip_count, length, model_width = own_data.shape
    row_count = clip_count * length
    own_rows = own_data.reshape(batches, row_count, model_width)
    kept_state = []
    upper_rows = []
    received = jnp.zeros((row_count, model_width), jnp.bfloat16)
    for instant in range(batches + 1):
        entering = jnp.where(is_first, own_rows[min(instant, batches - 1)], received)
        result, saved_state = layer_forward(entering.astype(jnp.float32), weights, clip_count)
        kept_state.append(saved_state)
        rounded = result.astype(jnp.bfloat16)
        if instant >= 1:
            upper_rows.append(rounded)
        if instant < batches:
            received = from_behind(rounded, "section", 1)
    received_grad = jnp.zeros((row_count, model_width), jnp.bfloat16)
    lower_rows, factor_rows, vector_terms = [], [], []
    for instant in range(batches + 1):
        position = batches - 1 - instant
        if position >= 0:
            own_grad = own_rows[position]
        else:
            own_grad = jnp.zeros((row_count, model_width), jnp.bfloat16)
        cotangent = jnp.where(is_first, received_grad, own_grad).astype(jnp.float32)
        hidden_grad, factors, vectors = layer_backward(
            cotangent, kept_state[batches - instant], weights, clip_count
        )
        factor_rows.append(factors)
        vector_terms.append(vectors)
        rounded = hidden_grad.astype(jnp.bfloat16)
        if instant >= 1:
            lower_rows.append(rounded)
        if instant < batches:
            received_grad = from_behind(rounded, "section", -1)
    ordered_lower = lower_rows[::-1]
    combined = jnp.stack(
        [
            jnp.where(is_first, lower_part, upper_part)
            for lower_part, upper_part in zip(ordered_lower, upper_rows)
        ]
    )
    section_outputs = combined.reshape(1, batches, clip_count, length, model_width)
    factors = [
        jnp.concatenate([jnp.where(is_first, b, a) for a, b in zip(rows[:-1], rows[1:])])
        for rows in zip(*factor_rows)
    ]
    totals = [sum(terms[1:], terms[0]) for terms in zip(*vector_terms)]
    attend, merge, up, down, gains, shifts, bias = reduce_gradients(factors, *totals)
    return (
        section_outputs,
        gains[None],
        shifts[None],
        attend[None],
        merge[None],
        up[None],
        bias[None],
        down[None],
    )


def solution(mesh):
    return jax.shard_map(
        body,
        mesh=mesh,
        in_specs=(
            P("section", None, "fsdp", None, None),
            P("section", None, "fsdp"),
            P("section", None, "fsdp"),
            P("section", "fsdp", None),
            P("section", "fsdp", None),
            P("section", "fsdp", None),
            P("section", "fsdp"),
            P("section", "fsdp", None),
        ),
        out_specs=(
            P("section", None, "fsdp", None, None),
            P("section", None, "fsdp"),
            P("section", None, "fsdp"),
            P("section", "fsdp", None),
            P("section", "fsdp", None),
            P("section", "fsdp", None),
            P("section", "fsdp"),
            P("section", "fsdp", None),
        ),
        check_vma=False,
    )
```

```python
import functools
import math

import jax
import jax.numpy as jnp
from jax import lax
from jax.experimental import pallas as pl
from jax.experimental.pallas import tpu as pltpu
from jax.sharding import PartitionSpec as P

MESH = pl.DeviceIdType.MESH


SIDE, ACROSS, UP, DOWN = range(4)


class Sends:
    def __init__(self):
        self.items = []

    def start(self, copy, when):
        if when is None:
            copy.start()
        else:
            pl.when(when)(copy.start)
        self.items.append((copy, when))

    def drain(self):
        for copy, when in self.items:
            if when is None:
                copy.wait_send()
            else:
                pl.when(when)(copy.wait_send)


def place():
    section, mine = lax.axis_index("section"), lax.axis_index("fsdp")
    return section, mine, lax.div(mine, 4), lax.rem(lax.div(mine, 2), 2), lax.rem(mine, 2)


def greet(section, mine, level, levels):
    barrier = pltpu.get_barrier_semaphore()

    def hello(target):
        pl.semaphore_signal(barrier, inc=1, device_id=(section, target), device_id_type=MESH)

    hello(mine ^ 1)
    hello(mine ^ 2)
    pl.when(level > 0)(lambda: hello(mine - 4))
    pl.when(level < levels - 1)(lambda: hello(mine + 4))
    ends = (level == 0).astype(jnp.int32) + (level == levels - 1).astype(jnp.int32)
    pl.semaphore_wait(barrier, 4 - ends)


def gather_kernel(levels, kinds, *refs):
    count = len(kinds)
    shards, wholes = refs[:count], refs[count : 2 * count]
    send_sem, recv_sem, local_sem = refs[2 * count :]
    section, mine, level, row, core = place()
    greet(section, mine, level, levels)
    has_up, has_down = level < levels - 1, level > 0
    targets = {SIDE: mine ^ 1, ACROSS: mine ^ 2, UP: mine + 4, DOWN: mine - 4}
    sends = Sends()

    def send(chunk, block, way, own=False, when=None):
        copy = pltpu.make_async_remote_copy(
            src_ref=shards[chunk] if own else wholes[chunk].at[block],
            dst_ref=wholes[chunk].at[block],
            send_sem=send_sem.at[chunk, block, way],
            recv_sem=recv_sem.at[chunk, block],
            device_id=(section, targets[way]),
            device_id_type=MESH,
        )
        sends.start(copy, when)

    def arrived(chunk, block):
        pltpu.make_async_remote_copy(
            src_ref=wholes[chunk].at[block],
            dst_ref=wholes[chunk].at[block],
            send_sem=send_sem.at[chunk, block, 0],
            recv_sem=recv_sem.at[chunk, block],
            device_id=(section, mine),
            device_id_type=MESH,
        ).wait_recv()

    def both(one, two):
        return jnp.logical_and(one, two)

    def guarded(when, action):
        pl.when(when)(action)

    local = []
    for chunk in range(count):
        copy = pltpu.make_async_copy(shards[chunk], wholes[chunk].at[mine], local_sem.at[chunk])
        copy.start()
        local.append(copy)
    for chunk in range(count):
        send(chunk, mine, ACROSS, own=True)
        send(chunk, mine, UP, own=True, when=has_up)
        send(chunk, mine, DOWN, own=True, when=has_down)
        send(chunk, mine, SIDE, own=True)

    def block_of(block_level, block_row, block_core):
        return block_level * 4 + block_row * 2 + block_core

    for chunk in range(count):
        if kinds[chunk] == "across":
            block = mine ^ 2
            arrived(chunk, block)
            send(chunk, block, UP, when=has_up)
            send(chunk, block, DOWN, when=has_down)
            send(chunk, block, SIDE)

    def across_arrivals(distance, chunk):
        if kinds[chunk] == "across":
            return
        if distance == 0:
            arrived(chunk, mine ^ 2)
            send(chunk, mine ^ 2, SIDE)
            return
        for sign in (-1, 1):
            other = level + sign * distance
            here = other >= 0 if sign < 0 else other < levels
            block = block_of(other, 1 - row, core)
            pl.when(here)(functools.partial(arrived, chunk, block))
            send(chunk, block, SIDE, when=here)

    for distance in range(1, levels):
        for chunk in range(count):
            rows = (row,) if kinds[chunk] == "level" else (row, 1 - row)
            for block_row in rows:
                for sign in (-1, 1):
                    other = level + sign * distance
                    here = other >= 0 if sign < 0 else other < levels
                    onward = has_up if sign < 0 else has_down
                    block = block_of(other, block_row, core)
                    pl.when(here)(functools.partial(arrived, chunk, block))
                    if distance < levels - 1:
                        send(chunk, block, UP if sign < 0 else DOWN, when=both(here, onward))
                    if kinds[chunk] == "level":
                        send(chunk, block, ACROSS, when=here)
                    send(chunk, block, SIDE, when=here)
            across_arrivals(distance - 1, chunk)
    for chunk in range(count):
        across_arrivals(levels - 1, chunk)
    for chunk in range(count):
        for block_level in range(levels):
            for block_row in range(2):
                arrived(chunk, block_of(block_level, block_row, 1 - core))
    for copy in local:
        copy.wait()
    sends.drain()


def gather_all(shards, kinds, ways, collective_id):
    levels = ways // 4
    count = len(shards)
    return pl.pallas_call(
        functools.partial(gather_kernel, levels, kinds),
        out_shape=[jax.ShapeDtypeStruct((ways,) + s.shape, s.dtype) for s in shards],
        in_specs=[pl.BlockSpec(memory_space=pl.ANY)] * count,
        out_specs=[pl.BlockSpec(memory_space=pl.ANY)] * count,
        scratch_shapes=[
            pltpu.SemaphoreType.DMA((count, ways, 4)),
            pltpu.SemaphoreType.DMA((count, ways)),
            pltpu.SemaphoreType.DMA((count,)),
        ],
        compiler_params=pltpu.CompilerParams(collective_id=collective_id, has_side_effects=True),
    )(*shards)


LEVELS_FIRST, ACROSS_FIRST = 0, 1


class Chunk:
    def __init__(self, levels, order, refs, sems, where):
        self.levels, self.order = levels, order
        self.part, self.from_side, self.from_across, self.from_below, self.from_above = refs
        (
            self.side_out,
            self.side_in,
            self.across_out,
            self.across_in,
            self.up_out,
            self.up_in,
            self.down_out,
            self.down_in,
        ) = sems
        self.section, self.mine, self.level, self.row, self.core = where

    def copy(self, source, target, out_sem, in_sem, device):
        return pltpu.make_async_remote_copy(
            src_ref=source,
            dst_ref=target,
            send_sem=out_sem,
            recv_sem=in_sem,
            device_id=(self.section, device),
            device_id_type=MESH,
        )

    def block(self, level, row, core):
        return level * 4 + row * 2 + core

    def side(self, pair):
        return self.copy(
            self.part.at[pair * 2 + 1 - self.core],
            self.from_side.at[pair],
            self.side_out.at[pair],
            self.side_in.at[pair],
            self.mine ^ 1,
        )

    def across(self, level, slot):
        return self.copy(
            self.part.at[self.block(level, 1 - self.row, self.core)],
            self.from_across.at[slot],
            self.across_out.at[slot],
            self.across_in.at[slot],
            self.mine ^ 2,
        )

    def up(self, row, slot, level):
        return self.copy(
            self.part.at[self.block(level, row, self.core)],
            self.from_below.at[slot, level],
            self.up_out.at[slot, level],
            self.up_in.at[slot, level],
            self.mine + 4,
        )

    def down(self, row, slot, level):
        return self.copy(
            self.part.at[self.block(level, row, self.core)],
            self.from_above.at[slot, level],
            self.down_out.at[slot, level],
            self.down_in.at[slot, level],
            self.mine - 4,
        )

    def add(self, block, term):
        total = self.part[block].astype(jnp.float32) + term.astype(jnp.float32)
        self.part[block] = total.astype(self.part.dtype)

    def send_side(self):
        @pl.loop(0, self.levels * 2)
        def _(pair):
            self.side(pair).start()

    def join_side(self):
        for other in (True, False):
            row = 1 - self.row if other else self.row

            @pl.loop(0, self.levels)
            def _(level):
                pair = level * 2 + row
                self.side(pair).wait_recv()
                self.add(pair * 2 + self.core, self.from_side[pair])
                if other and self.order == ACROSS_FIRST:
                    self.across(level, level).start()

    def join_across(self):
        @pl.loop(0, self.levels)
        def _(level):
            self.across(level, level).wait_recv()
            self.add(self.block(level, self.row, self.core), self.from_across[level])

    def rows(self):
        return ((0, self.row), (1, 1 - self.row)) if self.order == LEVELS_FIRST else ((0, self.row),)

    def chain_start(self):
        for slot, row in self.rows():
            for target in range(self.levels):
                if target:
                    pl.when(self.level == 0)(self.up(row, slot, self.levels - target).start)
                    pl.when(self.level == self.levels - 1)(self.down(row, slot, target - 1).start)

    def chain_pass(self, distance):
        last = self.levels - 1
        for slot, row in self.rows():
            for target in range(last, 0, -1):
                if target > distance:

                    @pl.when(self.level == distance)
                    def _():
                        self.up(row, slot, target).wait_recv()
                        self.add(self.block(target, row, self.core), self.from_below[slot, target])
                        self.up(row, slot, target).start()

            for target in range(last):
                if target < last - distance:

                    @pl.when(self.level == last - distance)
                    def _():
                        self.down(row, slot, target).wait_recv()
                        self.add(self.block(target, row, self.core), self.from_above[slot, target])
                        self.down(row, slot, target).start()

    def chain_end(self, out):
        last = self.levels - 1
        for slot, row in reversed(self.rows()):
            block = self.block(self.level, row, self.core)

            @pl.when(self.level > 0)
            def _():
                self.up(row, slot, self.level).wait_recv()
                self.add(block, self.from_below[slot, self.level])

            @pl.when(self.level < last)
            def _():
                self.down(row, slot, self.level).wait_recv()
                self.add(block, self.from_above[slot, self.level])

            if slot == 1:
                self.across(self.level, 0).start()
        if self.order == ACROSS_FIRST:
            out[...] = self.part[self.mine].astype(jnp.float32)

    def finish(self, out):
        if self.order == LEVELS_FIRST:
            self.across(self.level, 0).wait_recv()
            out[...] = self.part[self.mine].astype(jnp.float32) + self.from_across[0].astype(jnp.float32)

    def drain(self):
        @pl.loop(0, self.levels * 2)
        def _(pair):
            self.side(pair).wait_send()

        if self.order == ACROSS_FIRST:

            @pl.loop(0, self.levels)
            def _(level):
                self.across(level, level).wait_send()

        else:
            self.across(self.level, 0).wait_send()
        for slot, row in self.rows():
            for target in range(self.levels):
                pl.when(self.level < target)(self.up(row, slot, target).wait_send)
                pl.when(self.level > target)(self.down(row, slot, target).wait_send)


def chunk_scratch(levels, order, rows, cols, dtype):
    block = (rows, cols)
    slots = 2 if order == LEVELS_FIRST else 1
    crossing = 1 if order == LEVELS_FIRST else levels
    buffers = [
        pltpu.VMEM((levels * 4,) + block, dtype),
        pltpu.VMEM((levels * 2,) + block, dtype),
        pltpu.VMEM((crossing,) + block, dtype),
        pltpu.VMEM((slots, levels) + block, dtype),
        pltpu.VMEM((slots, levels) + block, dtype),
    ]
    dma = pltpu.SemaphoreType.DMA
    sems = [dma((levels * 2,))] * 2 + [dma((crossing,))] * 2 + [dma((slots, levels))] * 4
    return buffers + sems


CHUNK_REFS = 13


def weights_kernel(levels, plan, *refs):
    inputs, refs = refs[:9], refs[9:]
    outs, refs = refs[:6], refs[6:]
    wide_one, narrow_one, wide_two, narrow_two, turned, load_sem = refs[:6]
    refs = refs[6:]
    where = place()
    section, mine, level, row, core = where
    normed, attended, normed_two, activated, joined, middle, raised, low, vectors = inputs
    attend_out, merge_out, up_out, down_out, vector_out = outs[0], outs[1], outs[2], outs[3], outs[4]
    chunks = []
    for index, (name, order, rows, cols, dtype) in enumerate(plan):
        held = refs[index * CHUNK_REFS : (index + 1) * CHUNK_REFS]
        chunks.append(Chunk(levels, order, held[:5], held[5:], where))
    down_a, down_b, up_a, up_b, attend_a, attend_b, merge, vector = chunks
    width = normed.shape[1]

    def load(source, target, index):
        copy = pltpu.make_async_copy(source, target, load_sem.at[index])
        copy.start()
        return copy

    loads_down = [load(activated, wide_one, 0), load(low, narrow_one, 1)]
    loads_up = [load(normed_two, narrow_two, 2), load(raised, wide_two, 3)]
    load_vector = load(vectors, vector.part, 4)
    greet(section, mine, level, levels)

    for copy in loads_down:
        copy.wait()
    pair_cols = 2 * down_a.part.shape[1]
    half = down_a.part.shape[2]
    shard = down_a.part.shape[1]

    @pl.loop(0, levels * 2)
    def _(pair):
        tile = wide_one[:, pl.ds(pl.multiple_of(pair * pair_cols, 128), pair_cols)]
        for which, chunk in enumerate((down_a, down_b)):
            product = lax.dot_general(
                tile,
                narrow_one[:, which * half : (which + 1) * half],
                (((0,), (0,)), ((), ())),
                preferred_element_type=jnp.float32,
            ).astype(chunk.part.dtype)
            chunk.part[pair * 2] = product[:shard]
            chunk.part[pair * 2 + 1] = product[shard:]
            chunk.side(pair).start()

    load_vector.wait()
    vector.send_side()
    down_a.join_side()
    down_a.chain_start()
    down_b.join_side()
    vector.join_side()

    def turn(source):
        turned[...] = source[...].T

    def columns(source, start, chunk):
        cols = chunk.part.shape[2]
        step = 128 * max(d for d in (1, 2, 3) if cols % (128 * d) == 0)

        @pl.loop(0, cols // step)
        def _(index):
            at = pl.multiple_of(index * step, 128)
            product = jnp.dot(
                turned[...],
                source[:, pl.ds(pl.multiple_of(start + at, 128), step)],
                preferred_element_type=jnp.float32,
            )
            blocks = chunk.part.shape[0]
            chunk.part[:, :, pl.ds(at, step)] = product.astype(chunk.part.dtype).reshape(
                blocks, width // blocks, step
            )

        chunk.send_side()

    for copy in loads_up:
        copy.wait()
    turn(narrow_two)
    columns(wide_two, 0, up_a)
    loads_attend = [load(normed, narrow_one, 0), load(joined, wide_one.at[:, : joined.shape[1]], 1)]
    columns(wide_two, up_a.part.shape[2], up_b)
    loads_merge = [load(attended, narrow_two, 2), load(middle, wide_two.at[:, :width], 3)]
    up_a.join_side()
    down_a.chain_pass(1)
    up_b.join_side()
    for copy in loads_attend:
        copy.wait()
    turn(narrow_one)
    columns(wide_one, 0, attend_a)
    down_a.chain_pass(2)
    down_b.join_across()
    down_b.chain_start()
    vector.join_across()
    vector.chain_start()
    columns(wide_one, attend_a.part.shape[2], attend_b)
    attend_a.join_side()
    for copy in loads_merge:
        copy.wait()
    turn(narrow_two)
    columns(wide_two, 0, merge)
    attend_b.join_side()
    down_b.chain_pass(1)
    merge.join_side()
    down_a.chain_end(None)
    up_a.join_across()
    up_a.chain_start()
    down_b.chain_pass(2)
    vector.chain_pass(1)
    up_a.chain_pass(1)
    up_b.join_across()
    up_b.chain_start()
    vector.chain_pass(2)
    down_b.chain_end(down_out.at[:, half:])
    up_a.chain_pass(2)
    up_b.chain_pass(1)
    attend_a.join_across()
    attend_a.chain_start()
    vector.chain_end(vector_out)
    up_a.chain_end(up_out.at[:, : up_a.part.shape[2]])
    up_b.chain_pass(2)
    attend_a.chain_pass(1)
    attend_b.join_across()
    attend_b.chain_start()
    up_b.chain_end(up_out.at[:, up_a.part.shape[2] :])
    attend_a.chain_pass(2)
    attend_b.chain_pass(1)
    merge.join_across()
    merge.chain_start()
    attend_a.chain_end(attend_out.at[:, : attend_a.part.shape[2]])
    attend_b.chain_pass(2)
    merge.chain_pass(1)
    attend_b.chain_end(attend_out.at[:, attend_a.part.shape[2] :])
    merge.chain_pass(2)
    down_a.finish(down_out.at[:, :half])
    merge.chain_end(merge_out)
    for chunk in chunks:
        chunk.drain()


def reduce_weights(states, vectors, ways, collective_id):
    normed, attended, normed_two, activated, joined, middle, raised, low = states
    levels = ways // 4
    total_rows, width = normed.shape
    wide = activated.shape[1]
    rows, shard = width // ways, wide // ways
    low_type = jnp.bfloat16
    plan = [
        ("down_a", LEVELS_FIRST, shard, width // 2, low_type),
        ("down_b", ACROSS_FIRST, shard, width // 2, low_type),
        ("up_a", ACROSS_FIRST, rows, wide // 2, low_type),
        ("up_b", ACROSS_FIRST, rows, wide // 2, low_type),
        ("attend_a", ACROSS_FIRST, rows, 3 * width // 2, low_type),
        ("attend_b", ACROSS_FIRST, rows, 3 * width // 2, low_type),
        ("merge", ACROSS_FIRST, rows, width, low_type),
        ("vector", ACROSS_FIRST, vectors.shape[1], vectors.shape[2], jnp.float32),
    ]
    scratch = [
        pltpu.VMEM((total_rows, wide), low_type),
        pltpu.VMEM((total_rows, width), low_type),
        pltpu.VMEM((total_rows, wide), low_type),
        pltpu.VMEM((total_rows, width), low_type),
        pltpu.VMEM((width, total_rows), low_type),
        pltpu.SemaphoreType.DMA((5,)),
    ]
    for name, order, r, c, dtype in plan:
        scratch += chunk_scratch(levels, order, r, c, dtype)
    f32 = jnp.float32
    vmem = pl.BlockSpec(memory_space=pltpu.VMEM)
    return pl.pallas_call(
        functools.partial(weights_kernel, levels, plan),
        out_shape=[
            jax.ShapeDtypeStruct((rows, 3 * width), f32),
            jax.ShapeDtypeStruct((rows, width), f32),
            jax.ShapeDtypeStruct((rows, wide), f32),
            jax.ShapeDtypeStruct((shard, width), f32),
            jax.ShapeDtypeStruct(vectors.shape[1:], f32),
            jax.ShapeDtypeStruct((8, 128), f32),
        ],
        in_specs=[pl.BlockSpec(memory_space=pl.ANY)] * 9,
        out_specs=[vmem] * 6,
        scratch_shapes=scratch,
        compiler_params=pltpu.CompilerParams(
            collective_id=collective_id, has_side_effects=True, vmem_limit_bytes=62 * 2**20
        ),
    )(*states, vectors)


HEADS = 12
HEAD_DIM = 64
epsilon = 1e-05
BF, F32 = jnp.bfloat16, jnp.float32
NT = (((1,), (1,)), ((), ()))
TN = (((0,), (0,)), ((), ()))


def matmul(left, right, dims=(((1,), (0,)), ((), ()))):
    return lax.dot_general(left, right, dims, preferred_element_type=F32)


def standard(features):
    centred = features - jnp.mean(features, axis=-1, keepdims=True)
    scale = lax.rsqrt(jnp.mean(centred * centred, axis=-1, keepdims=True) + epsilon)
    return centred * scale, scale


def gelu_and_slope(raised):
    share = 0.5 + 0.5 * lax.erf(raised * math.sqrt(0.5))
    bell = jnp.exp(raised * raised * -0.5) * (1.0 / math.sqrt(2.0 * math.pi))
    return raised * share, share + raised * bell


def norm_back(upper, normal, scale):
    shift = jnp.mean(upper, axis=-1, keepdims=True)
    slope = jnp.mean(upper * normal, axis=-1, keepdims=True)
    return (upper - shift - normal * slope) * scale


def column_sum(values):
    return jnp.sum(values, axis=0, keepdims=True)


def pair_parts(matrix):
    lane = lax.broadcasted_iota(jnp.int32, matrix.shape, 1)
    zero = jnp.zeros_like(matrix)
    first = lane < HEAD_DIM
    return jnp.concatenate([jnp.where(first, matrix, zero), jnp.where(first, zero, matrix)], axis=0)


def pair_join(stacked):
    rows = stacked.shape[0] // 2
    lane = lax.broadcasted_iota(jnp.int32, (rows, stacked.shape[1]), 1)
    return jnp.where(lane < HEAD_DIM, stacked[:rows], stacked[rows:])


def halves(scores):
    keys = scores.shape[1] // 2
    return scores[:, :keys], scores[:, keys:]


def pipeline_kernel(clips, *refs):
    (own, attend_hbm, merge_hbm, up_hbm, down_hbm, vectors, bias) = refs[:7]
    (out, *factor_out, vector_sum, bias_sum) = refs[7:18]
    (
        entry,
        attend,
        merge,
        up,
        down,
        projected,
        probability,
        normed,
        attended,
        middle,
        normed_two,
        activated,
        slope,
        middle_low,
        leaving,
        wide_temp,
        temp,
        load_sem,
        save_sem,
        send_sem,
        recv_sem,
        out_sem,
    ) = refs[18:]
    batches, rows, width = own.shape
    wide = up.shape[1]
    length = rows // clips
    pairs = HEADS // 2
    section, mine = lax.axis_index("section"), lax.axis_index("fsdp")
    first = section == 0
    last_section = 1 - section
    fed, back = section, 1 - section
    loads = [
        pltpu.make_async_copy(source, target, load_sem.at[index])
        for index, (source, target) in enumerate(
            [
                (own, entry.at[0]),
                (attend_hbm, attend),
                (merge_hbm, merge),
                (up_hbm, up),
                (down_hbm, down),
            ]
        )
    ]
    for copy in loads:
        copy.start()
    barrier = pltpu.get_barrier_semaphore()
    pl.semaphore_signal(barrier, inc=1, device_id=(1 - section, mine), device_id_type=MESH)
    pl.semaphore_wait(barrier, 1)

    def relay(batch):
        return pltpu.make_async_remote_copy(
            src_ref=leaving.at[batch],
            dst_ref=entry.at[1, batch],
            send_sem=send_sem.at[batch],
            recv_sem=recv_sem.at[batch],
            device_id=(1 - section, mine),
            device_id_type=MESH,
        )

    def keep(batch):
        return pltpu.make_async_copy(leaving.at[batch], out.at[batch], out_sem.at[batch])

    forward_saves = [(normed, 0), (attended, 1), (normed_two, 2), (activated, 3)]
    backward_saves = [(projected, 4), (middle_low, 5), (slope, 6)]

    def save(buffer, index, batch):
        return pltpu.make_async_copy(buffer.at[batch], factor_out[index].at[batch], save_sem.at[index, batch])

    def save_low(batch):
        return pltpu.make_async_copy(entry.at[back, batch], factor_out[7].at[batch], save_sem.at[7, batch])

    vector_sum[...] = jnp.zeros_like(vector_sum)
    bias_sum[...] = jnp.zeros_like(bias_sum)

    def row(index):
        return vectors[index : index + 1, :]

    def forward(batch):
        normal, _ = standard(entry[fed, batch].astype(F32))
        normed[batch] = (normal * row(0) + row(2)).astype(BF)
        for part, shift in ((0, 4), (1, None), (2, 5)):
            at = slice(part * width, (part + 1) * width)
            value = matmul(normed[batch], attend[:, at])
            if shift is not None:
                value = value + row(shift)
            projected[batch, :, at] = value.astype(BF)
        for clip in range(clips):
            span = slice(clip * length, (clip + 1) * length)
            for pair in range(pairs):
                lanes = [slice(p * width + pair * 128, p * width + pair * 128 + 128) for p in range(3)]
                query = projected[batch, span, lanes[0]] * jnp.asarray(HEAD_DIM**-0.5, BF)
                key = pair_parts(projected[batch, span, lanes[1]])
                scores = matmul(query, key, NT)
                parts = []
                for half in halves(scores):
                    exponent = jnp.exp(half - jnp.max(half, axis=-1, keepdims=True))
                    parts.append(exponent * (1.0 / jnp.sum(exponent, axis=-1, keepdims=True)))
                weight = jnp.concatenate(parts, axis=1).astype(BF)
                probability[batch, clip * pairs + pair] = weight
                value = pair_parts(projected[batch, span, lanes[2]])
                attended[batch, span, lanes[0]] = matmul(weight, value).astype(BF)
        joined = matmul(attended[batch], merge[...]) + row(6)
        middle[batch] = entry[fed, batch].astype(F32) + joined
        normal, _ = standard(middle[batch])
        normed_two[batch] = (normal * row(1) + row(3)).astype(BF)
        tile = 256
        for start in range(0, wide, tile):
            at = slice(start, start + tile)
            value, rate = gelu_and_slope(matmul(normed_two[batch], up[:, at]) + bias[:, at])
            activated[batch, :, at] = value.astype(BF)
            slope[batch, :, at] = rate.astype(BF)
        result = middle[batch] + matmul(activated[batch], down[...]) + row(7)
        leaving[batch] = result.astype(BF)

    def backward(batch, slot):
        low = entry[back, batch]
        vector_sum[7:8] += column_sum(low.astype(F32))
        tile = 256
        for start in range(0, wide, tile):
            at = slice(start, start + tile)
            rate = matmul(low, down[at, :], NT) * slope[batch, :, at].astype(F32)
            bias_sum[:, at] += column_sum(rate)
            slope[batch, :, at] = rate.astype(BF)
        temp[...] = matmul(slope[batch], up[...], NT)
        normal, scale = standard(middle[batch])
        grad = temp[...]
        vector_sum[1:2] += column_sum(grad * normal)
        vector_sum[3:4] += column_sum(grad)
        grad = entry[back, batch].astype(F32) + norm_back(grad * row(1), normal, scale)
        middle[batch] = grad
        vector_sum[6:7] += column_sum(grad)
        middle_low[batch] = grad.astype(BF)
        wide_temp[...] = matmul(middle_low[batch], merge[...], NT).astype(BF)
        for clip in range(clips):
            span = slice(clip * length, (clip + 1) * length)
            for pair in range(pairs):
                lanes = [slice(p * width + pair * 128, p * width + pair * 128 + 128) for p in range(3)]
                query = projected[batch, span, lanes[0]]
                key = pair_parts(projected[batch, span, lanes[1]])
                value = pair_parts(projected[batch, span, lanes[2]])
                upper = wide_temp[span, lanes[0]]
                weight = probability[batch, clip * pairs + pair]
                rise = matmul(upper, value, NT)
                value_grad = pair_join(matmul(weight, upper, TN))
                parts = []
                for part, heavy in zip(halves(rise), halves(weight)):
                    heavy = heavy.astype(F32)
                    mean = jnp.sum(part * heavy, axis=-1, keepdims=True)
                    parts.append(heavy * (part - mean) * HEAD_DIM**-0.5)
                change = jnp.concatenate(parts, axis=1).astype(BF)
                query_grad = matmul(change, key)
                key_grad = pair_join(matmul(change, query, TN))
                vector_sum[4:5, lanes[0]] += column_sum(query_grad)
                vector_sum[5:6, lanes[0]] += column_sum(value_grad)
                for at, piece in zip(lanes, (query_grad, key_grad, value_grad)):
                    projected[batch, span, at] = piece.astype(BF)
        temp[...] = matmul(projected[batch], attend[...], NT)
        normal, scale = standard(entry[fed, batch].astype(F32))
        grad = temp[...]
        vector_sum[0:1] += column_sum(grad * normal)
        vector_sum[2:3] += column_sum(grad)
        leaving[slot] = (middle[batch] + norm_back(grad * row(0), normal, scale)).astype(BF)

    for copy in loads:
        copy.wait()

    @pl.loop(0, 2 * batches)
    def _(step):
        is_forward = jnp.where(first, step < batches, lax.rem(step, 2) == 0)
        batch = jnp.where(first, lax.rem(step, batches), lax.div(step, 2))

        @pl.when(is_forward)
        def _():
            pl.when(section == 1)(relay(batch).wait_recv)
            forward(batch)
            pl.when(section == 0)(relay(batch).start)
            pl.when(section == 1)(keep(batch).start)
            for buffer, index in forward_saves:
                save(buffer, index, batch).start()

        @pl.when(jnp.logical_not(is_forward))
        def _():
            pl.when(section == 0)(relay(batch).wait_recv)
            pl.when(section == 0)(relay(batch).wait_send)
            pl.when(section == 1)(keep(batch).wait)
            backward(batch, batch)
            pl.when(section == 1)(relay(batch).start)
            pl.when(section == 0)(keep(batch).start)
            for buffer, index in backward_saves:
                save(buffer, index, batch).start()
            save_low(batch).start()

    @pl.loop(0, batches)
    def _(batch):
        pl.when(section == 1)(relay(batch).wait_send)
        pl.when(section == 0)(keep(batch).wait)
        for buffer, index in forward_saves + backward_saves:
            save(buffer, index, batch).wait()
        save_low(batch).wait()


def run_pipeline(own, weights, vectors, bias, clips, collective_id):
    attend, merge, up, down = weights
    batches, rows, width = own.shape
    wide = up.shape[1]
    pairs = clips * (HEADS // 2)
    length = rows // clips

    def state(cols, dtype=BF):
        return jax.ShapeDtypeStruct((batches, rows, cols), dtype)

    factor_cols = [width, width, width, wide, 3 * width, width, wide, width]
    dma = pltpu.SemaphoreType.DMA
    vmem, anywhere = pl.BlockSpec(memory_space=pltpu.VMEM), pl.BlockSpec(memory_space=pl.ANY)

    def held(cols, dtype=BF):
        return pltpu.VMEM((batches, rows, cols), dtype)

    return pl.pallas_call(
        functools.partial(pipeline_kernel, clips),
        out_shape=[state(width)]
        + [state(cols) for cols in factor_cols]
        + [jax.ShapeDtypeStruct((8, width), F32), jax.ShapeDtypeStruct((1, wide), F32)],
        in_specs=[anywhere] * 5 + [vmem, vmem],
        out_specs=[anywhere] * 9 + [vmem, vmem],
        scratch_shapes=[
            pltpu.VMEM((2, batches, rows, width), BF),
            pltpu.VMEM(attend.shape, BF),
            pltpu.VMEM(merge.shape, BF),
            pltpu.VMEM(up.shape, BF),
            pltpu.VMEM(down.shape, BF),
            held(3 * width),
            pltpu.VMEM((batches, pairs, length, 2 * length), BF),
            held(width),
            held(width),
            held(width, F32),
            held(width),
            held(wide),
            held(wide),
            held(width),
            held(width),
            pltpu.VMEM((rows, width), BF),
            pltpu.VMEM((rows, width), F32),
            dma((5,)),
            dma((8, batches)),
            dma((batches,)),
            dma((batches,)),
            dma((batches,)),
        ],
        compiler_params=pltpu.CompilerParams(
            collective_id=collective_id, has_side_effects=True, vmem_limit_bytes=62 * 2**20
        ),
    )(own, attend, merge, up, down, vectors, bias)


def pack_vectors(gains, shifts, bias, tile):
    flat = jnp.concatenate([gains.reshape(-1), shifts.reshape(-1), bias.reshape(-1)])
    rows = tile * (-(-flat.shape[0] // (tile * 128)))
    return jnp.pad(flat, (0, rows * 128 - flat.shape[0])).reshape(rows, 128)


def unpack_vectors(packed, width, wide):
    ways = packed.shape[0]
    flat = packed.reshape(ways, -1)
    own = width // ways
    gains = flat[:, : 2 * own].reshape(ways, 2, own).swapaxes(0, 1).reshape(2, width)
    shifts = flat[:, 2 * own : 8 * own].reshape(ways, 6, own).swapaxes(0, 1).reshape(6, width)
    bias = flat[:, 8 * own : 8 * own + wide // ways].reshape(wide)
    return gains, shifts, bias


def gather_weights(shards, gains, shifts, bias):
    ways = lax.axis_size("fsdp")
    width, wide = shards[0].shape[0] * ways, shards[2].shape[1]
    if shards[0].shape[0] % 16 or ways % 4:
        wholes = [lax.all_gather(shard, "fsdp", axis=0, tiled=True) for shard in shards]
        packed = lax.all_gather(pack_vectors(gains, shifts, bias, 16), "fsdp", axis=0)
        return (*wholes, *unpack_vectors(packed, width, wide))
    attend, merge, up, down = shards
    half = down.shape[0] // 2
    pieces = [attend, pack_vectors(gains, shifts, bias, 16), up, merge, down[:half], down[half:]]
    kinds = ["level", "level", "level", "level", "level", "across"]
    wholes = gather_all(pieces, kinds, ways, 1)
    attend, packed, up, merge, low_half, high_half = wholes
    down = jnp.concatenate([low_half, high_half], axis=1)
    return (
        attend.reshape(width, -1),
        merge.reshape(width, -1),
        up.reshape(width, -1),
        down.reshape(wide, -1),
        *unpack_vectors(packed, width, wide),
    )


def reduce_gradients(factors, gain_total, shift_total, bias_total):
    ways = lax.axis_size("fsdp")
    normed, attended, normed_two, activated, joined, middle, raised, low = factors
    width, wide = normed.shape[1], activated.shape[1]
    own = width // ways
    if own % 16 or ways % 4:

        def product(left, right):
            term = jnp.einsum("td,te->de", left, right, preferred_element_type=jnp.float32)
            return lax.psum_scatter(term, "fsdp", scatter_dimension=0, tiled=True)

        return (
            product(normed, joined),
            product(attended, middle),
            product(normed_two, raised),
            product(activated, low),
            lax.psum_scatter(gain_total, "fsdp", scatter_dimension=1, tiled=True),
            lax.psum_scatter(shift_total, "fsdp", scatter_dimension=1, tiled=True),
            lax.psum_scatter(bias_total, "fsdp", scatter_dimension=0, tiled=True),
        )
    flat = jnp.concatenate(
        [
            gain_total.reshape(2, ways, own).swapaxes(0, 1).reshape(ways, -1),
            shift_total.reshape(6, ways, own).swapaxes(0, 1).reshape(ways, -1),
            bias_total.reshape(ways, -1),
        ],
        axis=1,
    )
    rows = 8 * (-(-flat.shape[1] // 1024))
    vectors = jnp.pad(flat, ((0, 0), (0, rows * 128 - flat.shape[1]))).reshape(ways, rows, 128)
    attend, merge, up, down, vector, _ = reduce_weights(factors, vectors, ways, 2)
    vector = vector.reshape(-1)
    gains = vector[: 2 * own].reshape(2, own)
    shifts = vector[2 * own : 8 * own].reshape(6, own)
    return attend, merge, up, down, gains, shifts, vector[8 * own : 8 * own + wide // ways]


def body(
    section_inputs,
    norm_gains,
    offsets,
    attend_weight,
    merge_weight,
    up_weight,
    up_bias,
    down_weight,
):
    shards = (attend_weight[0], merge_weight[0], up_weight[0], down_weight[0])
    *weights, gains, shifts, bias = gather_weights(shards, norm_gains[0], offsets[0], up_bias[0])
    batches, clips, length, width = section_inputs.shape[1:]
    own = section_inputs.reshape(batches, clips * length, width)
    vectors = jnp.concatenate([gains, shifts]).astype(jnp.float32)
    bias = bias.astype(jnp.float32)[None]
    section_outputs, *factors, vector_sum, bias_sum = run_pipeline(own, weights, vectors, bias, clips, 3)
    factors = [factor.reshape(-1, factor.shape[2]) for factor in factors]
    attend, merge, up, down, gains, shifts, bias = reduce_gradients(
        factors, vector_sum[:2], vector_sum[2:], bias_sum[0]
    )
    return (
        section_outputs.reshape(section_inputs.shape),
        gains[None],
        shifts[None],
        attend[None],
        merge[None],
        up[None],
        bias[None],
        down[None],
    )


def solution(mesh):
    return jax.shard_map(
        body,
        mesh=mesh,
        in_specs=(
            P("section", None, "fsdp", None, None),
            P("section", None, "fsdp"),
            P("section", None, "fsdp"),
            P("section", "fsdp", None),
            P("section", "fsdp", None),
            P("section", "fsdp", None),
            P("section", "fsdp"),
            P("section", "fsdp", None),
        ),
        out_specs=(
            P("section", None, "fsdp", None, None),
            P("section", None, "fsdp"),
            P("section", None, "fsdp"),
            P("section", "fsdp", None),
            P("section", "fsdp", None),
            P("section", "fsdp", None),
            P("section", "fsdp"),
            P("section", "fsdp", None),
        ),
        check_vma=False,
    )
```

```python
import functools
import math

import jax
import jax.numpy as jnp
from jax import lax
from jax.experimental import pallas as pl
from jax.experimental.pallas import tpu as pltpu
from jax.sharding import PartitionSpec as P

MESH = pl.DeviceIdType.MESH

HEADS = 12
HEAD_DIM = 64
epsilon = 1e-05
BF, F32 = jnp.bfloat16, jnp.float32
NT = (((1,), (1,)), ((), ()))
TN = (((0,), (0,)), ((), ()))

SIDE, ACROSS, UP, DOWN = range(4)
LEVELS_FIRST, ACROSS_FIRST = 0, 1

class Sends:
    def __init__(self):
        self.items = []

    def start(self, copy, when):
        if when is None:
            copy.start()
        else:
            pl.when(when)(copy.start)
        self.items.append((copy, when))

    def drain(self):
        for copy, when in self.items:
            if when is None:
                copy.wait_send()
            else:
                pl.when(when)(copy.wait_send)


def matmul(left, right, dims=(((1,), (0,)), ((), ()))):
    return lax.dot_general(left, right, dims, preferred_element_type=F32)


def standard(features):
    centred = features - jnp.mean(features, axis=-1, keepdims=True)
    scale = lax.rsqrt(jnp.mean(centred * centred, axis=-1, keepdims=True) + epsilon)
    return centred * scale, scale


def gelu_and_slope(raised):
    share = 0.5 + 0.5 * lax.erf(raised * math.sqrt(0.5))
    bell = jnp.exp(raised * raised * -0.5) * (1.0 / math.sqrt(2.0 * math.pi))
    return raised * share, share + raised * bell


def norm_back(upper, normal, scale):
    shift = jnp.mean(upper, axis=-1, keepdims=True)
    slope = jnp.mean(upper * normal, axis=-1, keepdims=True)
    return (upper - shift - normal * slope) * scale


def column_sum(values):
    return jnp.sum(values, axis=0, keepdims=True)


def pair_parts(matrix):
    lane = lax.broadcasted_iota(jnp.int32, matrix.shape, 1)
    zero = jnp.zeros_like(matrix)
    first = lane < HEAD_DIM
    return jnp.concatenate([jnp.where(first, matrix, zero), jnp.where(first, zero, matrix)], axis=0)


def pair_join(stacked):
    rows = stacked.shape[0] // 2
    lane = lax.broadcasted_iota(jnp.int32, (rows, stacked.shape[1]), 1)
    return jnp.where(lane < HEAD_DIM, stacked[:rows], stacked[rows:])


def halves(scores):
    keys = scores.shape[1] // 2
    return scores[:, :keys], scores[:, keys:]


class Place:
    def __init__(self, levels):
        self.levels = levels
        self.section, self.mine = lax.axis_index("section"), lax.axis_index("fsdp")
        self.level = lax.div(self.mine, 4)
        self.row = lax.rem(lax.div(self.mine, 2), 2)
        self.core = lax.rem(self.mine, 2)
        self.has_up, self.has_down = self.level < levels - 1, self.level > 0
        self.targets = {SIDE: self.mine ^ 1, ACROSS: self.mine ^ 2, UP: self.mine + 4, DOWN: self.mine - 4}

    def block(self, level, row, core):
        return level * 4 + row * 2 + core

    def greet(self):
        barrier = pltpu.get_barrier_semaphore()

        def hello(section, target):
            pl.semaphore_signal(barrier, inc=1, device_id=(section, target), device_id_type=MESH)

        hello(1 - self.section, self.mine)
        hello(self.section, self.targets[SIDE])
        hello(self.section, self.targets[ACROSS])
        pl.when(self.has_down)(lambda: hello(self.section, self.targets[DOWN]))
        pl.when(self.has_up)(lambda: hello(self.section, self.targets[UP]))
        ends = (self.level == 0).astype(jnp.int32) + (self.level == self.levels - 1).astype(jnp.int32)
        pl.semaphore_wait(barrier, 5 - ends)


class Gather:
    def __init__(self, place, shards, wholes, kinds, send_sem, recv_sem, local_sem):
        self.place, self.shards, self.wholes, self.kinds = place, shards, wholes, kinds
        self.send_sem, self.recv_sem, self.local_sem = send_sem, recv_sem, local_sem
        self.sends, self.local = Sends(), []

    def send(self, piece, block, way, own=False, when=None):
        target = self.wholes[piece](block)
        copy = pltpu.make_async_remote_copy(
            src_ref=self.shards[piece] if own else target,
            dst_ref=target,
            send_sem=self.send_sem.at[piece, block, way],
            recv_sem=self.recv_sem.at[piece, block],
            device_id=(self.place.section, self.place.targets[way]),
            device_id_type=MESH,
        )
        self.sends.start(copy, when)

    def arrived(self, piece, block, when=None):
        target = self.wholes[piece](block)
        copy = pltpu.make_async_remote_copy(
            src_ref=target,
            dst_ref=target,
            send_sem=self.send_sem.at[piece, block, 0],
            recv_sem=self.recv_sem.at[piece, block],
            device_id=(self.place.section, self.place.targets[SIDE]),
            device_id_type=MESH,
        )
        if when is None:
            copy.wait_recv()
        else:
            pl.when(when)(copy.wait_recv)

    def start(self):
        mine = self.place.mine
        for piece in range(len(self.shards)):
            self.send(piece, mine, ACROSS, own=True)
            self.send(piece, mine, UP, own=True, when=self.place.has_up)
            self.send(piece, mine, DOWN, own=True, when=self.place.has_down)
            self.send(piece, mine, SIDE, own=True)
            copy = pltpu.make_async_copy(
                self.shards[piece], self.wholes[piece](mine), self.local_sem.at[piece]
            )
            copy.start()
            self.local.append(copy)

    def first_across(self, piece):
        block = self.place.mine ^ 2
        self.arrived(piece, block)
        self.send(piece, block, UP, when=self.place.has_up)
        self.send(piece, block, DOWN, when=self.place.has_down)
        self.send(piece, block, SIDE)

    def from_levels(self, piece, distance):
        place = self.place
        plain = self.kinds[piece] == "level"
        for row in (place.row,) if plain else (place.row, 1 - place.row):
            for sign in (-1, 1):
                other = place.level + sign * distance
                here = other >= 0 if sign < 0 else other < place.levels
                onward = place.has_up if sign < 0 else place.has_down
                block = place.block(other, row, place.core)
                self.arrived(piece, block, here)
                if distance < place.levels - 1:
                    self.send(piece, block, UP if sign < 0 else DOWN, when=jnp.logical_and(here, onward))
                if plain:
                    self.send(piece, block, ACROSS, when=here)
                self.send(piece, block, SIDE, when=here)

    def from_across(self, piece, distance):
        place = self.place
        if self.kinds[piece] != "level":
            return
        for sign in (-1, 1) if distance else (1,):
            other = place.level + sign * distance
            here = None
            if distance:
                here = other >= 0 if sign < 0 else other < place.levels
            block = place.block(other, 1 - place.row, place.core)
            self.arrived(piece, block, here)
            self.send(piece, block, SIDE, when=here)

    def from_side(self, piece):
        for level in range(self.place.levels):
            for row in range(2):
                self.arrived(piece, self.place.block(level, row, 1 - self.place.core))

    def drain(self):
        for copy in self.local:
            copy.wait()
        self.sends.drain()


class Chunk:
    def __init__(self, place, order, part, start, refs, sems):
        self.place, self.order, self.levels = place, order, place.levels
        self.whole, self.start = part, start
        self.from_side, self.from_across, self.from_chain = refs
        self.cols = self.from_side.shape[2]
        (
            self.side_out,
            self.side_in,
            self.across_out,
            self.across_in,
            self.up_out,
            self.down_out,
            self.chain_in,
        ) = sems

    def part(self, block):
        return self.whole.at[block, :, pl.ds(self.start, self.cols)]

    def copy(self, block, target, out_sem, in_sem, way):
        return pltpu.make_async_remote_copy(
            src_ref=self.part(block),
            dst_ref=target,
            send_sem=out_sem,
            recv_sem=in_sem,
            device_id=(self.place.section, self.place.targets[way]),
            device_id_type=MESH,
        )

    def side(self, pair):
        block = pair * 2 + 1 - self.place.core
        return self.copy(
            block, self.from_side.at[pair], self.side_out.at[pair], self.side_in.at[pair], SIDE
        )

    def across(self, level, slot):
        block = self.place.block(level, 1 - self.place.row, self.place.core)
        return self.copy(
            block,
            self.from_across.at[slot],
            self.across_out.at[slot],
            self.across_in.at[slot],
            ACROSS,
        )

    def below_index(self, target, level):
        return target - level

    def above_index(self, target):
        return self.levels - target

    def up(self, row, slot, target):
        index = self.below_index(target, self.place.level + 1)
        return self.copy(
            self.place.block(target, row, self.place.core),
            self.from_chain.at[slot, index],
            self.up_out.at[slot, target],
            self.chain_in.at[slot, index],
            UP,
        )

    def down(self, row, slot, target):
        index = self.above_index(target)
        return self.copy(
            self.place.block(target, row, self.place.core),
            self.from_chain.at[slot, index],
            self.down_out.at[slot, target],
            self.chain_in.at[slot, index],
            DOWN,
        )

    def arrived(self, slot, index):
        target = self.from_chain.at[slot, index]
        pltpu.make_async_remote_copy(
            src_ref=target,
            dst_ref=target,
            send_sem=self.side_out.at[0],
            recv_sem=self.chain_in.at[slot, index],
            device_id=(self.place.section, self.place.targets[SIDE]),
            device_id_type=MESH,
        ).wait_recv()

    def add(self, block, term):
        part = self.part(block)
        total = part[...].astype(F32) + term.astype(F32)
        part[...] = total.astype(part.dtype)

    def send_side(self):
        @pl.loop(0, self.levels * 2)
        def _(pair):
            self.side(pair).start()

    def join_side(self):
        place = self.place
        for other in (True, False):
            row = 1 - place.row if other else place.row

            @pl.loop(0, self.levels)
            def _(level):
                pair = level * 2 + row
                self.side(pair).wait_recv()
                self.add(pair * 2 + place.core, self.from_side[pair])
                if other and self.order == ACROSS_FIRST:
                    self.across(level, level).start()

    def join_across(self):
        place = self.place

        @pl.loop(0, self.levels)
        def _(level):
            self.across(level, level).wait_recv()
            self.add(place.block(level, place.row, place.core), self.from_across[level])

    def rows(self):
        row = self.place.row
        return ((0, row), (1, 1 - row)) if self.order == LEVELS_FIRST else ((0, row),)

    def chain_start(self):
        level, last = self.place.level, self.levels - 1
        for slot, row in self.rows():
            for target in range(self.levels):
                if target:
                    pl.when(level == 0)(self.up(row, slot, self.levels - target).start)
                    pl.when(level == last)(self.down(row, slot, target - 1).start)

    def chain_pass(self, distance):
        place, last = self.place, self.levels - 1
        for slot, row in self.rows():
            for target in range(last, distance, -1):

                @pl.when(place.level == distance)
                def _():
                    index = self.below_index(target, place.level)
                    self.arrived(slot, index)
                    self.add(place.block(target, row, place.core), self.from_chain[slot, index])
                    self.up(row, slot, target).start()

            for target in range(last - distance):

                @pl.when(place.level == last - distance)
                def _():
                    index = self.above_index(target)
                    self.arrived(slot, index)
                    self.add(place.block(target, row, place.core), self.from_chain[slot, index])
                    self.down(row, slot, target).start()

    def chain_end(self, out):
        place, last = self.place, self.levels - 1
        for slot, row in reversed(self.rows()):
            block = place.block(place.level, row, place.core)

            @pl.when(place.level > 0)
            def _():
                index = self.below_index(place.level, place.level)
                self.arrived(slot, index)
                self.add(block, self.from_chain[slot, index])

            @pl.when(place.level < last)
            def _():
                index = self.above_index(place.level)
                self.arrived(slot, index)
                self.add(block, self.from_chain[slot, index])

            if slot == 1:
                self.across(place.level, 0).start()
        if self.order == ACROSS_FIRST:
            out(self.part(place.mine)[...].astype(F32))

    def finish(self, out):
        if self.order == LEVELS_FIRST:
            self.across(self.place.level, 0).wait_recv()
            out(self.part(self.place.mine)[...].astype(F32) + self.from_across[0].astype(F32))

    def drain(self):
        @pl.loop(0, self.levels * 2)
        def _(pair):
            self.side(pair).wait_send()

        if self.order == ACROSS_FIRST:

            @pl.loop(0, self.levels)
            def _(level):
                self.across(level, level).wait_send()

        else:
            self.across(self.place.level, 0).wait_send()
        for slot, row in self.rows():
            for target in range(self.levels):
                pl.when(self.place.level < target)(self.up(row, slot, target).wait_send)
                pl.when(self.place.level > target)(self.down(row, slot, target).wait_send)


def chunk_scratch(levels, order, rows, cols, dtype, shared):
    block = (rows, cols)
    slots = 2 if order == LEVELS_FIRST else 1
    crossing = 1 if order == LEVELS_FIRST else levels
    dma = pltpu.SemaphoreType.DMA
    from_side = [] if shared else [pltpu.VMEM((levels * 2,) + block, dtype)]
    return from_side + [
        pltpu.VMEM((crossing,) + block, dtype),
        pltpu.VMEM((slots, levels + 1) + block, dtype),
        dma((levels * 2,)),
        dma((levels * 2,)),
        dma((crossing,)),
        dma((crossing,)),
        dma((slots, levels)),
        dma((slots, levels)),
        dma((slots, levels + 1)),
    ]


CHUNK_REFS = 9


def pad_lanes(rows, lanes=128):
    missing = lanes - rows.shape[1]
    if not missing:
        return rows
    return jnp.concatenate([rows, jnp.zeros((rows.shape[0], missing), rows.dtype)], axis=1)


def tile_of(rows):
    missing = 8 - rows.shape[0]
    if not missing:
        return rows
    return jnp.concatenate([rows, jnp.zeros((missing, rows.shape[1]), rows.dtype)], axis=0)


def fold(line):
    pieces = [pad_lanes(line[:, at : at + 128]) for at in range(0, line.shape[1], 128)]
    return tile_of(jnp.concatenate(pieces, axis=0))


def unfold(rows, count):
    pieces = []
    for index in range(-(-count // 128)):
        pieces.append(rows[index : index + 1, : min(128, count - index * 128)])
    return jnp.concatenate(pieces, axis=1)


def relay_kernel(levels, clips, plan, *refs):
    own, attend_shard, merge_shard, up_shard, down_shard, gain_shard, shift_shard, bias_shard = refs[:8]
    out, gain_out, shift_out, attend_out, merge_out, up_out, bias_out, down_out = refs[8:16]
    (
        packed,
        vector_blocks,
        attend_blocks,
        merge_blocks,
        up_blocks,
        down_blocks,
        vectors,
        bias,
        vector_sum,
        bias_sum,
        entry,
        projected,
        probability,
        normed,
        attended,
        middle,
        normed_two,
        activated,
        slope,
        leaving,
        low_temp,
        temp,
        sum_temp,
        gather_send,
        gather_recv,
        gather_local,
        load_sem,
        send_sem,
        recv_sem,
        out_sem,
        free_sem,
    ) = refs[16:47]
    chunk_refs = list(refs[47:])
    place = Place(levels)
    section, mine = place.section, place.mine
    batches, rows, width = own.shape
    wide = up_shard.shape[1]
    ways = levels * 4
    share, wide_share = width // ways, wide // ways
    length = rows // clips
    pairs = HEADS // 2
    total = batches * rows

    load_own = pltpu.make_async_copy(own, entry.at[0], load_sem)
    load_own.start()
    packed[0:8] = pad_lanes(
        jnp.concatenate([gain_shard[...], shift_shard[...]], axis=0).astype(F32)
    )
    packed[8:16] = fold(bias_shard[...].astype(F32))
    place.greet()

    half_share = wide_share // 2
    shards = [
        packed,
        attend_shard,
        up_shard,
        merge_shard,
        down_shard.at[pl.ds(0, half_share)],
        down_shard.at[pl.ds(half_share, half_share)],
    ]
    wholes = [
        lambda block: vector_blocks.at[block],
        lambda block: attend_blocks.at[block],
        lambda block: up_blocks.at[block],
        lambda block: merge_blocks.at[block],
        lambda block: down_blocks.at[block, pl.ds(0, half_share)],
        lambda block: down_blocks.at[block, pl.ds(half_share, half_share)],
    ]
    kinds = ["level"] * 5 + ["across"]
    gather = Gather(place, shards, wholes, kinds, gather_send, gather_recv, gather_local)
    count = len(shards)
    gather.start()
    gather.first_across(count - 1)
    for distance in range(1, levels):
        for piece in range(count):
            gather.from_levels(piece, distance)
            gather.from_across(piece, distance - 1)
    for piece in range(count):
        gather.from_across(piece, levels - 1)
    for piece in range(count):
        gather.from_side(piece)
    gather.drain()
    vectors[...] = jnp.concatenate([vector_blocks[block, 0:8, 0:share] for block in range(ways)], axis=1)
    bias[...] = jnp.concatenate(
        [unfold(vector_blocks[block, 8:16], wide_share) for block in range(ways)], axis=1
    )

    def flat(blocks):
        return blocks.reshape(-1, blocks.shape[-1])

    def relay(batch):
        return pltpu.make_async_remote_copy(
            src_ref=leaving.at[batch],
            dst_ref=entry.at[1, batch],
            send_sem=send_sem.at[batch],
            recv_sem=recv_sem.at[batch],
            device_id=(1 - section, mine),
            device_id_type=MESH,
        )

    def keep(batch):
        return pltpu.make_async_copy(leaving.at[batch], out.at[batch], out_sem.at[batch])

    vector_sum[...] = jnp.zeros_like(vector_sum)
    bias_sum[...] = jnp.zeros_like(bias_sum)
    fed, back = section, 1 - section

    def row(index):
        return vectors[index : index + 1, :]

    def chances(batch, index):
        at = pl.multiple_of(batch * 4 * length + (index % 2) * 2 * length, 128)
        return probability.at[pl.ds((index // 2) * length, length), pl.ds(at, 2 * length)]

    def forward(batch):
        normal, _ = standard(entry[fed, batch].astype(F32))
        normed[batch] = (normal * row(0) + row(2)).astype(BF)
        for part, shift in ((0, 4), (1, None), (2, 5)):
            at = slice(part * width, (part + 1) * width)
            value = matmul(normed[batch], flat(attend_blocks[:, :, at]))
            if shift is not None:
                value = value + row(shift)
            projected[batch, :, at] = value.astype(BF)
        for clip in range(clips):
            span = slice(clip * length, (clip + 1) * length)
            for pair in range(pairs):
                lanes = [slice(p * width + pair * 128, p * width + pair * 128 + 128) for p in range(3)]
                query = projected[batch, span, lanes[0]] * jnp.asarray(HEAD_DIM**-0.5, BF)
                key = pair_parts(projected[batch, span, lanes[1]])
                scores = matmul(query, key, NT)
                parts = []
                for half in halves(scores):
                    exponent = jnp.exp(half - jnp.max(half, axis=-1, keepdims=True))
                    parts.append(exponent * (1.0 / jnp.sum(exponent, axis=-1, keepdims=True)))
                weight = jnp.concatenate(parts, axis=1).astype(BF)
                chances(batch, clip * pairs + pair)[...] = weight
                value = pair_parts(projected[batch, span, lanes[2]])
                attended[batch, span, lanes[0]] = matmul(weight, value).astype(BF)
        joined = matmul(attended[batch], flat(merge_blocks[...])) + row(6)
        temp[...] = entry[fed, batch].astype(F32) + joined
        middle[batch] = temp[...].astype(BF)
        normal, _ = standard(temp[...])
        normed_two[batch] = (normal * row(1) + row(3)).astype(BF)
        tile = 256
        for start in range(0, wide, tile):
            at = slice(start, start + tile)
            value, rate = gelu_and_slope(
                matmul(normed_two[batch], flat(up_blocks[:, :, at])) + bias[:, at]
            )
            activated[batch, :, at] = value.astype(BF)
            slope[batch, :, at] = rate.astype(BF)
        result = temp[...] + matmul(activated[batch], flat(down_blocks[...])) + row(7)
        leaving[batch] = result.astype(BF)

    def backward(batch):
        low = entry[back, batch]
        vector_sum[7:8] += column_sum(low.astype(F32))
        blocks = 4
        for block in range(0, ways, blocks):
            at = slice(block * wide_share, (block + blocks) * wide_share)
            rate = matmul(low, flat(down_blocks[block : block + blocks]), NT)
            rate = rate * slope[batch, :, at].astype(F32)
            bias_sum[:, at] += column_sum(rate)
            slope[batch, :, at] = rate.astype(BF)
        temp[...] = matmul(slope[batch], flat(up_blocks[...]), NT)
        normal, scale = standard(middle[batch].astype(F32))
        grad = temp[...]
        vector_sum[1:2] += column_sum(grad * normal)
        vector_sum[3:4] += column_sum(grad)
        grad = entry[back, batch].astype(F32) + norm_back(grad * row(1), normal, scale)
        sum_temp[...] = grad
        vector_sum[6:7] += column_sum(grad)
        middle[batch] = grad.astype(BF)
        low_temp[...] = matmul(middle[batch], flat(merge_blocks[...]), NT).astype(BF)
        for clip in range(clips):
            span = slice(clip * length, (clip + 1) * length)
            for pair in range(pairs):
                lanes = [slice(p * width + pair * 128, p * width + pair * 128 + 128) for p in range(3)]
                query = projected[batch, span, lanes[0]]
                key = pair_parts(projected[batch, span, lanes[1]])
                value = pair_parts(projected[batch, span, lanes[2]])
                upper = low_temp[span, lanes[0]]
                weight = chances(batch, clip * pairs + pair)[...]
                rise = matmul(upper, value, NT)
                value_grad = pair_join(matmul(weight, upper, TN))
                parts = []
                for part, heavy in zip(halves(rise), halves(weight)):
                    heavy = heavy.astype(F32)
                    mean = jnp.sum(part * heavy, axis=-1, keepdims=True)
                    parts.append(heavy * (part - mean) * HEAD_DIM**-0.5)
                change = jnp.concatenate(parts, axis=1).astype(BF)
                query_grad = matmul(change, key)
                key_grad = pair_join(matmul(change, query, TN))
                vector_sum[4:5, lanes[0]] += column_sum(query_grad)
                vector_sum[5:6, lanes[0]] += column_sum(value_grad)
                for at, piece in zip(lanes, (query_grad, key_grad, value_grad)):
                    projected[batch, span, at] = piece.astype(BF)
        temp[...] = matmul(projected[batch], flat(attend_blocks[...]), NT)
        normal, scale = standard(entry[fed, batch].astype(F32))
        grad = temp[...]
        vector_sum[0:1] += column_sum(grad * normal)
        vector_sum[2:3] += column_sum(grad)
        leaving[batch] = (sum_temp[...] + norm_back(grad * row(0), normal, scale)).astype(BF)

    load_own.wait()

    @pl.loop(0, 2 * batches)
    def _(step):
        is_forward = jnp.where(section == 0, step < batches, lax.rem(step, 2) == 0)
        batch = jnp.where(section == 0, lax.rem(step, batches), lax.div(step, 2))

        @pl.when(is_forward)
        def _():
            pl.when(section == 1)(relay(batch).wait_recv)
            forward(batch)
            pl.when(section == 0)(relay(batch).start)
            pl.when(section == 1)(keep(batch).start)

        @pl.when(jnp.logical_not(is_forward))
        def _():
            pl.when(section == 0)(relay(batch).wait)
            pl.when(section == 1)(keep(batch).wait)
            backward(batch)
            pl.when(section == 1)(relay(batch).start)
            pl.when(section == 0)(keep(batch).start)

    chunks = []
    part_refs = [vector_blocks, attend_blocks, merge_blocks, up_blocks, down_blocks]
    for which, start, order, _, cols, _, shared in plan:
        if shared is None:
            from_side = chunk_refs.pop(0)
        else:
            from_side = chunks[shared].from_side.at[:, :, pl.ds(0, cols)]
        held, chunk_refs = chunk_refs[:CHUNK_REFS], chunk_refs[CHUNK_REFS:]
        chunks.append(Chunk(place, order, part_refs[which], start, [from_side] + held[:2], held[2:]))
    down_a, down_b, up_a, up_b, attend_a, attend_b, merge, vector = chunks

    def store(target, chunk):
        def put(value):
            target[:, pl.ds(chunk.start, chunk.cols)] = value

        return put

    def turn(source, place_at):
        target = probability.at[pl.ds(0, width), pl.ds(place_at * total, total)]
        target[...] = flat(source[...]).T
        return target

    def columns(left, source, chunk, credit=None):
        step = 128 * max(d for d in (1, 2, 3) if chunk.cols % (128 * d) == 0)

        @pl.loop(0, chunk.cols // step)
        def _(index):
            at = pl.multiple_of(chunk.start + index * step, 128)
            product = matmul(left[...], flat(source[:, :, pl.ds(at, step)]))
            chunk.whole[:, :, pl.ds(at, step)] = product.astype(BF).reshape(ways, width // ways, step)

        if credit is not None:
            pl.semaphore_wait(free_sem.at[credit], 1)
        chunk.send_side()

    def release(index):
        pl.semaphore_signal(
            free_sem.at[index], inc=1, device_id=(section, place.targets[SIDE]), device_id_type=MESH
        )

    pair_cols = 2 * wide_share

    @pl.loop(0, levels * 2)
    def _(pair):
        tile = flat(activated[:, :, pl.ds(pl.multiple_of(pair * pair_cols, 128), pair_cols)])
        for chunk in (down_a, down_b):
            at = pl.ds(chunk.start, chunk.cols)
            product = matmul(tile, flat(entry[back, :, :, at]), TN).astype(BF)
            for core in range(2):
                down_blocks[pair * 2 + core, :, at] = product[core * wide_share : (core + 1) * wide_share]
            chunk.side(pair).start()

    for block in range(ways):
        vector_blocks[block, 0:8] = pad_lanes(vector_sum[:, block * share : (block + 1) * share])
        vector_blocks[block, 8:16] = fold(bias_sum[:, block * wide_share : (block + 1) * wide_share])
    vector.send_side()
    down_a.join_side()
    down_a.chain_start()
    down_b.join_side()
    vector.join_side()
    turned = turn(normed_two, 0)
    columns(turned, slope, up_a)
    columns(turned, slope, up_b)
    up_a.join_side()
    release(0)
    down_a.chain_pass(1)
    up_b.join_side()
    release(1)
    turned = turn(normed, 1)
    columns(turned, projected, attend_a, 0)
    down_a.chain_pass(2)
    down_b.join_across()
    down_b.chain_start()
    vector.join_across()
    vector.chain_start()
    columns(turned, projected, attend_b, 1)
    attend_a.join_side()
    turned = turn(attended, 0)
    columns(turned, middle, merge)
    attend_b.join_side()
    down_b.chain_pass(1)
    merge.join_side()
    down_a.chain_end(None)
    up_a.join_across()
    up_a.chain_start()
    down_b.chain_pass(2)
    vector.chain_pass(1)
    up_a.chain_pass(1)
    up_b.join_across()
    up_b.chain_start()
    vector.chain_pass(2)
    down_b.chain_end(store(down_out, down_b))
    up_a.chain_pass(2)
    up_b.chain_pass(1)
    attend_a.join_across()
    attend_a.chain_start()

    def store_vectors(value):
        gain_out[...] = value[0:2, :share]
        shift_out[...] = value[2:8, :share]
        bias_out[...] = unfold(value[8:16], wide_share)

    vector.chain_end(store_vectors)
    up_a.chain_end(store(up_out, up_a))
    up_b.chain_pass(2)
    attend_a.chain_pass(1)
    attend_b.join_across()
    attend_b.chain_start()
    up_b.chain_end(store(up_out, up_b))
    attend_a.chain_pass(2)
    attend_b.chain_pass(1)
    merge.join_across()
    merge.chain_start()
    attend_a.chain_end(store(attend_out, attend_a))
    attend_b.chain_pass(2)
    merge.chain_pass(1)
    attend_b.chain_end(store(attend_out, attend_b))
    merge.chain_pass(2)
    down_a.finish(store(down_out, down_a))
    merge.chain_end(store(merge_out, merge))
    for chunk in chunks:
        chunk.drain()

    @pl.loop(0, batches)
    def _(batch):
        pl.when(section == 1)(relay(batch).wait_send)
        pl.when(section == 0)(keep(batch).wait)


def train_step(own, attend, merge, up, down, gains, shifts, bias, clips, ways, collective_id):
    levels = ways // 4
    batches, rows, width = own.shape
    wide = up.shape[1]
    share, wide_share = width // ways, wide // ways
    length = rows // clips
    plan = [
        (4, 0, LEVELS_FIRST, wide_share, width // 2, BF, None),
        (4, width // 2, ACROSS_FIRST, wide_share, width // 2, BF, None),
        (3, 0, ACROSS_FIRST, share, wide // 2, BF, None),
        (3, wide // 2, ACROSS_FIRST, share, wide // 2, BF, None),
        (1, 0, ACROSS_FIRST, share, 3 * width // 2, BF, 2),
        (1, 3 * width // 2, ACROSS_FIRST, share, 3 * width // 2, BF, 3),
        (2, 0, ACROSS_FIRST, share, width, BF, None),
        (0, 0, ACROSS_FIRST, 16, 128, F32, None),
    ]
    dma = pltpu.SemaphoreType.DMA
    vmem, anywhere = pl.BlockSpec(memory_space=pltpu.VMEM), pl.BlockSpec(memory_space=pl.ANY)

    def held(cols, dtype=BF):
        return pltpu.VMEM((batches, rows, cols), dtype)

    scratch = [
        pltpu.VMEM((16, 128), F32),
        pltpu.VMEM((ways, 16, 128), F32),
        pltpu.VMEM((ways, share, 3 * width), BF),
        pltpu.VMEM((ways, share, width), BF),
        pltpu.VMEM((ways, share, wide), BF),
        pltpu.VMEM((ways, wide_share, width), BF),
        pltpu.VMEM((8, width), F32),
        pltpu.VMEM((1, wide), F32),
        pltpu.VMEM((8, width), F32),
        pltpu.VMEM((1, wide), F32),
        pltpu.VMEM((2, batches, rows, width), BF),
        held(3 * width),
        pltpu.VMEM((clips * HEADS // 4 * length, batches * 4 * length), BF),
        held(width),
        held(width),
        held(width),
        held(width),
        held(wide),
        held(wide),
        held(width),
        pltpu.VMEM((rows, width), BF),
        pltpu.VMEM((rows, width), F32),
        pltpu.VMEM((rows, width), F32),
        dma((6, ways, 4)),
        dma((6, ways)),
        dma((6,)),
        dma(()),
        dma((batches,)),
        dma((batches,)),
        dma((batches,)),
        pltpu.SemaphoreType.REGULAR((2,)),
    ]
    for _, _, order, chunk_rows, cols, dtype, shared in plan:
        scratch += chunk_scratch(levels, order, chunk_rows, cols, dtype, shared is not None)

    def grad(*shape):
        return jax.ShapeDtypeStruct(shape, F32)

    return pl.pallas_call(
        functools.partial(relay_kernel, levels, clips, plan),
        out_shape=[
            jax.ShapeDtypeStruct(own.shape, BF),
            grad(2, share),
            grad(6, share),
            grad(share, 3 * width),
            grad(share, width),
            grad(share, wide),
            grad(1, wide_share),
            grad(wide_share, width),
        ],
        in_specs=[anywhere] * 5 + [vmem] * 3,
        out_specs=[anywhere] + [vmem] * 7,
        scratch_shapes=scratch,
        compiler_params=pltpu.CompilerParams(
            collective_id=collective_id, has_side_effects=True, vmem_limit_bytes=63 * 2**20
        ),
    )(own, attend, merge, up, down, gains, shifts, bias)


def from_behind(block, axis, distance):
    devices = range(lax.axis_size(axis))
    route = [(i - distance, i) for i in devices if i - distance in devices]
    return lax.ppermute(block, axis, route)


def normalize(features, gain_row, offset):
    centred = features - jnp.mean(features, axis=-1, keepdims=True)
    spread = jnp.mean(centred * centred, axis=-1, keepdims=True)
    return centred * lax.rsqrt(spread + epsilon) * gain_row + offset


def gelu_exact(features):
    return jax.nn.gelu(features, approximate=False)


def split_heads(matrix, clip_count):
    return matrix.reshape(clip_count, matrix.shape[0] // clip_count, HEADS, HEAD_DIM)


def layer_forward(hidden, weights, clip_count):
    attend_weight, merge_weight, up_weight, down_weight, gain_rows, offset_rows, up_bias = weights
    gain_rows = gain_rows.astype(jnp.float32)
    offset_rows = offset_rows.astype(jnp.float32)
    row_count, model_width = hidden.shape
    score_scale = HEAD_DIM ** (-0.5)
    normed = normalize(hidden, gain_rows[0], offset_rows[0]).astype(jnp.bfloat16)
    projected = jnp.dot(normed, attend_weight, preferred_element_type=jnp.float32)
    query_heads = split_heads(
        (projected[:, :model_width] + offset_rows[2]).astype(jnp.bfloat16), clip_count
    )
    key_heads = split_heads(
        projected[:, model_width : 2 * model_width].astype(jnp.bfloat16), clip_count
    )
    value_heads = split_heads(
        (projected[:, 2 * model_width :] + offset_rows[3]).astype(jnp.bfloat16), clip_count
    )
    scores = (
        jnp.einsum("clhe,cmhe->chlm", query_heads, key_heads, preferred_element_type=jnp.float32)
        * score_scale
    )
    row_peak = jnp.max(scores, axis=-1, keepdims=True)
    exponent = jnp.exp(scores - row_peak)
    row_total = jnp.sum(exponent, axis=-1, keepdims=True)
    probability = (exponent / row_total).astype(jnp.bfloat16)
    log_total = (row_peak + jnp.log(row_total))[..., 0]
    attended = jnp.einsum(
        "chlm,cmhe->clhe", probability, value_heads, preferred_element_type=jnp.float32
    )
    attended = attended.reshape(row_count, model_width).astype(jnp.bfloat16)
    middle = (
        hidden
        + jnp.dot(attended, merge_weight, preferred_element_type=jnp.float32)
        + offset_rows[4]
    )
    normed_two = normalize(middle, gain_rows[1], offset_rows[1]).astype(jnp.bfloat16)
    raised = jnp.dot(normed_two, up_weight, preferred_element_type=jnp.float32) + up_bias.astype(
        jnp.float32
    )
    activated = gelu_exact(raised).astype(jnp.bfloat16)
    result = (
        middle
        + jnp.dot(activated, down_weight, preferred_element_type=jnp.float32)
        + offset_rows[5]
    )
    saved_state = (
        hidden,
        normed,
        query_heads,
        key_heads,
        value_heads,
        log_total,
        attended,
        middle,
        normed_two,
        raised,
        activated,
    )
    return (result, saved_state)


def layer_backward(out_grad, saved_state, weights, clip_count):
    attend_weight, merge_weight, up_weight, down_weight, gain_rows, offset_rows, up_bias = weights
    gain_rows = gain_rows.astype(jnp.float32)
    offset_rows = offset_rows.astype(jnp.float32)
    (
        hidden,
        normed,
        query_heads,
        key_heads,
        value_heads,
        log_total,
        attended,
        middle,
        normed_two,
        raised,
        activated,
    ) = saved_state
    row_count, model_width = hidden.shape
    score_scale = HEAD_DIM ** (-0.5)
    low_grad = out_grad.astype(jnp.bfloat16)
    down_term = jnp.einsum("tf,td->fd", activated, low_grad, preferred_element_type=jnp.float32)
    last_bias = jnp.sum(out_grad, axis=0)
    act_grad = jnp.einsum("td,fd->tf", low_grad, down_weight, preferred_element_type=jnp.float32)
    raised_grad = jax.vjp(gelu_exact, raised)[1](act_grad)[0]
    up_bias_term = jnp.sum(raised_grad, axis=0)
    raised_low = raised_grad.astype(jnp.bfloat16)
    up_term = jnp.einsum("td,tf->df", normed_two, raised_low, preferred_element_type=jnp.float32)
    normed_two_grad = jnp.einsum(
        "tf,df->td", raised_low, up_weight, preferred_element_type=jnp.float32
    )
    second_back = jax.vjp(normalize, middle, gain_rows[1], offset_rows[1])[1]
    middle_part, gain_two, offset_two = second_back(normed_two_grad)
    middle_grad = out_grad + middle_part
    merge_bias = jnp.sum(middle_grad, axis=0)
    middle_low = middle_grad.astype(jnp.bfloat16)
    merge_term = jnp.einsum("td,te->de", attended, middle_low, preferred_element_type=jnp.float32)
    attended_grad = jnp.einsum(
        "te,de->td", middle_low, merge_weight, preferred_element_type=jnp.float32
    )
    attended_grad = split_heads(attended_grad.astype(jnp.bfloat16), clip_count)
    scores = (
        jnp.einsum("clhe,cmhe->chlm", query_heads, key_heads, preferred_element_type=jnp.float32)
        * score_scale
    )
    probability = jnp.exp(scores - log_total[..., None])
    prob_grad = jnp.einsum(
        "clhe,cmhe->chlm", attended_grad, value_heads, preferred_element_type=jnp.float32
    )
    value_grad = jnp.einsum(
        "chlm,clhe->cmhe",
        probability.astype(jnp.bfloat16),
        attended_grad,
        preferred_element_type=jnp.float32,
    )
    score_grad = probability * (
        prob_grad - jnp.sum(prob_grad * probability, axis=-1, keepdims=True)
    )
    score_grad = score_grad.astype(jnp.bfloat16)
    query_grad = (
        jnp.einsum("chlm,cmhe->clhe", score_grad, key_heads, preferred_element_type=jnp.float32)
        * score_scale
    )
    key_grad = (
        jnp.einsum("chlm,clhe->cmhe", score_grad, query_heads, preferred_element_type=jnp.float32)
        * score_scale
    )
    query_grad = query_grad.reshape(row_count, model_width)
    key_grad = key_grad.reshape(row_count, model_width)
    value_grad = value_grad.reshape(row_count, model_width)
    query_bias = jnp.sum(query_grad, axis=0)
    value_bias = jnp.sum(value_grad, axis=0)
    joined_low = jnp.concatenate([query_grad, key_grad, value_grad], axis=1).astype(jnp.bfloat16)
    attend_term = jnp.einsum("td,te->de", normed, joined_low, preferred_element_type=jnp.float32)
    normed_grad = jnp.einsum(
        "te,de->td", joined_low, attend_weight, preferred_element_type=jnp.float32
    )
    first_back = jax.vjp(normalize, hidden, gain_rows[0], offset_rows[0])[1]
    hidden_part, gain_one, offset_one = first_back(normed_grad)
    hidden_grad = middle_grad + hidden_part
    gain_term = jnp.stack([gain_one, gain_two])
    offset_term = jnp.stack([offset_one, offset_two, query_bias, value_bias, merge_bias, last_bias])
    return (
        hidden_grad,
        (attend_term, merge_term, up_term, down_term, gain_term, offset_term, up_bias_term),
    )


def plain_body(
    section_inputs,
    norm_gains,
    offsets,
    attend_weight,
    merge_weight,
    up_weight,
    up_bias,
    down_weight,
):
    shards = (attend_weight, merge_weight, up_weight, down_weight, norm_gains, offsets, up_bias)
    gathered = (
        lax.all_gather(shards[0], "fsdp", axis=1, tiled=True),
        lax.all_gather(shards[1], "fsdp", axis=1, tiled=True),
        lax.all_gather(shards[2], "fsdp", axis=1, tiled=True),
        lax.all_gather(shards[3], "fsdp", axis=1, tiled=True),
        lax.all_gather(shards[4], "fsdp", axis=2, tiled=True),
        lax.all_gather(shards[5], "fsdp", axis=2, tiled=True),
        lax.all_gather(shards[6], "fsdp", axis=1, tiled=True),
    )
    weights = tuple((tensor[0] for tensor in gathered))
    is_first = lax.axis_index("section") == 0
    own_data = section_inputs[0]
    batches, clip_count, length, model_width = own_data.shape
    row_count = clip_count * length
    own_rows = own_data.reshape(batches, row_count, model_width)
    kept_state = []
    upper_rows = []
    received = jnp.zeros((row_count, model_width), jnp.bfloat16)
    for instant in range(batches + 1):
        entering = jnp.where(is_first, own_rows[min(instant, batches - 1)], received)
        result, saved_state = layer_forward(entering.astype(jnp.float32), weights, clip_count)
        kept_state.append(saved_state)
        rounded = result.astype(jnp.bfloat16)
        if instant >= 1:
            upper_rows.append(rounded)
        if instant < batches:
            received = from_behind(rounded, "section", 1)
    gathered = (
        lax.all_gather(shards[0], "fsdp", axis=1, tiled=True),
        lax.all_gather(shards[1], "fsdp", axis=1, tiled=True),
        lax.all_gather(shards[2], "fsdp", axis=1, tiled=True),
        lax.all_gather(shards[3], "fsdp", axis=1, tiled=True),
        lax.all_gather(shards[4], "fsdp", axis=2, tiled=True),
        lax.all_gather(shards[5], "fsdp", axis=2, tiled=True),
        lax.all_gather(shards[6], "fsdp", axis=1, tiled=True),
    )
    weights = tuple((tensor[0] for tensor in gathered))
    totals = (
        jnp.zeros(weights[0].shape, jnp.float32),
        jnp.zeros(weights[1].shape, jnp.float32),
        jnp.zeros(weights[2].shape, jnp.float32),
        jnp.zeros(weights[3].shape, jnp.float32),
        jnp.zeros(weights[4].shape, jnp.float32),
        jnp.zeros(weights[5].shape, jnp.float32),
        jnp.zeros(weights[6].shape, jnp.float32),
    )
    received_grad = jnp.zeros((row_count, model_width), jnp.bfloat16)
    lower_rows = []
    for instant in range(batches + 1):
        position = batches - 1 - instant
        if position >= 0:
            own_grad = own_rows[position]
        else:
            own_grad = jnp.zeros((row_count, model_width), jnp.bfloat16)
        cotangent = jnp.where(is_first, received_grad, own_grad).astype(jnp.float32)
        hidden_grad, param_terms = layer_backward(
            cotangent, kept_state[batches - instant], weights, clip_count
        )
        totals = jax.tree.map(jnp.add, totals, param_terms)
        rounded = hidden_grad.astype(jnp.bfloat16)
        if instant >= 1:
            lower_rows.append(rounded)
        if instant < batches:
            received_grad = from_behind(rounded, "section", -1)
    ordered_lower = lower_rows[::-1]
    combined = jnp.stack(
        [
            jnp.where(is_first, lower_part, upper_part)
            for lower_part, upper_part in zip(ordered_lower, upper_rows)
        ]
    )
    section_outputs = combined.reshape(1, batches, clip_count, length, model_width)
    reduced = (
        lax.psum_scatter(totals[0][None], "fsdp", scatter_dimension=1, tiled=True),
        lax.psum_scatter(totals[1][None], "fsdp", scatter_dimension=1, tiled=True),
        lax.psum_scatter(totals[2][None], "fsdp", scatter_dimension=1, tiled=True),
        lax.psum_scatter(totals[3][None], "fsdp", scatter_dimension=1, tiled=True),
        lax.psum_scatter(totals[4][None], "fsdp", scatter_dimension=2, tiled=True),
        lax.psum_scatter(totals[5][None], "fsdp", scatter_dimension=2, tiled=True),
        lax.psum_scatter(totals[6][None], "fsdp", scatter_dimension=1, tiled=True),
    )
    return (
        section_outputs,
        reduced[4],
        reduced[5],
        reduced[0],
        reduced[1],
        reduced[2],
        reduced[6],
        reduced[3],
    )


def body(
    section_inputs,
    norm_gains,
    offsets,
    attend_weight,
    merge_weight,
    up_weight,
    up_bias,
    down_weight,
):
    ways = lax.axis_size("fsdp")
    if ways % 4 or attend_weight.shape[1] % 16:
        return plain_body(
            section_inputs,
            norm_gains,
            offsets,
            attend_weight,
            merge_weight,
            up_weight,
            up_bias,
            down_weight,
        )
    batches, clips, length, width = section_inputs.shape[1:]
    own = section_inputs.reshape(batches, clips * length, width)
    results = train_step(
        own,
        attend_weight[0],
        merge_weight[0],
        up_weight[0],
        down_weight[0],
        norm_gains[0],
        offsets[0],
        up_bias,
        clips,
        ways,
        1,
    )
    section_outputs, gains, shifts, attend, merge, up, bias, down = results
    return (
        section_outputs.reshape(section_inputs.shape),
        gains[None],
        shifts[None],
        attend[None],
        merge[None],
        up[None],
        bias,
        down[None],
    )


def solution(mesh):
    return jax.shard_map(
        body,
        mesh=mesh,
        in_specs=(
            P("section", None, "fsdp", None, None),
            P("section", None, "fsdp"),
            P("section", None, "fsdp"),
            P("section", "fsdp", None),
            P("section", "fsdp", None),
            P("section", "fsdp", None),
            P("section", "fsdp"),
            P("section", "fsdp", None),
        ),
        out_specs=(
            P("section", None, "fsdp", None, None),
            P("section", None, "fsdp"),
            P("section", None, "fsdp"),
            P("section", "fsdp", None),
            P("section", "fsdp", None),
            P("section", "fsdp", None),
            P("section", "fsdp"),
            P("section", "fsdp", None),
        ),
        check_vma=False,
    )
```

```python
import functools
import math

import jax
import jax.numpy as jnp
from jax import lax
from jax.experimental import pallas as pl
from jax.experimental.pallas import tpu as pltpu
from jax.sharding import PartitionSpec as P

MESH = pl.DeviceIdType.MESH

HEADS = 12
HEAD_DIM = 64
epsilon = 1e-05
BF, F32 = jnp.bfloat16, jnp.float32
NT = (((1,), (1,)), ((), ()))
TN = (((0,), (0,)), ((), ()))

SIDE, ACROSS, UP, DOWN = range(4)
LEVELS_FIRST, ACROSS_FIRST = 0, 1

class Sends:
    def __init__(self):
        self.items = []

    def start(self, copy, when):
        if when is None:
            copy.start()
        else:
            pl.when(when)(copy.start)
        self.items.append((copy, when))

    def drain(self):
        for copy, when in self.items:
            if when is None:
                copy.wait_send()
            else:
                pl.when(when)(copy.wait_send)


def matmul(left, right, dims=(((1,), (0,)), ((), ()))):
    return lax.dot_general(left, right, dims, preferred_element_type=F32)


def standard(features):
    centred = features - jnp.mean(features, axis=-1, keepdims=True)
    scale = lax.rsqrt(jnp.mean(centred * centred, axis=-1, keepdims=True) + epsilon)
    return centred * scale, scale


def gelu_and_slope(raised):
    share = 0.5 + 0.5 * lax.erf(raised * math.sqrt(0.5))
    bell = jnp.exp(raised * raised * -0.5) * (1.0 / math.sqrt(2.0 * math.pi))
    return raised * share, share + raised * bell


def norm_back(upper, normal, scale):
    shift = jnp.mean(upper, axis=-1, keepdims=True)
    slope = jnp.mean(upper * normal, axis=-1, keepdims=True)
    return (upper - shift - normal * slope) * scale


def column_sum(values):
    return jnp.sum(values, axis=0, keepdims=True)


def pair_parts(matrix):
    lane = lax.broadcasted_iota(jnp.int32, matrix.shape, 1)
    zero = jnp.zeros_like(matrix)
    first = lane < HEAD_DIM
    return jnp.concatenate([jnp.where(first, matrix, zero), jnp.where(first, zero, matrix)], axis=0)


def pair_join(stacked):
    rows = stacked.shape[0] // 2
    lane = lax.broadcasted_iota(jnp.int32, (rows, stacked.shape[1]), 1)
    return jnp.where(lane < HEAD_DIM, stacked[:rows], stacked[rows:])


def halves(scores):
    keys = scores.shape[1] // 2
    return scores[:, :keys], scores[:, keys:]


class Place:
    def __init__(self, levels):
        self.levels = levels
        self.section, self.mine = lax.axis_index("section"), lax.axis_index("fsdp")
        self.level = lax.div(self.mine, 4)
        self.row = lax.rem(lax.div(self.mine, 2), 2)
        self.core = lax.rem(self.mine, 2)
        self.has_up, self.has_down = self.level < levels - 1, self.level > 0
        self.targets = {SIDE: self.mine ^ 1, ACROSS: self.mine ^ 2, UP: self.mine + 4, DOWN: self.mine - 4}

    def block(self, level, row, core):
        return level * 4 + row * 2 + core

    def greet(self):
        barrier = pltpu.get_barrier_semaphore()

        def hello(section, target):
            pl.semaphore_signal(barrier, inc=1, device_id=(section, target), device_id_type=MESH)

        hello(1 - self.section, self.mine)
        hello(self.section, self.targets[SIDE])
        hello(self.section, self.targets[ACROSS])
        pl.when(self.has_down)(lambda: hello(self.section, self.targets[DOWN]))
        pl.when(self.has_up)(lambda: hello(self.section, self.targets[UP]))
        ends = (self.level == 0).astype(jnp.int32) + (self.level == self.levels - 1).astype(jnp.int32)
        pl.semaphore_wait(barrier, 5 - ends)


class Piece:
    def __init__(self, shard, ref, kind, start=0, size=None):
        self.shard, self.ref, self.plain = shard, ref, kind == "level"
        self.rows = None if size is None else pl.ds(start, size)

    def block(self, index):
        return self.ref.at[index] if self.rows is None else self.ref.at[index, self.rows]

    def span(self, count):
        return self.block(pl.ds(0, count))


class Gather:
    def __init__(self, place, pieces, send_sem, recv_sem, local_sem):
        self.place, self.pieces = place, pieces
        self.send_sem, self.recv_sem, self.local_sem = send_sem, recv_sem, local_sem
        self.side = 2 * place.levels

    def copy(self, source, target, out_sem, in_sem, way):
        return pltpu.make_async_remote_copy(
            src_ref=source,
            dst_ref=target,
            send_sem=out_sem,
            recv_sem=in_sem,
            device_id=(self.place.section, self.place.targets[way]),
            device_id_type=MESH,
        )

    def send(self, piece, level, row, way, own=False, when=None):
        held = self.pieces[piece]
        target = held.block(self.place.block(level, row, self.place.core))
        kind = {SIDE: 0, ACROSS: 1, UP: 2, DOWN: 2}[way]
        copy = self.copy(
            held.shard if own else target,
            target,
            self.send_sem.at[piece, kind],
            self.recv_sem.at[piece, self.side if way == SIDE else level * 2 + row],
            way,
        )
        if when is None:
            copy.start()
        else:
            pl.when(when)(copy.start)

    def arrived(self, piece, level, row, when=None):
        target = self.pieces[piece].block(self.place.block(level, row, self.place.core))
        index = level * 2 + row
        copy = self.copy(target, target, self.send_sem.at[piece, 0], self.recv_sem.at[piece, index], SIDE)
        if when is None:
            copy.wait_recv()
        else:
            pl.when(when)(copy.wait_recv)

    def local(self, piece):
        held = self.pieces[piece]
        return pltpu.make_async_copy(held.shard, held.block(self.place.mine), self.local_sem.at[piece])

    def start(self, piece):
        place = self.place
        self.send(piece, place.level, place.row, ACROSS, own=True)
        self.send(piece, place.level, place.row, UP, own=True, when=place.has_up)
        self.send(piece, place.level, place.row, DOWN, own=True, when=place.has_down)
        self.send(piece, place.level, place.row, SIDE, own=True)
        self.local(piece).start()

    def first_across(self, piece):
        place = self.place
        level, row = place.level, 1 - place.row
        self.arrived(piece, level, row)
        self.send(piece, level, row, UP, when=place.has_up)
        self.send(piece, level, row, DOWN, when=place.has_down)
        self.send(piece, level, row, SIDE)

    def from_levels(self, piece, distance):
        place = self.place
        plain = self.pieces[piece].plain
        for row in (place.row,) if plain else (place.row, 1 - place.row):
            for sign in (-1, 1):
                other = place.level + sign * distance
                here = other >= 0 if sign < 0 else other < place.levels
                onward = place.has_up if sign < 0 else place.has_down
                self.arrived(piece, other, row, here)
                if distance < place.levels - 1:
                    way = UP if sign < 0 else DOWN
                    self.send(piece, other, row, way, when=jnp.logical_and(here, onward))
                if plain:
                    self.send(piece, other, row, ACROSS, when=here)
                self.send(piece, other, row, SIDE, when=here)

    def from_across(self, piece, distance):
        place = self.place
        if not self.pieces[piece].plain:
            return
        for sign in (-1, 1) if distance else (1,):
            other = place.level + sign * distance
            here = None
            if distance:
                here = other >= 0 if sign < 0 else other < place.levels
            self.arrived(piece, other, 1 - place.row, here)
            self.send(piece, other, 1 - place.row, SIDE, when=here)

    def from_side(self, piece):
        span = self.pieces[piece].span(self.side)
        self.copy(span, span, self.send_sem.at[piece, 0], self.recv_sem.at[piece, self.side], SIDE).wait_recv()

    def drain(self, piece):
        place, held = self.place, self.pieces[piece]

        def sent(count, kind):
            span = held.span(count)
            return self.copy(span, span, self.send_sem.at[piece, kind], self.recv_sem.at[piece, 0], SIDE)

        rows = 1 if held.plain else 2
        self.local(piece).wait()
        sent(self.side, 0).wait_send()
        sent(place.levels if held.plain else 1, 1).wait_send()
        inner = jnp.logical_and(place.has_up, place.has_down)
        pl.when(inner)(sent(rows * (place.levels + 1), 2).wait_send)
        pl.when(jnp.logical_not(inner))(sent(rows, 2).wait_send)


class Chunk:
    def __init__(self, place, order, part, start, refs, sems):
        self.place, self.order, self.levels = place, order, place.levels
        self.whole, self.start = part, start
        self.from_side, self.from_across, self.from_chain = refs
        self.cols = self.from_side.shape[2]
        (
            self.side_out,
            self.side_in,
            self.across_out,
            self.across_in,
            self.chain_out,
            self.chain_in,
        ) = sems

    def part(self, block):
        return self.whole.at[block, :, pl.ds(self.start, self.cols)]

    def copy(self, block, target, out_sem, in_sem, way):
        return pltpu.make_async_remote_copy(
            src_ref=self.part(block),
            dst_ref=target,
            send_sem=out_sem,
            recv_sem=in_sem,
            device_id=(self.place.section, self.place.targets[way]),
            device_id_type=MESH,
        )

    def side(self, pair):
        block = pair * 2 + 1 - self.place.core
        return self.copy(
            block, self.from_side.at[pair], self.side_out, self.side_in.at[pair], SIDE
        )

    def across(self, level, slot):
        block = self.place.block(level, 1 - self.place.row, self.place.core)
        return self.copy(
            block,
            self.from_across.at[slot],
            self.across_out,
            self.across_in.at[slot],
            ACROSS,
        )

    def below_index(self, target, level):
        return target - level

    def above_index(self, target):
        return self.levels - target

    def up(self, row, slot, target):
        index = self.below_index(target, self.place.level + 1)
        return self.copy(
            self.place.block(target, row, self.place.core),
            self.from_chain.at[slot, index],
            self.chain_out.at[slot],
            self.chain_in.at[slot, index],
            UP,
        )

    def down(self, row, slot, target):
        index = self.above_index(target)
        return self.copy(
            self.place.block(target, row, self.place.core),
            self.from_chain.at[slot, index],
            self.chain_out.at[slot],
            self.chain_in.at[slot, index],
            DOWN,
        )

    def arrived(self, slot, index):
        target = self.from_chain.at[slot, index]
        pltpu.make_async_remote_copy(
            src_ref=target,
            dst_ref=target,
            send_sem=self.side_out,
            recv_sem=self.chain_in.at[slot, index],
            device_id=(self.place.section, self.place.targets[SIDE]),
            device_id_type=MESH,
        ).wait_recv()

    def add(self, block, term):
        part = self.part(block)
        part[...] = part[...] + term

    def send_side(self):
        @pl.loop(0, self.levels * 2)
        def _(pair):
            self.side(pair).start()

    def join_pair(self, level, row):
        pair = level * 2 + row
        self.side(pair).wait_recv()
        self.add(pair * 2 + self.place.core, self.from_side[pair])

    def join_side(self):
        place = self.place
        for other in (True, False):
            row = 1 - place.row if other else place.row

            @pl.loop(0, self.levels)
            def _(level):
                self.join_pair(level, row)
                if other and self.order == ACROSS_FIRST:
                    self.across(level, level).start()

    def join_across(self):
        place = self.place

        @pl.loop(0, self.levels)
        def _(level):
            self.across(level, level).wait_recv()
            self.add(place.block(level, place.row, place.core), self.from_across[level])

    def rows(self):
        row = self.place.row
        return ((0, row), (1, 1 - row)) if self.order == LEVELS_FIRST else ((0, row),)

    def chain_start(self):
        level, last = self.place.level, self.levels - 1
        for slot, row in self.rows():
            for target in range(self.levels):
                if target:
                    pl.when(level == 0)(self.up(row, slot, self.levels - target).start)
                    pl.when(level == last)(self.down(row, slot, target - 1).start)

    def chain_pass(self, distance):
        place, last = self.place, self.levels - 1
        for slot, row in self.rows():
            for target in range(last, distance, -1):

                @pl.when(place.level == distance)
                def _():
                    index = self.below_index(target, place.level)
                    self.arrived(slot, index)
                    self.add(place.block(target, row, place.core), self.from_chain[slot, index])
                    self.up(row, slot, target).start()

            for target in range(last - distance):

                @pl.when(place.level == last - distance)
                def _():
                    index = self.above_index(target)
                    self.arrived(slot, index)
                    self.add(place.block(target, row, place.core), self.from_chain[slot, index])
                    self.down(row, slot, target).start()

    def chain_end(self, out):
        place, last = self.place, self.levels - 1
        for slot, row in reversed(self.rows()):
            block = place.block(place.level, row, place.core)

            @pl.when(place.level > 0)
            def _():
                index = self.below_index(place.level, place.level)
                self.arrived(slot, index)
                self.add(block, self.from_chain[slot, index])

            @pl.when(place.level < last)
            def _():
                index = self.above_index(place.level)
                self.arrived(slot, index)
                self.add(block, self.from_chain[slot, index])

            if slot == 1:
                self.across(place.level, 0).start()
        if self.order == ACROSS_FIRST:
            out(self.part(place.mine)[...].astype(F32))

    def finish(self, out):
        if self.order == LEVELS_FIRST:
            self.across(self.place.level, 0).wait_recv()
            out(self.part(self.place.mine)[...].astype(F32) + self.from_across[0].astype(F32))

    def drain(self):
        def sent(span, out_sem):
            pltpu.make_async_remote_copy(
                src_ref=span,
                dst_ref=span,
                send_sem=out_sem,
                recv_sem=self.side_in.at[0],
                device_id=(self.place.section, self.place.targets[SIDE]),
                device_id_type=MESH,
            ).wait_send()

        sent(self.from_side, self.side_out)
        sent(self.from_across, self.across_out)
        for slot, _ in self.rows():
            sent(self.from_chain.at[slot, pl.ds(0, self.levels - 1)], self.chain_out.at[slot])


def chunk_scratch(levels, order, rows, cols, dtype, shared):
    block = (rows, cols)
    slots = 2 if order == LEVELS_FIRST else 1
    crossing = 1 if order == LEVELS_FIRST else levels
    dma = pltpu.SemaphoreType.DMA
    from_side = [] if shared else [pltpu.VMEM((levels * 2,) + block, dtype)]
    return from_side + [
        pltpu.VMEM((crossing,) + block, dtype),
        pltpu.VMEM((slots, levels + 1) + block, dtype),
        dma(()),
        dma((levels * 2,)),
        dma(()),
        dma((crossing,)),
        dma((slots,)),
        dma((slots, levels + 1)),
    ]


CHUNK_REFS = 8


def pad_lanes(rows, lanes=128):
    missing = lanes - rows.shape[1]
    if not missing:
        return rows
    return jnp.concatenate([rows, jnp.zeros((rows.shape[0], missing), rows.dtype)], axis=1)


def tile_of(rows):
    missing = 8 - rows.shape[0]
    if not missing:
        return rows
    return jnp.concatenate([rows, jnp.zeros((missing, rows.shape[1]), rows.dtype)], axis=0)


def fold(line):
    pieces = [pad_lanes(line[:, at : at + 128]) for at in range(0, line.shape[1], 128)]
    return tile_of(jnp.concatenate(pieces, axis=0))


def unfold(rows, count):
    pieces = []
    for index in range(-(-count // 128)):
        pieces.append(rows[index : index + 1, : min(128, count - index * 128)])
    return jnp.concatenate(pieces, axis=1)


def relay_kernel(levels, clips, plan, *refs):
    own, attend_shard, merge_shard, up_shard, down_shard, gain_shard, shift_shard, bias_shard = refs[:8]
    out, gain_out, shift_out, attend_out, merge_out, up_out, bias_out, down_out = refs[8:16]
    (
        packed,
        vector_blocks,
        attend_blocks,
        merge_blocks,
        up_blocks,
        down_blocks,
        vectors,
        bias,
        vector_sum,
        bias_sum,
        entry,
        projected,
        probability,
        normed,
        attended,
        middle,
        normed_two,
        activated,
        slope,
        leaving,
        low_temp,
        temp,
        sum_temp,
        gather_send,
        gather_recv,
        gather_local,
        load_sem,
        send_sem,
        recv_sem,
        out_sem,
        free_sem,
        store_sem,
    ) = refs[16:48]
    chunk_refs = list(refs[48:])
    place = Place(levels)
    section, mine = place.section, place.mine
    batches, rows, width = own.shape
    wide = up_shard.shape[1]
    ways = levels * 4
    share, wide_share = width // ways, wide // ways
    length = rows // clips
    pairs = HEADS // 2
    total = batches * rows

    load_own = pltpu.make_async_copy(own, entry.at[0], load_sem)
    load_own.start()
    packed[0:8] = pad_lanes(
        jnp.concatenate([gain_shard[...], shift_shard[...]], axis=0).astype(F32)
    )
    packed[8:16] = fold(bias_shard[...].astype(F32))
    place.greet()

    half_share = wide_share // 2
    pieces = [
        Piece(packed, vector_blocks, "level"),
        Piece(attend_shard, attend_blocks, "level"),
        Piece(up_shard, up_blocks, "level"),
        Piece(merge_shard, merge_blocks, "level"),
        Piece(down_shard.at[pl.ds(0, half_share)], down_blocks, "level", 0, half_share),
        Piece(down_shard.at[pl.ds(half_share, half_share)], down_blocks, "across", half_share, half_share),
    ]
    gather = Gather(place, pieces, gather_send, gather_recv, gather_local)
    count = len(pieces)
    for piece in range(count):
        gather.start(piece)
    gather.first_across(count - 1)
    for distance in range(1, levels):
        for piece in range(count):
            gather.from_levels(piece, distance)
            gather.from_across(piece, distance - 1)
    for piece in range(count):
        gather.from_across(piece, levels - 1)
    for piece in range(count):
        gather.from_side(piece)
    for piece in range(count):
        gather.drain(piece)
    vectors[...] = jnp.concatenate([vector_blocks[block, 0:8, 0:share] for block in range(ways)], axis=1)
    bias[...] = jnp.concatenate(
        [unfold(vector_blocks[block, 8:16], wide_share) for block in range(ways)], axis=1
    )

    def flat(blocks):
        return blocks.reshape(-1, blocks.shape[-1])

    def relay(batch, slot=0):
        return pltpu.make_async_remote_copy(
            src_ref=leaving.at[slot],
            dst_ref=entry.at[1, batch],
            send_sem=send_sem.at[batch],
            recv_sem=recv_sem.at[batch],
            device_id=(1 - section, mine),
            device_id_type=MESH,
        )

    def keep(batch, slot=0):
        return pltpu.make_async_copy(leaving.at[slot], out.at[batch], out_sem.at[batch])

    vector_sum[...] = jnp.zeros_like(vector_sum)
    bias_sum[...] = jnp.zeros_like(bias_sum)
    fed, back = section, 1 - section

    def row(index):
        return vectors[index : index + 1, :]

    def chances(batch, index):
        at = pl.multiple_of(batch * 4 * length + (index % 2) * 2 * length, 128)
        return probability.at[pl.ds((index // 2) * length, length), pl.ds(at, 2 * length)]

    def forward(batch, slot):
        normal, _ = standard(entry[fed, batch].astype(F32))
        normed[batch] = (normal * row(0) + row(2)).astype(BF)
        for part, shift in ((0, 4), (1, None), (2, 5)):
            at = slice(part * width, (part + 1) * width)
            value = matmul(normed[batch], flat(attend_blocks[:, :, at]))
            if shift is not None:
                value = value + row(shift)
            projected[batch, :, at] = value.astype(BF)
        for clip in range(clips):
            span = slice(clip * length, (clip + 1) * length)
            for pair in range(pairs):
                lanes = [slice(p * width + pair * 128, p * width + pair * 128 + 128) for p in range(3)]
                query = projected[batch, span, lanes[0]] * jnp.asarray(HEAD_DIM**-0.5, BF)
                key = pair_parts(projected[batch, span, lanes[1]])
                scores = matmul(query, key, NT)
                parts = []
                for half in halves(scores):
                    exponent = jnp.exp(half - jnp.max(half, axis=-1, keepdims=True))
                    parts.append(exponent * (1.0 / jnp.sum(exponent, axis=-1, keepdims=True)))
                weight = jnp.concatenate(parts, axis=1).astype(BF)
                chances(batch, clip * pairs + pair)[...] = weight
                value = pair_parts(projected[batch, span, lanes[2]])
                attended[batch, span, lanes[0]] = matmul(weight, value).astype(BF)
        joined = matmul(attended[batch], flat(merge_blocks[...])) + row(6)
        temp[...] = entry[fed, batch].astype(F32) + joined
        middle[batch] = temp[...].astype(BF)
        normal, _ = standard(temp[...])
        normed_two[batch] = (normal * row(1) + row(3)).astype(BF)
        tile = 256
        for start in range(0, wide, tile):
            at = slice(start, start + tile)
            value, rate = gelu_and_slope(
                matmul(normed_two[batch], flat(up_blocks[:, :, at])) + bias[:, at]
            )
            activated[batch, :, at] = value.astype(BF)
            slope[batch, :, at] = rate.astype(BF)
        result = temp[...] + matmul(activated[batch], flat(down_blocks[...])) + row(7)
        leaving[slot] = result.astype(BF)

    def backward(batch, slot, between):
        low = entry[back, batch]
        vector_sum[7:8] += column_sum(low.astype(F32))
        blocks = 4
        for block in range(0, ways, blocks):
            at = slice(block * wide_share, (block + blocks) * wide_share)
            rate = matmul(low, flat(down_blocks[block : block + blocks]), NT)
            rate = rate * slope[batch, :, at].astype(F32)
            bias_sum[:, at] += column_sum(rate)
            slope[batch, :, at] = rate.astype(BF)
        between()
        temp[...] = matmul(slope[batch], flat(up_blocks[...]), NT)
        normal, scale = standard(middle[batch].astype(F32))
        grad = temp[...]
        vector_sum[1:2] += column_sum(grad * normal)
        vector_sum[3:4] += column_sum(grad)
        grad = entry[back, batch].astype(F32) + norm_back(grad * row(1), normal, scale)
        sum_temp[...] = grad
        vector_sum[6:7] += column_sum(grad)
        middle[batch] = grad.astype(BF)
        low_temp[...] = matmul(middle[batch], flat(merge_blocks[...]), NT).astype(BF)
        for clip in range(clips):
            span = slice(clip * length, (clip + 1) * length)
            for pair in range(pairs):
                lanes = [slice(p * width + pair * 128, p * width + pair * 128 + 128) for p in range(3)]
                query = projected[batch, span, lanes[0]]
                key = pair_parts(projected[batch, span, lanes[1]])
                value = pair_parts(projected[batch, span, lanes[2]])
                upper = low_temp[span, lanes[0]]
                weight = chances(batch, clip * pairs + pair)[...]
                rise = matmul(upper, value, NT)
                value_grad = pair_join(matmul(weight, upper, TN))
                parts = []
                for part, heavy in zip(halves(rise), halves(weight)):
                    heavy = heavy.astype(F32)
                    mean = jnp.sum(part * heavy, axis=-1, keepdims=True)
                    parts.append(heavy * (part - mean) * HEAD_DIM**-0.5)
                change = jnp.concatenate(parts, axis=1).astype(BF)
                query_grad = matmul(change, key)
                key_grad = pair_join(matmul(change, query, TN))
                vector_sum[4:5, lanes[0]] += column_sum(query_grad)
                vector_sum[5:6, lanes[0]] += column_sum(value_grad)
                for at, piece in zip(lanes, (query_grad, key_grad, value_grad)):
                    projected[batch, span, at] = piece.astype(BF)
        temp[...] = matmul(projected[batch], flat(attend_blocks[...]), NT)
        normal, scale = standard(entry[fed, batch].astype(F32))
        grad = temp[...]
        vector_sum[0:1] += column_sum(grad * normal)
        vector_sum[2:3] += column_sum(grad)
        leaving[slot] = (sum_temp[...] + norm_back(grad * row(0), normal, scale)).astype(BF)

    load_own.wait()

    chunks = []
    part_refs = [vector_blocks, attend_blocks, merge_blocks, up_blocks, down_blocks]
    for which, start, order, _, cols, _, shared in plan:
        if shared is None:
            from_side = chunk_refs.pop(0)
        else:
            from_side = chunks[shared].from_side.at[:, :, pl.ds(0, cols)]
        held, chunk_refs = chunk_refs[:CHUNK_REFS], chunk_refs[CHUNK_REFS:]
        chunks.append(Chunk(place, order, part_refs[which], start, [from_side] + held[:2], held[2:]))
    down_a, down_b, up_a, up_b, attend_a, attend_b, merge, vector = chunks

    def down_gradient():
        def pair_at(index):
            late = lax.div(index, levels)
            return lax.rem(index, levels), jnp.where(late == 0, 1 - place.row, place.row), late == 0

        def multiply(index):
            level, row, _ = pair_at(index)
            pair = level * 2 + row
            at = pl.ds(pl.multiple_of(pair * 2 * wide_share, 128), 2 * wide_share)
            tile = flat(activated[:, :, at])
            for chunk in (down_a, down_b):
                at = pl.ds(chunk.start, chunk.cols)
                product = matmul(tile, flat(entry[back, :, :, at]), TN).astype(BF)
                for core in range(2):
                    down_blocks[pair * 2 + core, :, at] = product[core * wide_share : (core + 1) * wide_share]
                chunk.side(pair).start()

        def join(index):
            level, row, early = pair_at(index)
            down_a.join_pair(level, row)
            down_b.join_pair(level, row)
            pl.when(early)(down_b.across(level, level).start)

        multiply(jnp.int32(0))

        @pl.loop(1, 2 * levels)
        def _(index):
            multiply(index)
            join(index - 1)

        join(jnp.int32(2 * levels - 1))
        down_a.chain_start()

    @pl.loop(0, 2 * batches)
    def _(step):
        is_forward = jnp.where(section == 0, step < batches, lax.rem(step, 2) == 0)
        batch = jnp.where(section == 0, lax.rem(step, batches), lax.div(step, 2))

        slot = jnp.where(section == 0, lax.rem(batch, 2), jnp.where(is_forward, 0, 1))

        @pl.when(is_forward)
        def _():
            pl.when(section == 1)(relay(batch).wait_recv)
            pl.when(jnp.logical_and(section == 0, batch >= 2))(relay(batch - 2).wait_send)
            pl.when(jnp.logical_and(section == 1, batch >= 1))(keep(batch - 1).wait)
            forward(batch, slot)
            pl.when(section == 0)(relay(batch, slot).start)
            pl.when(section == 1)(keep(batch, slot).start)

        @pl.when(jnp.logical_not(is_forward))
        def _():
            pl.when(section == 0)(relay(batch).wait_recv)
            pl.when(jnp.logical_and(section == 0, batch < 2))(relay(batch + batches - 2).wait_send)
            pl.when(jnp.logical_and(section == 0, batch >= 2))(keep(batch - 2).wait)
            pl.when(jnp.logical_and(section == 1, batch >= 1))(relay(batch - 1).wait_send)
            last = jnp.logical_and(section == 0, step == 2 * batches - 1)
            backward(batch, slot, lambda: pl.when(last)(down_gradient))
            pl.when(section == 1)(relay(batch, slot).start)
            pl.when(section == 0)(keep(batch, slot).start)

    pl.when(section == 1)(down_gradient)
    stores = []

    def store(target, chunk, through=None, first=0):
        def put(value):
            if through is None:
                target[:, pl.ds(chunk.start, chunk.cols)] = value
                return
            done = 0
            while done < chunk.cols:
                column = chunk.start + done
                size = min(width - column % width, chunk.cols - done)
                at = (pl.ds(first + column // width * share, share), pl.ds(column % width, size))
                through[at] = value[:, done : done + size]
                copy = pltpu.make_async_copy(
                    through.at[at], target.at[:, pl.ds(column, size)], store_sem.at[len(stores)]
                )
                copy.start()
                stores.append(copy)
                done += size

        return put

    def turn(source, place_at):
        target = probability.at[pl.ds(0, width), pl.ds(place_at * total, total)]
        target[...] = flat(source[...]).T
        return target

    def columns(left, source, chunk, credit=None):
        step = 128 * max(d for d in (1, 2, 3) if chunk.cols % (128 * d) == 0)

        @pl.loop(0, chunk.cols // step)
        def _(index):
            at = pl.multiple_of(chunk.start + index * step, 128)
            product = matmul(left[...], flat(source[:, :, pl.ds(at, step)]))
            chunk.whole[:, :, pl.ds(at, step)] = product.astype(BF).reshape(ways, width // ways, step)

        if credit is not None:
            pl.semaphore_wait(free_sem.at[credit], 1)
        chunk.send_side()

    def release(index):
        pl.semaphore_signal(
            free_sem.at[index], inc=1, device_id=(section, place.targets[SIDE]), device_id_type=MESH
        )

    for block in range(ways):
        vector_blocks[block, 0:8] = pad_lanes(vector_sum[:, block * share : (block + 1) * share])
        vector_blocks[block, 8:16] = fold(bias_sum[:, block * wide_share : (block + 1) * wide_share])
    vector.send_side()
    turned = turn(normed_two, 0)
    columns(turned, slope, up_a)
    columns(turned, slope, up_b)
    vector.join_side()
    up_a.join_side()
    release(0)
    down_a.chain_pass(1)
    up_b.join_side()
    release(1)
    turned = turn(normed, 1)
    columns(turned, projected, attend_a, 0)
    down_a.chain_pass(2)
    down_b.join_across()
    down_b.chain_start()
    vector.join_across()
    vector.chain_start()
    columns(turned, projected, attend_b, 1)
    attend_a.join_side()
    release(2)
    turned = turn(attended, 0)
    columns(turned, middle, merge, 2)
    attend_b.join_side()
    down_b.chain_pass(1)
    merge.join_side()
    down_a.chain_end(None)
    up_a.join_across()
    up_a.chain_start()
    down_b.chain_pass(2)
    vector.chain_pass(1)
    up_a.chain_pass(1)
    up_b.join_across()
    up_b.chain_start()
    vector.chain_pass(2)
    down_b.chain_end(store(down_out, down_b))
    up_a.chain_pass(2)
    up_b.chain_pass(1)
    attend_a.join_across()
    attend_a.chain_start()

    def store_vectors(value):
        gain_out[...] = value[0:2, :share]
        for index in range(6):
            shift_out[index] = value[2 + index : 3 + index, :share]
        bias_out[...] = unfold(value[8:16], wide_share)

    vector.chain_end(store_vectors)
    up_a.chain_end(store(up_out, up_a, temp, 0))
    up_b.chain_pass(2)
    attend_a.chain_pass(1)
    attend_b.join_across()
    attend_b.chain_start()
    up_b.chain_end(store(up_out, up_b, temp, 0))
    attend_a.chain_pass(2)
    attend_b.chain_pass(1)
    merge.join_across()
    merge.chain_start()
    attend_a.chain_end(store(attend_out, attend_a, sum_temp, 0))
    attend_b.chain_pass(2)
    merge.chain_pass(1)
    attend_b.chain_end(store(attend_out, attend_b, sum_temp, 0))
    merge.chain_pass(2)
    down_a.finish(store(down_out, down_a))
    merge.chain_end(store(merge_out, merge, sum_temp, 3 * share))
    for chunk in chunks:
        chunk.drain()

    for copy in stores:
        copy.wait()

    @pl.when(section == 0)
    def _():
        keep(batches - 2).wait()
        keep(batches - 1).wait()

    @pl.when(section == 1)
    def _():
        keep(batches - 1).wait()
        relay(batches - 1).wait_send()


def settle_kernel(*refs):
    count = (len(refs) - 2) // 3
    load_sem, store_sem = refs[-2:]
    sources, targets, held = refs[:count], refs[count : 2 * count], refs[2 * count : 3 * count]
    loads = [pltpu.make_async_copy(sources[i], held[i], load_sem.at[i]) for i in range(count)]
    stores = [pltpu.make_async_copy(held[i], targets[i], store_sem.at[i]) for i in range(count)]
    for copy in loads:
        copy.start()
    for load, store in zip(loads, stores):
        load.wait()
        store.start()
    for copy in stores:
        copy.wait()


def train_step(own, attend, merge, up, down, gains, shifts, bias, clips, ways, collective_id):
    levels = ways // 4
    batches, rows, width = own.shape
    wide = up.shape[1]
    share, wide_share = width // ways, wide // ways
    length = rows // clips
    plan = [
        (4, 0, LEVELS_FIRST, wide_share, width // 2, BF, None),
        (4, width // 2, ACROSS_FIRST, wide_share, width // 2, BF, None),
        (3, 0, ACROSS_FIRST, share, wide // 2, BF, None),
        (3, wide // 2, ACROSS_FIRST, share, wide // 2, BF, None),
        (1, 0, ACROSS_FIRST, share, 3 * width // 2, BF, 2),
        (1, 3 * width // 2, ACROSS_FIRST, share, 3 * width // 2, BF, 3),
        (2, 0, ACROSS_FIRST, share, width, BF, 2),
        (0, 0, ACROSS_FIRST, 16, 128, F32, None),
    ]
    dma = pltpu.SemaphoreType.DMA
    vmem, anywhere = pl.BlockSpec(memory_space=pltpu.VMEM), pl.BlockSpec(memory_space=pl.ANY)

    def held(cols, dtype=BF):
        return pltpu.VMEM((batches, rows, cols), dtype)

    scratch = [
        pltpu.VMEM((16, 128), F32),
        pltpu.VMEM((ways, 16, 128), F32),
        pltpu.VMEM((ways, share, 3 * width), BF),
        pltpu.VMEM((ways, share, width), BF),
        pltpu.VMEM((ways, share, wide), BF),
        pltpu.VMEM((ways, wide_share, width), BF),
        pltpu.VMEM((8, width), F32),
        pltpu.VMEM((1, wide), F32),
        pltpu.VMEM((8, width), F32),
        pltpu.VMEM((1, wide), F32),
        pltpu.VMEM((2, batches, rows, width), BF),
        held(3 * width),
        pltpu.VMEM((clips * HEADS // 4 * length, batches * 4 * length), BF),
        held(width),
        held(width),
        held(width),
        held(width),
        held(wide),
        held(wide),
        pltpu.VMEM((2, rows, width), BF),
        pltpu.VMEM((rows, width), BF),
        pltpu.VMEM((rows, width), F32),
        pltpu.VMEM((rows, width), F32),
        dma((6, 3)),
        dma((6, 2 * levels + 1)),
        dma((6,)),
        dma(()),
        dma((batches,)),
        dma((batches,)),
        dma((batches,)),
        pltpu.SemaphoreType.REGULAR((3,)),
        dma((9,)),
    ]
    for _, _, order, chunk_rows, cols, dtype, shared in plan:
        scratch += chunk_scratch(levels, order, chunk_rows, cols, dtype, shared is not None)

    def grad(*shape):
        return jax.ShapeDtypeStruct(shape, F32)

    results = pl.pallas_call(
        functools.partial(relay_kernel, levels, clips, plan),
        out_shape=[
            jax.ShapeDtypeStruct(own.shape, BF),
            grad(2, share),
            grad(6, 1, share),
            grad(share, 3 * width),
            grad(share, width),
            grad(share, wide),
            grad(1, wide_share),
            grad(wide_share, width),
        ],
        in_specs=[anywhere] * 5 + [vmem] * 3,
        out_specs=[anywhere, vmem, vmem, anywhere, anywhere, anywhere, vmem, vmem],
        scratch_shapes=scratch,
        compiler_params=pltpu.CompilerParams(
            collective_id=collective_id, has_side_effects=True, vmem_limit_bytes=62 * 2**20
        ),
    )(own, attend, merge, up, down, gains, shifts, bias)
    return pl.pallas_call(
        settle_kernel,
        out_shape=[jax.ShapeDtypeStruct(result.shape, result.dtype) for result in results],
        in_specs=[anywhere] * len(results),
        out_specs=[anywhere] * len(results),
        scratch_shapes=[pltpu.VMEM(result.shape, result.dtype) for result in results]
        + [dma((len(results),))] * 2,
    )(*results)


def from_behind(block, axis, distance):
    devices = range(lax.axis_size(axis))
    route = [(i - distance, i) for i in devices if i - distance in devices]
    return lax.ppermute(block, axis, route)


def normalize(features, gain_row, offset):
    centred = features - jnp.mean(features, axis=-1, keepdims=True)
    spread = jnp.mean(centred * centred, axis=-1, keepdims=True)
    return centred * lax.rsqrt(spread + epsilon) * gain_row + offset


def gelu_exact(features):
    return jax.nn.gelu(features, approximate=False)


def split_heads(matrix, clip_count):
    return matrix.reshape(clip_count, matrix.shape[0] // clip_count, HEADS, HEAD_DIM)


def layer_forward(hidden, weights, clip_count):
    attend_weight, merge_weight, up_weight, down_weight, gain_rows, offset_rows, up_bias = weights
    gain_rows = gain_rows.astype(jnp.float32)
    offset_rows = offset_rows.astype(jnp.float32)
    row_count, model_width = hidden.shape
    score_scale = HEAD_DIM ** (-0.5)
    normed = normalize(hidden, gain_rows[0], offset_rows[0]).astype(jnp.bfloat16)
    projected = jnp.dot(normed, attend_weight, preferred_element_type=jnp.float32)
    query_heads = split_heads(
        (projected[:, :model_width] + offset_rows[2]).astype(jnp.bfloat16), clip_count
    )
    key_heads = split_heads(
        projected[:, model_width : 2 * model_width].astype(jnp.bfloat16), clip_count
    )
    value_heads = split_heads(
        (projected[:, 2 * model_width :] + offset_rows[3]).astype(jnp.bfloat16), clip_count
    )
    scores = (
        jnp.einsum("clhe,cmhe->chlm", query_heads, key_heads, preferred_element_type=jnp.float32)
        * score_scale
    )
    row_peak = jnp.max(scores, axis=-1, keepdims=True)
    exponent = jnp.exp(scores - row_peak)
    row_total = jnp.sum(exponent, axis=-1, keepdims=True)
    probability = (exponent / row_total).astype(jnp.bfloat16)
    log_total = (row_peak + jnp.log(row_total))[..., 0]
    attended = jnp.einsum(
        "chlm,cmhe->clhe", probability, value_heads, preferred_element_type=jnp.float32
    )
    attended = attended.reshape(row_count, model_width).astype(jnp.bfloat16)
    middle = (
        hidden
        + jnp.dot(attended, merge_weight, preferred_element_type=jnp.float32)
        + offset_rows[4]
    )
    normed_two = normalize(middle, gain_rows[1], offset_rows[1]).astype(jnp.bfloat16)
    raised = jnp.dot(normed_two, up_weight, preferred_element_type=jnp.float32) + up_bias.astype(
        jnp.float32
    )
    activated = gelu_exact(raised).astype(jnp.bfloat16)
    result = (
        middle
        + jnp.dot(activated, down_weight, preferred_element_type=jnp.float32)
        + offset_rows[5]
    )
    saved_state = (
        hidden,
        normed,
        query_heads,
        key_heads,
        value_heads,
        log_total,
        attended,
        middle,
        normed_two,
        raised,
        activated,
    )
    return (result, saved_state)


def layer_backward(out_grad, saved_state, weights, clip_count):
    attend_weight, merge_weight, up_weight, down_weight, gain_rows, offset_rows, up_bias = weights
    gain_rows = gain_rows.astype(jnp.float32)
    offset_rows = offset_rows.astype(jnp.float32)
    (
        hidden,
        normed,
        query_heads,
        key_heads,
        value_heads,
        log_total,
        attended,
        middle,
        normed_two,
        raised,
        activated,
    ) = saved_state
    row_count, model_width = hidden.shape
    score_scale = HEAD_DIM ** (-0.5)
    low_grad = out_grad.astype(jnp.bfloat16)
    down_term = jnp.einsum("tf,td->fd", activated, low_grad, preferred_element_type=jnp.float32)
    last_bias = jnp.sum(out_grad, axis=0)
    act_grad = jnp.einsum("td,fd->tf", low_grad, down_weight, preferred_element_type=jnp.float32)
    raised_grad = jax.vjp(gelu_exact, raised)[1](act_grad)[0]
    up_bias_term = jnp.sum(raised_grad, axis=0)
    raised_low = raised_grad.astype(jnp.bfloat16)
    up_term = jnp.einsum("td,tf->df", normed_two, raised_low, preferred_element_type=jnp.float32)
    normed_two_grad = jnp.einsum(
        "tf,df->td", raised_low, up_weight, preferred_element_type=jnp.float32
    )
    second_back = jax.vjp(normalize, middle, gain_rows[1], offset_rows[1])[1]
    middle_part, gain_two, offset_two = second_back(normed_two_grad)
    middle_grad = out_grad + middle_part
    merge_bias = jnp.sum(middle_grad, axis=0)
    middle_low = middle_grad.astype(jnp.bfloat16)
    merge_term = jnp.einsum("td,te->de", attended, middle_low, preferred_element_type=jnp.float32)
    attended_grad = jnp.einsum(
        "te,de->td", middle_low, merge_weight, preferred_element_type=jnp.float32
    )
    attended_grad = split_heads(attended_grad.astype(jnp.bfloat16), clip_count)
    scores = (
        jnp.einsum("clhe,cmhe->chlm", query_heads, key_heads, preferred_element_type=jnp.float32)
        * score_scale
    )
    probability = jnp.exp(scores - log_total[..., None])
    prob_grad = jnp.einsum(
        "clhe,cmhe->chlm", attended_grad, value_heads, preferred_element_type=jnp.float32
    )
    value_grad = jnp.einsum(
        "chlm,clhe->cmhe",
        probability.astype(jnp.bfloat16),
        attended_grad,
        preferred_element_type=jnp.float32,
    )
    score_grad = probability * (
        prob_grad - jnp.sum(prob_grad * probability, axis=-1, keepdims=True)
    )
    score_grad = score_grad.astype(jnp.bfloat16)
    query_grad = (
        jnp.einsum("chlm,cmhe->clhe", score_grad, key_heads, preferred_element_type=jnp.float32)
        * score_scale
    )
    key_grad = (
        jnp.einsum("chlm,clhe->cmhe", score_grad, query_heads, preferred_element_type=jnp.float32)
        * score_scale
    )
    query_grad = query_grad.reshape(row_count, model_width)
    key_grad = key_grad.reshape(row_count, model_width)
    value_grad = value_grad.reshape(row_count, model_width)
    query_bias = jnp.sum(query_grad, axis=0)
    value_bias = jnp.sum(value_grad, axis=0)
    joined_low = jnp.concatenate([query_grad, key_grad, value_grad], axis=1).astype(jnp.bfloat16)
    attend_term = jnp.einsum("td,te->de", normed, joined_low, preferred_element_type=jnp.float32)
    normed_grad = jnp.einsum(
        "te,de->td", joined_low, attend_weight, preferred_element_type=jnp.float32
    )
    first_back = jax.vjp(normalize, hidden, gain_rows[0], offset_rows[0])[1]
    hidden_part, gain_one, offset_one = first_back(normed_grad)
    hidden_grad = middle_grad + hidden_part
    gain_term = jnp.stack([gain_one, gain_two])
    offset_term = jnp.stack([offset_one, offset_two, query_bias, value_bias, merge_bias, last_bias])
    return (
        hidden_grad,
        (attend_term, merge_term, up_term, down_term, gain_term, offset_term, up_bias_term),
    )


def plain_body(
    section_inputs,
    norm_gains,
    offsets,
    attend_weight,
    merge_weight,
    up_weight,
    up_bias,
    down_weight,
):
    shards = (attend_weight, merge_weight, up_weight, down_weight, norm_gains, offsets, up_bias)
    gathered = (
        lax.all_gather(shards[0], "fsdp", axis=1, tiled=True),
        lax.all_gather(shards[1], "fsdp", axis=1, tiled=True),
        lax.all_gather(shards[2], "fsdp", axis=1, tiled=True),
        lax.all_gather(shards[3], "fsdp", axis=1, tiled=True),
        lax.all_gather(shards[4], "fsdp", axis=2, tiled=True),
        lax.all_gather(shards[5], "fsdp", axis=2, tiled=True),
        lax.all_gather(shards[6], "fsdp", axis=1, tiled=True),
    )
    weights = tuple((tensor[0] for tensor in gathered))
    is_first = lax.axis_index("section") == 0
    own_data = section_inputs[0]
    batches, clip_count, length, model_width = own_data.shape
    row_count = clip_count * length
    own_rows = own_data.reshape(batches, row_count, model_width)
    kept_state = []
    upper_rows = []
    received = jnp.zeros((row_count, model_width), jnp.bfloat16)
    for instant in range(batches + 1):
        entering = jnp.where(is_first, own_rows[min(instant, batches - 1)], received)
        result, saved_state = layer_forward(entering.astype(jnp.float32), weights, clip_count)
        kept_state.append(saved_state)
        rounded = result.astype(jnp.bfloat16)
        if instant >= 1:
            upper_rows.append(rounded)
        if instant < batches:
            received = from_behind(rounded, "section", 1)
    gathered = (
        lax.all_gather(shards[0], "fsdp", axis=1, tiled=True),
        lax.all_gather(shards[1], "fsdp", axis=1, tiled=True),
        lax.all_gather(shards[2], "fsdp", axis=1, tiled=True),
        lax.all_gather(shards[3], "fsdp", axis=1, tiled=True),
        lax.all_gather(shards[4], "fsdp", axis=2, tiled=True),
        lax.all_gather(shards[5], "fsdp", axis=2, tiled=True),
        lax.all_gather(shards[6], "fsdp", axis=1, tiled=True),
    )
    weights = tuple((tensor[0] for tensor in gathered))
    totals = (
        jnp.zeros(weights[0].shape, jnp.float32),
        jnp.zeros(weights[1].shape, jnp.float32),
        jnp.zeros(weights[2].shape, jnp.float32),
        jnp.zeros(weights[3].shape, jnp.float32),
        jnp.zeros(weights[4].shape, jnp.float32),
        jnp.zeros(weights[5].shape, jnp.float32),
        jnp.zeros(weights[6].shape, jnp.float32),
    )
    received_grad = jnp.zeros((row_count, model_width), jnp.bfloat16)
    lower_rows = []
    for instant in range(batches + 1):
        position = batches - 1 - instant
        if position >= 0:
            own_grad = own_rows[position]
        else:
            own_grad = jnp.zeros((row_count, model_width), jnp.bfloat16)
        cotangent = jnp.where(is_first, received_grad, own_grad).astype(jnp.float32)
        hidden_grad, param_terms = layer_backward(
            cotangent, kept_state[batches - instant], weights, clip_count
        )
        totals = jax.tree.map(jnp.add, totals, param_terms)
        rounded = hidden_grad.astype(jnp.bfloat16)
        if instant >= 1:
            lower_rows.append(rounded)
        if instant < batches:
            received_grad = from_behind(rounded, "section", -1)
    ordered_lower = lower_rows[::-1]
    combined = jnp.stack(
        [
            jnp.where(is_first, lower_part, upper_part)
            for lower_part, upper_part in zip(ordered_lower, upper_rows)
        ]
    )
    section_outputs = combined.reshape(1, batches, clip_count, length, model_width)
    reduced = (
        lax.psum_scatter(totals[0][None], "fsdp", scatter_dimension=1, tiled=True),
        lax.psum_scatter(totals[1][None], "fsdp", scatter_dimension=1, tiled=True),
        lax.psum_scatter(totals[2][None], "fsdp", scatter_dimension=1, tiled=True),
        lax.psum_scatter(totals[3][None], "fsdp", scatter_dimension=1, tiled=True),
        lax.psum_scatter(totals[4][None], "fsdp", scatter_dimension=2, tiled=True),
        lax.psum_scatter(totals[5][None], "fsdp", scatter_dimension=2, tiled=True),
        lax.psum_scatter(totals[6][None], "fsdp", scatter_dimension=1, tiled=True),
    )
    return (
        section_outputs,
        reduced[4],
        reduced[5],
        reduced[0],
        reduced[1],
        reduced[2],
        reduced[6],
        reduced[3],
    )


def body(
    section_inputs,
    norm_gains,
    offsets,
    attend_weight,
    merge_weight,
    up_weight,
    up_bias,
    down_weight,
):
    ways = lax.axis_size("fsdp")
    if ways % 4 or attend_weight.shape[1] % 16:
        return plain_body(
            section_inputs,
            norm_gains,
            offsets,
            attend_weight,
            merge_weight,
            up_weight,
            up_bias,
            down_weight,
        )
    batches, clips, length, width = section_inputs.shape[1:]
    own = section_inputs.reshape(batches, clips * length, width)
    results = train_step(
        own,
        attend_weight[0],
        merge_weight[0],
        up_weight[0],
        down_weight[0],
        norm_gains[0],
        offsets[0],
        up_bias,
        clips,
        ways,
        1,
    )
    section_outputs, gains, shifts, attend, merge, up, bias, down = results
    return (
        section_outputs.reshape(section_inputs.shape),
        gains[None],
        shifts.swapaxes(0, 1),
        attend[None],
        merge[None],
        up[None],
        bias,
        down[None],
    )


def solution(mesh):
    return jax.shard_map(
        body,
        mesh=mesh,
        in_specs=(
            P("section", None, "fsdp", None, None),
            P("section", None, "fsdp"),
            P("section", None, "fsdp"),
            P("section", "fsdp", None),
            P("section", "fsdp", None),
            P("section", "fsdp", None),
            P("section", "fsdp"),
            P("section", "fsdp", None),
        ),
        out_specs=(
            P("section", None, "fsdp", None, None),
            P("section", None, "fsdp"),
            P("section", None, "fsdp"),
            P("section", "fsdp", None),
            P("section", "fsdp", None),
            P("section", "fsdp", None),
            P("section", "fsdp"),
            P("section", "fsdp", None),
        ),
        check_vma=False,
    )
```

```python
import functools
import math

import jax
import jax.numpy as jnp
from jax import lax
from jax.experimental import pallas as pl
from jax.experimental.pallas import tpu as pltpu
from jax.sharding import PartitionSpec as P

MESH = pl.DeviceIdType.MESH

HEADS = 12
HEAD_DIM = 64
epsilon = 1e-05
BF, F32 = jnp.bfloat16, jnp.float32
NT = (((1,), (1,)), ((), ()))
TN = (((0,), (0,)), ((), ()))

SIDE, ACROSS, UP, DOWN = range(4)
LEVELS_FIRST, ACROSS_FIRST = 0, 1

class Sends:
    def __init__(self):
        self.items = []

    def start(self, copy, when):
        if when is None:
            copy.start()
        else:
            pl.when(when)(copy.start)
        self.items.append((copy, when))

    def drain(self):
        for copy, when in self.items:
            if when is None:
                copy.wait_send()
            else:
                pl.when(when)(copy.wait_send)


def matmul(left, right, dims=(((1,), (0,)), ((), ()))):
    return lax.dot_general(left, right, dims, preferred_element_type=F32)


def standard(features):
    centred = features - jnp.mean(features, axis=-1, keepdims=True)
    scale = lax.rsqrt(jnp.mean(centred * centred, axis=-1, keepdims=True) + epsilon)
    return centred * scale, scale


def gelu_and_slope(raised):
    share = 0.5 + 0.5 * lax.erf(raised * math.sqrt(0.5))
    bell = jnp.exp(raised * raised * -0.5) * (1.0 / math.sqrt(2.0 * math.pi))
    return raised * share, share + raised * bell


def norm_back(upper, normal, scale):
    shift = jnp.mean(upper, axis=-1, keepdims=True)
    slope = jnp.mean(upper * normal, axis=-1, keepdims=True)
    return (upper - shift - normal * slope) * scale


def column_sum(values):
    return jnp.sum(values, axis=0, keepdims=True)


def pair_parts(matrix):
    lane = lax.broadcasted_iota(jnp.int32, matrix.shape, 1)
    zero = jnp.zeros_like(matrix)
    first = lane < HEAD_DIM
    return jnp.concatenate([jnp.where(first, matrix, zero), jnp.where(first, zero, matrix)], axis=0)


def pair_join(stacked):
    rows = stacked.shape[0] // 2
    lane = lax.broadcasted_iota(jnp.int32, (rows, stacked.shape[1]), 1)
    return jnp.where(lane < HEAD_DIM, stacked[:rows], stacked[rows:])


def halves(scores):
    keys = scores.shape[1] // 2
    return scores[:, :keys], scores[:, keys:]


class Place:
    def __init__(self, levels):
        self.levels = levels
        self.section, self.mine = lax.axis_index("section"), lax.axis_index("fsdp")
        self.level = lax.div(self.mine, 4)
        self.row = lax.rem(lax.div(self.mine, 2), 2)
        self.core = lax.rem(self.mine, 2)
        self.has_up, self.has_down = self.level < levels - 1, self.level > 0
        self.targets = {SIDE: self.mine ^ 1, ACROSS: self.mine ^ 2, UP: self.mine + 4, DOWN: self.mine - 4}

    def block(self, level, row, core):
        return level * 4 + row * 2 + core

    def greet(self):
        barrier = pltpu.get_barrier_semaphore()

        def hello(section, target):
            pl.semaphore_signal(barrier, inc=1, device_id=(section, target), device_id_type=MESH)

        hello(1 - self.section, self.mine)
        hello(self.section, self.targets[SIDE])
        hello(self.section, self.targets[ACROSS])
        pl.when(self.has_down)(lambda: hello(self.section, self.targets[DOWN]))
        pl.when(self.has_up)(lambda: hello(self.section, self.targets[UP]))
        ends = (self.level == 0).astype(jnp.int32) + (self.level == self.levels - 1).astype(jnp.int32)
        pl.semaphore_wait(barrier, 5 - ends)


class Piece:
    def __init__(self, shard, ref, kind, start=0, size=None):
        self.shard, self.ref, self.plain = shard, ref, kind == "level"
        self.rows = None if size is None else pl.ds(start, size)

    def block(self, index):
        return self.ref.at[index] if self.rows is None else self.ref.at[index, self.rows]

    def span(self, count):
        return self.block(pl.ds(0, count))


class Gather:
    def __init__(self, place, pieces, send_sem, recv_sem, local_sem):
        self.place, self.pieces = place, pieces
        self.send_sem, self.recv_sem, self.local_sem = send_sem, recv_sem, local_sem
        self.side = 2 * place.levels

    def copy(self, source, target, out_sem, in_sem, way):
        return pltpu.make_async_remote_copy(
            src_ref=source,
            dst_ref=target,
            send_sem=out_sem,
            recv_sem=in_sem,
            device_id=(self.place.section, self.place.targets[way]),
            device_id_type=MESH,
        )

    def send(self, piece, level, row, way, own=False, when=None):
        held = self.pieces[piece]
        target = held.block(self.place.block(level, row, self.place.core))
        kind = {SIDE: 0, ACROSS: 1, UP: 2, DOWN: 2}[way]
        copy = self.copy(
            held.shard if own else target,
            target,
            self.send_sem.at[piece, kind],
            self.recv_sem.at[piece, self.side if way == SIDE else level * 2 + row],
            way,
        )
        if when is None:
            copy.start()
        else:
            pl.when(when)(copy.start)

    def arrived(self, piece, level, row, when=None):
        target = self.pieces[piece].block(self.place.block(level, row, self.place.core))
        index = level * 2 + row
        copy = self.copy(target, target, self.send_sem.at[piece, 0], self.recv_sem.at[piece, index], SIDE)
        if when is None:
            copy.wait_recv()
        else:
            pl.when(when)(copy.wait_recv)

    def local(self, piece):
        held = self.pieces[piece]
        return pltpu.make_async_copy(held.shard, held.block(self.place.mine), self.local_sem.at[piece])

    def start(self, piece):
        place = self.place
        self.send(piece, place.level, place.row, ACROSS, own=True)
        self.send(piece, place.level, place.row, UP, own=True, when=place.has_up)
        self.send(piece, place.level, place.row, DOWN, own=True, when=place.has_down)
        self.send(piece, place.level, place.row, SIDE, own=True)
        self.local(piece).start()

    def first_across(self, piece):
        place = self.place
        level, row = place.level, 1 - place.row
        self.arrived(piece, level, row)
        self.send(piece, level, row, UP, when=place.has_up)
        self.send(piece, level, row, DOWN, when=place.has_down)
        self.send(piece, level, row, SIDE)

    def from_levels(self, piece, distance):
        place = self.place
        plain = self.pieces[piece].plain
        for row in (place.row,) if plain else (place.row, 1 - place.row):
            for sign in (-1, 1):
                other = place.level + sign * distance
                here = other >= 0 if sign < 0 else other < place.levels
                onward = place.has_up if sign < 0 else place.has_down
                self.arrived(piece, other, row, here)
                if distance < place.levels - 1:
                    way = UP if sign < 0 else DOWN
                    self.send(piece, other, row, way, when=jnp.logical_and(here, onward))
                if plain:
                    self.send(piece, other, row, ACROSS, when=here)
                self.send(piece, other, row, SIDE, when=here)

    def from_across(self, piece, distance):
        place = self.place
        if not self.pieces[piece].plain:
            return
        for sign in (-1, 1) if distance else (1,):
            other = place.level + sign * distance
            here = None
            if distance:
                here = other >= 0 if sign < 0 else other < place.levels
            self.arrived(piece, other, 1 - place.row, here)
            self.send(piece, other, 1 - place.row, SIDE, when=here)

    def from_side(self, piece):
        self.local(piece).wait()
        span = self.pieces[piece].span(self.side)
        self.copy(span, span, self.send_sem.at[piece, 0], self.recv_sem.at[piece, self.side], SIDE).wait_recv()

    def drain(self, piece):
        place, held = self.place, self.pieces[piece]

        def sent(count, kind):
            span = held.span(count)
            return self.copy(span, span, self.send_sem.at[piece, kind], self.recv_sem.at[piece, 0], SIDE)

        rows = 1 if held.plain else 2
        sent(self.side, 0).wait_send()
        sent(place.levels if held.plain else 1, 1).wait_send()
        inner = jnp.logical_and(place.has_up, place.has_down)
        pl.when(inner)(sent(rows * (place.levels + 1), 2).wait_send)
        pl.when(jnp.logical_not(inner))(sent(rows, 2).wait_send)


class Chunk:
    def __init__(self, place, order, part, start, refs, sems):
        self.place, self.order, self.levels = place, order, place.levels
        self.whole, self.start = part, start
        self.from_side, self.from_across, self.from_chain = refs
        self.cols = self.from_side.shape[2]
        (
            self.side_out,
            self.side_in,
            self.across_out,
            self.across_in,
            self.chain_out,
            self.chain_in,
        ) = sems

    def part(self, block):
        return self.whole.at[block, :, pl.ds(self.start, self.cols)]

    def copy(self, block, target, out_sem, in_sem, way):
        return pltpu.make_async_remote_copy(
            src_ref=self.part(block),
            dst_ref=target,
            send_sem=out_sem,
            recv_sem=in_sem,
            device_id=(self.place.section, self.place.targets[way]),
            device_id_type=MESH,
        )

    def side(self, pair):
        block = pair * 2 + 1 - self.place.core
        return self.copy(
            block, self.from_side.at[pair], self.side_out, self.side_in.at[pair], SIDE
        )

    def across(self, level, slot):
        block = self.place.block(level, 1 - self.place.row, self.place.core)
        return self.copy(
            block,
            self.from_across.at[slot],
            self.across_out,
            self.across_in.at[slot],
            ACROSS,
        )

    def below_index(self, target, level):
        return target - level

    def above_index(self, target):
        return self.levels - target

    def up(self, row, slot, target):
        index = self.below_index(target, self.place.level + 1)
        return self.copy(
            self.place.block(target, row, self.place.core),
            self.from_chain.at[slot, index],
            self.chain_out.at[slot],
            self.chain_in.at[slot, index],
            UP,
        )

    def down(self, row, slot, target):
        index = self.above_index(target)
        return self.copy(
            self.place.block(target, row, self.place.core),
            self.from_chain.at[slot, index],
            self.chain_out.at[slot],
            self.chain_in.at[slot, index],
            DOWN,
        )

    def arrived(self, slot, index):
        target = self.from_chain.at[slot, index]
        pltpu.make_async_remote_copy(
            src_ref=target,
            dst_ref=target,
            send_sem=self.side_out,
            recv_sem=self.chain_in.at[slot, index],
            device_id=(self.place.section, self.place.targets[SIDE]),
            device_id_type=MESH,
        ).wait_recv()

    def add(self, block, term):
        part = self.part(block)
        part[...] = part[...] + term

    def send_side(self):
        @pl.loop(0, self.levels * 2)
        def _(pair):
            self.side(pair).start()

    def join_pair(self, level, row):
        pair = level * 2 + row
        self.side(pair).wait_recv()
        self.add(pair * 2 + self.place.core, self.from_side[pair])

    def level_at(self, index):
        return jnp.where(self.place.level < self.levels // 2, self.levels - 1 - index, index)

    def join_side(self):
        place = self.place
        for other in (True, False):
            row = 1 - place.row if other else place.row

            @pl.loop(0, self.levels)
            def _(index):
                level = self.level_at(index)
                self.join_pair(level, row)
                if other and self.order == ACROSS_FIRST:
                    self.across(level, level).start()

    def chain_open(self, row, slot, target):
        level, last = self.place.level, self.levels - 1
        pl.when(jnp.logical_and(level == 0, target > 0))(lambda: self.up(row, slot, target).start())
        pl.when(jnp.logical_and(level == last, target < last))(
            lambda: self.down(row, slot, target).start()
        )

    def join_across(self):
        place = self.place

        @pl.loop(0, self.levels)
        def _(index):
            level = self.level_at(index)
            self.across(level, level).wait_recv()
            self.add(place.block(level, place.row, place.core), self.from_across[level])
            self.chain_open(place.row, 0, level)

    def rows(self):
        row = self.place.row
        return ((0, row), (1, 1 - row)) if self.order == LEVELS_FIRST else ((0, row),)

    def chain_pass(self, distance):
        place, last = self.place, self.levels - 1
        for slot, row in self.rows():
            for target in range(last, distance, -1):

                @pl.when(place.level == distance)
                def _():
                    index = self.below_index(target, place.level)
                    self.arrived(slot, index)
                    self.add(place.block(target, row, place.core), self.from_chain[slot, index])
                    self.up(row, slot, target).start()

            for target in range(last - distance):

                @pl.when(place.level == last - distance)
                def _():
                    index = self.above_index(target)
                    self.arrived(slot, index)
                    self.add(place.block(target, row, place.core), self.from_chain[slot, index])
                    self.down(row, slot, target).start()

    def chain_end(self, out):
        place, last = self.place, self.levels - 1
        for slot, row in reversed(self.rows()):
            block = place.block(place.level, row, place.core)

            @pl.when(place.level > 0)
            def _():
                index = self.below_index(place.level, place.level)
                self.arrived(slot, index)
                self.add(block, self.from_chain[slot, index])

            @pl.when(place.level < last)
            def _():
                index = self.above_index(place.level)
                self.arrived(slot, index)
                self.add(block, self.from_chain[slot, index])

            if slot == 1:
                self.across(place.level, 0).start()
        if self.order == ACROSS_FIRST:
            out(self.part(place.mine)[...].astype(F32))

    def finish(self, out):
        if self.order == LEVELS_FIRST:
            self.across(self.place.level, 0).wait_recv()
            out(self.part(self.place.mine)[...].astype(F32) + self.from_across[0].astype(F32))

    def drain(self):
        def sent(span, out_sem):
            pltpu.make_async_remote_copy(
                src_ref=span,
                dst_ref=span,
                send_sem=out_sem,
                recv_sem=self.side_in.at[0],
                device_id=(self.place.section, self.place.targets[SIDE]),
                device_id_type=MESH,
            ).wait_send()

        sent(self.from_side, self.side_out)
        sent(self.from_across, self.across_out)
        for slot, _ in self.rows():
            sent(self.from_chain.at[slot, pl.ds(0, self.levels - 1)], self.chain_out.at[slot])


def chunk_scratch(levels, order, rows, cols, dtype, shared):
    block = (rows, cols)
    slots = 2 if order == LEVELS_FIRST else 1
    crossing = 1 if order == LEVELS_FIRST else levels
    dma = pltpu.SemaphoreType.DMA
    from_side = [] if shared else [pltpu.VMEM((levels * 2,) + block, dtype)]
    return from_side + [
        pltpu.VMEM((crossing,) + block, dtype),
        pltpu.VMEM((slots, levels + 1) + block, dtype),
        dma(()),
        dma((levels * 2,)),
        dma(()),
        dma((crossing,)),
        dma((slots,)),
        dma((slots, levels + 1)),
    ]


CHUNK_REFS = 8
STEP = 512


def pad_lanes(rows, lanes=128):
    missing = lanes - rows.shape[1]
    if not missing:
        return rows
    return jnp.concatenate([rows, jnp.zeros((rows.shape[0], missing), rows.dtype)], axis=1)


def tile_of(rows):
    missing = 8 - rows.shape[0]
    if not missing:
        return rows
    return jnp.concatenate([rows, jnp.zeros((missing, rows.shape[1]), rows.dtype)], axis=0)


def fold(line):
    pieces = [pad_lanes(line[:, at : at + 128]) for at in range(0, line.shape[1], 128)]
    return tile_of(jnp.concatenate(pieces, axis=0))


def unfold(rows, count):
    pieces = []
    for index in range(-(-count // 128)):
        pieces.append(rows[index : index + 1, : min(128, count - index * 128)])
    return jnp.concatenate(pieces, axis=1)


def relay_kernel(levels, clips, plan, *refs):
    own, attend_shard, merge_shard, up_shard, down_shard, gain_shard, shift_shard, bias_shard = refs[:8]
    out, gain_out, shift_out, attend_out, merge_out, up_out, bias_out, down_out = refs[8:16]
    (
        packed,
        vector_blocks,
        attend_blocks,
        merge_blocks,
        up_blocks,
        down_blocks,
        vectors,
        bias,
        vector_sum,
        bias_sum,
        entry,
        projected,
        probability,
        normed,
        attended,
        middle,
        normed_two,
        activated,
        slope,
        leaving,
        low_temp,
        temp,
        sum_temp,
        gather_send,
        gather_recv,
        gather_local,
        load_sem,
        send_sem,
        recv_sem,
        out_sem,
        free_sem,
        store_sem,
    ) = refs[16:48]
    chunk_refs = list(refs[48:])
    place = Place(levels)
    section, mine = place.section, place.mine
    batches, rows, width = own.shape
    wide = up_shard.shape[1]
    ways = levels * 4
    share, wide_share = width // ways, wide // ways
    length = rows // clips
    pairs = HEADS // 2
    total = batches * rows

    load_own = pltpu.make_async_copy(own, entry.at[0], load_sem)
    load_own.start()
    packed[0:8] = pad_lanes(
        jnp.concatenate([gain_shard[...], shift_shard[...]], axis=0).astype(F32)
    )
    packed[8:16] = fold(bias_shard[...].astype(F32))
    place.greet()

    half_share = wide_share // 2
    pieces = [
        Piece(packed, vector_blocks, "level"),
        Piece(attend_shard, attend_blocks, "level"),
        Piece(merge_shard, merge_blocks, "level"),
        Piece(up_shard, up_blocks, "level"),
        Piece(down_shard.at[pl.ds(0, half_share)], down_blocks, "level", 0, half_share),
        Piece(down_shard.at[pl.ds(half_share, half_share)], down_blocks, "across", half_share, half_share),
    ]
    gather = Gather(place, pieces, gather_send, gather_recv, gather_local)
    def flat(blocks):
        return blocks.reshape(-1, blocks.shape[-1])

    half = rows // 2 if clips % 2 == 0 else rows
    portions = rows // half

    def relay_part(batch, portion, slot=0):
        here = pl.ds(portion * half, half)
        return pltpu.make_async_remote_copy(
            src_ref=leaving.at[slot, here],
            dst_ref=entry.at[1, batch, here],
            send_sem=send_sem.at[batch, portion],
            recv_sem=recv_sem.at[batch, portion],
            device_id=(1 - section, mine),
            device_id_type=MESH,
        )

    class Relay:
        def __init__(self, batch, slot=0):
            self.copies = [relay_part(batch, portion, slot) for portion in range(portions)]

        def start(self):
            for copy in self.copies:
                copy.start()

        def wait_send(self):
            for copy in self.copies:
                copy.wait_send()

        def wait_recv(self):
            for copy in self.copies:
                copy.wait_recv()

    relay = Relay

    def keep(batch, slot=0):
        return pltpu.make_async_copy(leaving.at[slot], out.at[batch], out_sem.at[batch])

    vector_sum[...] = jnp.zeros_like(vector_sum)
    bias_sum[...] = jnp.zeros_like(bias_sum)
    fed, back = section, 1 - section

    def row(index):
        return vectors[index : index + 1, :]

    def chances(batch, start, pair):
        at = pl.multiple_of(batch * 4 * length + (pair % 2) * 2 * length, 128)
        first = start * (pairs // 2) + (pair // 2) * length
        return probability.at[pl.ds(first, length), pl.ds(at, 2 * length)]

    def attend_part(batch, start, size):
        here = pl.ds(start, size)
        normal, _ = standard(entry[fed, batch, here].astype(F32))
        normed[batch, here] = (normal * row(0) + row(2)).astype(BF)
        for part, shift in ((0, 4), (1, None), (2, 5)):
            at = slice(part * width, (part + 1) * width)
            value = matmul(normed[batch, here], flat(attend_blocks[:, :, at]))
            if shift is not None:
                value = value + row(shift)
            projected[batch, here, at] = value.astype(BF)
        for clip in range(size // length):
            span = pl.ds(start + clip * length, length)
            for pair in range(pairs):
                lanes = [slice(p * width + pair * 128, p * width + pair * 128 + 128) for p in range(3)]
                query = projected[batch, span, lanes[0]] * jnp.asarray(HEAD_DIM**-0.5, BF)
                key = pair_parts(projected[batch, span, lanes[1]])
                scores = matmul(query, key, NT)
                parts = []
                for half in halves(scores):
                    exponent = jnp.exp(half - jnp.max(half, axis=-1, keepdims=True))
                    parts.append(exponent * (1.0 / jnp.sum(exponent, axis=-1, keepdims=True)))
                weight = jnp.concatenate(parts, axis=1).astype(BF)
                chances(batch, start + clip * length, pair)[...] = weight
                value = pair_parts(projected[batch, span, lanes[2]])
                attended[batch, span, lanes[0]] = matmul(weight, value).astype(BF)
        joined = matmul(attended[batch, here], flat(merge_blocks[...])) + row(6)
        temp[here] = entry[fed, batch, here].astype(F32) + joined
        middle[batch, here] = temp[here].astype(BF)
        normal, _ = standard(temp[here])
        normed_two[batch, here] = (normal * row(1) + row(3)).astype(BF)

    def rise_part(batch, start, size):
        here = pl.ds(start, size)
        tile = 256
        for first in range(0, wide, tile):
            at = slice(first, first + tile)
            value, rate = gelu_and_slope(
                matmul(normed_two[batch, here], flat(up_blocks[:, :, at])) + bias[:, at]
            )
            activated[batch, here, at] = value.astype(BF)
            slope[batch, here, at] = rate.astype(BF)

    def fall_part(batch, start, size, slot):
        here = pl.ds(start, size)
        result = temp[here] + matmul(activated[batch, here], flat(down_blocks[...])) + row(7)
        leaving[slot, here] = result.astype(BF)

    def forward(batch, start, size, slot):
        attend_part(batch, start, size)
        rise_part(batch, start, size)
        fall_part(batch, start, size, slot)

    def backward(batch, start, size, slot):
        here = pl.ds(start, size)
        low = entry[back, batch, here]
        vector_sum[7:8] += column_sum(low.astype(F32))
        blocks = 4
        for block in range(0, ways, blocks):
            at = slice(block * wide_share, (block + blocks) * wide_share)
            rate = matmul(low, flat(down_blocks[block : block + blocks]), NT)
            rate = rate * slope[batch, here, at].astype(F32)
            bias_sum[:, at] += column_sum(rate)
            slope[batch, here, at] = rate.astype(BF)
        temp[here] = matmul(slope[batch, here], flat(up_blocks[...]), NT)
        normal, scale = standard(middle[batch, here].astype(F32))
        grad = temp[here]
        vector_sum[1:2] += column_sum(grad * normal)
        vector_sum[3:4] += column_sum(grad)
        grad = entry[back, batch, here].astype(F32) + norm_back(grad * row(1), normal, scale)
        sum_temp[here] = grad
        vector_sum[6:7] += column_sum(grad)
        middle[batch, here] = grad.astype(BF)
        low_temp[here] = matmul(middle[batch, here], flat(merge_blocks[...]), NT).astype(BF)
        for clip in range(size // length):
            span = pl.ds(start + clip * length, length)
            for pair in range(pairs):
                lanes = [slice(p * width + pair * 128, p * width + pair * 128 + 128) for p in range(3)]
                query = projected[batch, span, lanes[0]]
                key = pair_parts(projected[batch, span, lanes[1]])
                value = pair_parts(projected[batch, span, lanes[2]])
                upper = low_temp[span, lanes[0]]
                weight = chances(batch, start + clip * length, pair)[...]
                rise = matmul(upper, value, NT)
                value_grad = pair_join(matmul(weight, upper, TN))
                parts = []
                for part, heavy in zip(halves(rise), halves(weight)):
                    heavy = heavy.astype(F32)
                    mean = jnp.sum(part * heavy, axis=-1, keepdims=True)
                    parts.append(heavy * (part - mean) * HEAD_DIM**-0.5)
                change = jnp.concatenate(parts, axis=1).astype(BF)
                query_grad = matmul(change, key)
                key_grad = pair_join(matmul(change, query, TN))
                vector_sum[4:5, lanes[0]] += column_sum(query_grad)
                vector_sum[5:6, lanes[0]] += column_sum(value_grad)
                for at, piece in zip(lanes, (query_grad, key_grad, value_grad)):
                    projected[batch, span, at] = piece.astype(BF)
        temp[here] = matmul(projected[batch, here], flat(attend_blocks[...]), NT)
        normal, scale = standard(entry[fed, batch, here].astype(F32))
        grad = temp[here]
        vector_sum[0:1] += column_sum(grad * normal)
        vector_sum[2:3] += column_sum(grad)
        leaving[slot, here] = (sum_temp[here] + norm_back(grad * row(0), normal, scale)).astype(BF)

    count = len(pieces)
    early, late = range(3), range(4, count)
    for piece in range(count):
        gather.start(piece)
    gather.first_across(count - 1)
    for distance in range(1, levels - 1):
        for piece in range(count):
            gather.from_levels(piece, distance)
            gather.from_across(piece, distance - 1)
    for piece in range(4):
        gather.from_levels(piece, levels - 1)
        gather.from_across(piece, levels - 2)
    for piece in early:
        gather.from_across(piece, levels - 1)
    for piece in early:
        gather.from_side(piece)
    vectors[...] = jnp.concatenate([vector_blocks[block, 0:8, 0:share] for block in range(ways)], axis=1)
    bias[...] = jnp.concatenate(
        [unfold(vector_blocks[block, 8:16], wide_share) for block in range(ways)], axis=1
    )
    load_own.wait()
    for piece in late:
        gather.from_levels(piece, levels - 1)
        gather.from_across(piece, levels - 2)
    for piece in (3, *late):
        gather.from_across(piece, levels - 1)
    gather.from_side(3)
    for piece in late:
        gather.from_side(piece)
    for piece in range(count):
        gather.drain(piece)

    chunks = []
    part_refs = [vector_blocks, attend_blocks, merge_blocks, up_blocks, down_blocks]
    for which, start, order, _, cols, _, shared in plan:
        if shared is None:
            from_side = chunk_refs.pop(0)
        else:
            from_side = chunks[shared].from_side.at[:, :, pl.ds(0, cols)]
        held, chunk_refs = chunk_refs[:CHUNK_REFS], chunk_refs[CHUNK_REFS:]
        chunks.append(Chunk(place, order, part_refs[which], start, [from_side] + held[:2], held[2:]))
    down_a, down_b, up_a, up_b, attend_a, attend_b, merge, vector = chunks

    def down_gradient():
        def pair_at(index):
            late = lax.div(index, levels)
            level = down_a.level_at(lax.rem(index, levels))
            return level, jnp.where(late == 0, 1 - place.row, place.row), late == 0

        def multiply(index):
            level, row, _ = pair_at(index)
            pair = level * 2 + row
            at = pl.ds(pl.multiple_of(pair * 2 * wide_share, 128), 2 * wide_share)
            tile = flat(activated[:, :, at])
            product = matmul(tile, flat(entry[back]), TN).astype(BF)
            for core in range(2):
                down_blocks[pair * 2 + core] = product[core * wide_share : (core + 1) * wide_share]
            for chunk in (down_b, down_a):
                chunk.side(pair).start()

        def join(index):
            level, row, early = pair_at(index)
            down_b.join_pair(level, row)
            pl.when(early)(down_b.across(level, level).start)
            down_a.join_pair(level, row)
            down_a.chain_open(row, jnp.where(early, 1, 0), level)

        multiply(jnp.int32(0))

        @pl.loop(1, 2 * levels)
        def _(index):
            multiply(index)
            join(index - 1)

        join(jnp.int32(2 * levels - 1))

    stores = []

    def store(target, chunk, through=None, first=0):
        def put(value):
            if through is None:
                target[:, pl.ds(chunk.start, chunk.cols)] = value
                return
            done = 0
            while done < chunk.cols:
                column = chunk.start + done
                size = min(width - column % width, chunk.cols - done)
                at = (pl.ds(first + column // width * share, share), pl.ds(column % width, size))
                through[at] = value[:, done : done + size]
                copy = pltpu.make_async_copy(
                    through.at[at], target.at[:, pl.ds(column, size)], store_sem.at[len(stores)]
                )
                copy.start()
                stores.append(copy)
                done += size

        return put

    def turn(source, place_at):
        target = probability.at[pl.ds(0, width), pl.ds(place_at * total, total)]
        target[...] = flat(source[...]).T
        return target

    def columns(left, source, chunk, credit=None):
        step = STEP if chunk.cols % STEP == 0 else chunk.cols

        @pl.loop(0, chunk.cols // step)
        def _(index):
            at = pl.multiple_of(chunk.start + index * step, 128)
            product = matmul(left[...], flat(source[:, :, pl.ds(at, step)]))
            chunk.whole[:, :, pl.ds(at, step)] = product.astype(BF).reshape(ways, width // ways, step)

        if credit is not None:
            pl.semaphore_wait(free_sem.at[credit], 1)
        chunk.send_side()

    def release(index):
        pl.semaphore_signal(
            free_sem.at[index], inc=1, device_id=(section, place.targets[SIDE]), device_id_type=MESH
        )

    def up_gradient():
        turned = turn(normed_two, 0)
        columns(turned, slope, up_a)
        columns(turned, slope, up_b)
        up_a.join_side()
        release(0)
        down_b.join_across()
        up_b.join_side()
        release(1)

    @pl.loop(0, portions)
    def _(portion):
        pl.when(section == 1)(relay_part(0, portion).wait_recv)
        forward(0, pl.multiple_of(portion * half, length), half, 0)
        pl.when(section == 0)(relay_part(0, portion).start)

    pl.when(section == 1)(keep(0).start)

    @pl.loop(1, 2 * batches)
    def _(step):
        is_forward = jnp.where(section == 0, step < batches, lax.rem(step, 2) == 0)
        batch = jnp.where(section == 0, lax.rem(step, batches), lax.div(step, 2))
        slot = jnp.where(section == 0, lax.rem(batch, 2), jnp.where(is_forward, 0, 1))

        def when(*conditions):
            return pl.when(functools.reduce(jnp.logical_and, conditions))

        @pl.when(is_forward)
        def _():
            pl.when(section == 1)(lambda: relay(batch).wait_recv())
            when(section == 0, batch >= 2)(lambda: relay(batch - 2).wait_send())
            pl.when(section == 1)(lambda: keep(batch - 1).wait())
            forward(batch, 0, rows, slot)
            pl.when(section == 0)(lambda: relay(batch, slot).start())
            pl.when(section == 1)(lambda: keep(batch, slot).start())

        @pl.when(jnp.logical_not(is_forward))
        def _():
            pl.when(section == 0)(lambda: relay(batch).wait_recv())
            when(section == 0, batch < 2)(lambda: relay(batch + batches - 2).wait_send())
            when(section == 0, batch >= 2)(lambda: keep(batch - 2).wait())
            when(section == 1, batch >= 1)(lambda: relay(batch - 1).wait_send())
            backward(batch, 0, rows, slot)
            pl.when(section == 1)(lambda: relay(batch, slot).start())
            pl.when(section == 0)(lambda: keep(batch, slot).start())

    down_gradient()
    up_gradient()

    for block in range(ways):
        vector_blocks[block, 0:8] = pad_lanes(vector_sum[:, block * share : (block + 1) * share])
        vector_blocks[block, 8:16] = fold(bias_sum[:, block * wide_share : (block + 1) * wide_share])
    vector.send_side()
    down_a.chain_pass(1)
    turned = turn(normed, 1)
    columns(turned, projected, attend_a, 0)
    vector.join_side()
    down_a.chain_pass(2)
    down_b.chain_pass(1)
    columns(turned, projected, attend_b, 1)
    attend_a.join_side()
    release(2)
    up_a.join_across()
    turned = turn(attended, 0)
    columns(turned, middle, merge, 2)
    attend_b.join_side()
    down_a.chain_end(None)
    merge.join_side()
    vector.join_across()
    up_b.join_across()
    down_b.chain_pass(2)
    vector.chain_pass(1)
    up_a.chain_pass(1)
    vector.chain_pass(2)
    down_b.chain_end(store(down_out, down_b))
    up_a.chain_pass(2)
    attend_a.join_across()
    up_b.chain_pass(1)

    def store_vectors(value):
        gain_out[...] = value[0:2, :share]
        for index in range(6):
            shift_out[index] = value[2 + index : 3 + index, :share]
        bias_out[...] = unfold(value[8:16], wide_share)

    vector.chain_end(store_vectors)
    up_a.chain_end(store(up_out, up_a, temp, 0))
    up_b.chain_pass(2)
    attend_b.join_across()
    attend_a.chain_pass(1)
    up_b.chain_end(store(up_out, up_b, temp, 0))
    attend_a.chain_pass(2)
    merge.join_across()
    attend_b.chain_pass(1)
    attend_a.chain_end(store(attend_out, attend_a, sum_temp, 0))
    attend_b.chain_pass(2)
    merge.chain_pass(1)
    attend_b.chain_end(store(attend_out, attend_b, sum_temp, 0))
    merge.chain_pass(2)
    down_a.finish(store(down_out, down_a))
    merge.chain_end(store(merge_out, merge, sum_temp, 3 * share))
    for chunk in chunks:
        chunk.drain()

    for copy in stores:
        copy.wait()

    @pl.when(section == 0)
    def _():
        keep(batches - 2).wait()
        keep(batches - 1).wait()

    @pl.when(section == 1)
    def _():
        keep(batches - 1).wait()
        relay(batches - 1).wait_send()


def settle_kernel(*refs):
    count = (len(refs) - 2) // 3
    load_sem, store_sem = refs[-2:]
    sources, targets, held = refs[:count], refs[count : 2 * count], refs[2 * count : 3 * count]
    loads = [pltpu.make_async_copy(sources[i], held[i], load_sem.at[i]) for i in range(count)]
    stores = [pltpu.make_async_copy(held[i], targets[i], store_sem.at[i]) for i in range(count)]
    for copy in loads:
        copy.start()
    for load, store in zip(loads, stores):
        load.wait()
        store.start()
    for copy in stores:
        copy.wait()


def train_step(own, attend, merge, up, down, gains, shifts, bias, clips, ways, collective_id):
    levels = ways // 4
    batches, rows, width = own.shape
    wide = up.shape[1]
    share, wide_share = width // ways, wide // ways
    length = rows // clips
    plan = [
        (4, 0, LEVELS_FIRST, wide_share, width // 2, BF, None),
        (4, width // 2, ACROSS_FIRST, wide_share, width // 2, BF, None),
        (3, 0, ACROSS_FIRST, share, wide // 2, BF, None),
        (3, wide // 2, ACROSS_FIRST, share, wide // 2, BF, None),
        (1, 0, ACROSS_FIRST, share, 2 * width, BF, 2),
        (1, 2 * width, ACROSS_FIRST, share, width, BF, 3),
        (2, 0, ACROSS_FIRST, share, width, BF, 2),
        (0, 0, ACROSS_FIRST, 16, 128, F32, None),
    ]
    dma = pltpu.SemaphoreType.DMA
    vmem, anywhere = pl.BlockSpec(memory_space=pltpu.VMEM), pl.BlockSpec(memory_space=pl.ANY)

    def held(cols, dtype=BF):
        return pltpu.VMEM((batches, rows, cols), dtype)

    scratch = [
        pltpu.VMEM((16, 128), F32),
        pltpu.VMEM((ways, 16, 128), F32),
        pltpu.VMEM((ways, share, 3 * width), BF),
        pltpu.VMEM((ways, share, width), BF),
        pltpu.VMEM((ways, share, wide), BF),
        pltpu.VMEM((ways, wide_share, width), BF),
        pltpu.VMEM((8, width), F32),
        pltpu.VMEM((1, wide), F32),
        pltpu.VMEM((8, width), F32),
        pltpu.VMEM((1, wide), F32),
        pltpu.VMEM((2, batches, rows, width), BF),
        held(3 * width),
        pltpu.VMEM((clips * HEADS // 4 * length, batches * 4 * length), BF),
        held(width),
        held(width),
        held(width),
        held(width),
        held(wide),
        held(wide),
        pltpu.VMEM((2, rows, width), BF),
        pltpu.VMEM((rows, width), BF),
        pltpu.VMEM((rows, width), F32),
        pltpu.VMEM((rows, width), F32),
        dma((6, 3)),
        dma((6, 2 * levels + 1)),
        dma((6,)),
        dma(()),
        dma((batches, 2)),
        dma((batches, 2)),
        dma((batches,)),
        pltpu.SemaphoreType.REGULAR((3,)),
        dma((9,)),
    ]
    for _, _, order, chunk_rows, cols, dtype, shared in plan:
        scratch += chunk_scratch(levels, order, chunk_rows, cols, dtype, shared is not None)

    def grad(*shape):
        return jax.ShapeDtypeStruct(shape, F32)

    results = pl.pallas_call(
        functools.partial(relay_kernel, levels, clips, plan),
        out_shape=[
            jax.ShapeDtypeStruct(own.shape, BF),
            grad(2, share),
            grad(6, 1, share),
            grad(share, 3 * width),
            grad(share, width),
            grad(share, wide),
            grad(1, wide_share),
            grad(wide_share, width),
        ],
        in_specs=[anywhere] * 5 + [vmem] * 3,
        out_specs=[anywhere, vmem, vmem, anywhere, anywhere, anywhere, vmem, vmem],
        scratch_shapes=scratch,
        compiler_params=pltpu.CompilerParams(
            collective_id=collective_id, has_side_effects=True, vmem_limit_bytes=62 * 2**20
        ),
    )(own, attend, merge, up, down, gains, shifts, bias)
    return pl.pallas_call(
        settle_kernel,
        out_shape=[jax.ShapeDtypeStruct(result.shape, result.dtype) for result in results],
        in_specs=[anywhere] * len(results),
        out_specs=[anywhere] * len(results),
        scratch_shapes=[pltpu.VMEM(result.shape, result.dtype) for result in results]
        + [dma((len(results),))] * 2,
    )(*results)


def from_behind(block, axis, distance):
    devices = range(lax.axis_size(axis))
    route = [(i - distance, i) for i in devices if i - distance in devices]
    return lax.ppermute(block, axis, route)


def normalize(features, gain_row, offset):
    centred = features - jnp.mean(features, axis=-1, keepdims=True)
    spread = jnp.mean(centred * centred, axis=-1, keepdims=True)
    return centred * lax.rsqrt(spread + epsilon) * gain_row + offset


def gelu_exact(features):
    return jax.nn.gelu(features, approximate=False)


def split_heads(matrix, clip_count):
    return matrix.reshape(clip_count, matrix.shape[0] // clip_count, HEADS, HEAD_DIM)


def layer_forward(hidden, weights, clip_count):
    attend_weight, merge_weight, up_weight, down_weight, gain_rows, offset_rows, up_bias = weights
    gain_rows = gain_rows.astype(jnp.float32)
    offset_rows = offset_rows.astype(jnp.float32)
    row_count, model_width = hidden.shape
    score_scale = HEAD_DIM ** (-0.5)
    normed = normalize(hidden, gain_rows[0], offset_rows[0]).astype(jnp.bfloat16)
    projected = jnp.dot(normed, attend_weight, preferred_element_type=jnp.float32)
    query_heads = split_heads(
        (projected[:, :model_width] + offset_rows[2]).astype(jnp.bfloat16), clip_count
    )
    key_heads = split_heads(
        projected[:, model_width : 2 * model_width].astype(jnp.bfloat16), clip_count
    )
    value_heads = split_heads(
        (projected[:, 2 * model_width :] + offset_rows[3]).astype(jnp.bfloat16), clip_count
    )
    scores = (
        jnp.einsum("clhe,cmhe->chlm", query_heads, key_heads, preferred_element_type=jnp.float32)
        * score_scale
    )
    row_peak = jnp.max(scores, axis=-1, keepdims=True)
    exponent = jnp.exp(scores - row_peak)
    row_total = jnp.sum(exponent, axis=-1, keepdims=True)
    probability = (exponent / row_total).astype(jnp.bfloat16)
    log_total = (row_peak + jnp.log(row_total))[..., 0]
    attended = jnp.einsum(
        "chlm,cmhe->clhe", probability, value_heads, preferred_element_type=jnp.float32
    )
    attended = attended.reshape(row_count, model_width).astype(jnp.bfloat16)
    middle = (
        hidden
        + jnp.dot(attended, merge_weight, preferred_element_type=jnp.float32)
        + offset_rows[4]
    )
    normed_two = normalize(middle, gain_rows[1], offset_rows[1]).astype(jnp.bfloat16)
    raised = jnp.dot(normed_two, up_weight, preferred_element_type=jnp.float32) + up_bias.astype(
        jnp.float32
    )
    activated = gelu_exact(raised).astype(jnp.bfloat16)
    result = (
        middle
        + jnp.dot(activated, down_weight, preferred_element_type=jnp.float32)
        + offset_rows[5]
    )
    saved_state = (
        hidden,
        normed,
        query_heads,
        key_heads,
        value_heads,
        log_total,
        attended,
        middle,
        normed_two,
        raised,
        activated,
    )
    return (result, saved_state)


def layer_backward(out_grad, saved_state, weights, clip_count):
    attend_weight, merge_weight, up_weight, down_weight, gain_rows, offset_rows, up_bias = weights
    gain_rows = gain_rows.astype(jnp.float32)
    offset_rows = offset_rows.astype(jnp.float32)
    (
        hidden,
        normed,
        query_heads,
        key_heads,
        value_heads,
        log_total,
        attended,
        middle,
        normed_two,
        raised,
        activated,
    ) = saved_state
    row_count, model_width = hidden.shape
    score_scale = HEAD_DIM ** (-0.5)
    low_grad = out_grad.astype(jnp.bfloat16)
    down_term = jnp.einsum("tf,td->fd", activated, low_grad, preferred_element_type=jnp.float32)
    last_bias = jnp.sum(out_grad, axis=0)
    act_grad = jnp.einsum("td,fd->tf", low_grad, down_weight, preferred_element_type=jnp.float32)
    raised_grad = jax.vjp(gelu_exact, raised)[1](act_grad)[0]
    up_bias_term = jnp.sum(raised_grad, axis=0)
    raised_low = raised_grad.astype(jnp.bfloat16)
    up_term = jnp.einsum("td,tf->df", normed_two, raised_low, preferred_element_type=jnp.float32)
    normed_two_grad = jnp.einsum(
        "tf,df->td", raised_low, up_weight, preferred_element_type=jnp.float32
    )
    second_back = jax.vjp(normalize, middle, gain_rows[1], offset_rows[1])[1]
    middle_part, gain_two, offset_two = second_back(normed_two_grad)
    middle_grad = out_grad + middle_part
    merge_bias = jnp.sum(middle_grad, axis=0)
    middle_low = middle_grad.astype(jnp.bfloat16)
    merge_term = jnp.einsum("td,te->de", attended, middle_low, preferred_element_type=jnp.float32)
    attended_grad = jnp.einsum(
        "te,de->td", middle_low, merge_weight, preferred_element_type=jnp.float32
    )
    attended_grad = split_heads(attended_grad.astype(jnp.bfloat16), clip_count)
    scores = (
        jnp.einsum("clhe,cmhe->chlm", query_heads, key_heads, preferred_element_type=jnp.float32)
        * score_scale
    )
    probability = jnp.exp(scores - log_total[..., None])
    prob_grad = jnp.einsum(
        "clhe,cmhe->chlm", attended_grad, value_heads, preferred_element_type=jnp.float32
    )
    value_grad = jnp.einsum(
        "chlm,clhe->cmhe",
        probability.astype(jnp.bfloat16),
        attended_grad,
        preferred_element_type=jnp.float32,
    )
    score_grad = probability * (
        prob_grad - jnp.sum(prob_grad * probability, axis=-1, keepdims=True)
    )
    score_grad = score_grad.astype(jnp.bfloat16)
    query_grad = (
        jnp.einsum("chlm,cmhe->clhe", score_grad, key_heads, preferred_element_type=jnp.float32)
        * score_scale
    )
    key_grad = (
        jnp.einsum("chlm,clhe->cmhe", score_grad, query_heads, preferred_element_type=jnp.float32)
        * score_scale
    )
    query_grad = query_grad.reshape(row_count, model_width)
    key_grad = key_grad.reshape(row_count, model_width)
    value_grad = value_grad.reshape(row_count, model_width)
    query_bias = jnp.sum(query_grad, axis=0)
    value_bias = jnp.sum(value_grad, axis=0)
    joined_low = jnp.concatenate([query_grad, key_grad, value_grad], axis=1).astype(jnp.bfloat16)
    attend_term = jnp.einsum("td,te->de", normed, joined_low, preferred_element_type=jnp.float32)
    normed_grad = jnp.einsum(
        "te,de->td", joined_low, attend_weight, preferred_element_type=jnp.float32
    )
    first_back = jax.vjp(normalize, hidden, gain_rows[0], offset_rows[0])[1]
    hidden_part, gain_one, offset_one = first_back(normed_grad)
    hidden_grad = middle_grad + hidden_part
    gain_term = jnp.stack([gain_one, gain_two])
    offset_term = jnp.stack([offset_one, offset_two, query_bias, value_bias, merge_bias, last_bias])
    return (
        hidden_grad,
        (attend_term, merge_term, up_term, down_term, gain_term, offset_term, up_bias_term),
    )


def plain_body(
    section_inputs,
    norm_gains,
    offsets,
    attend_weight,
    merge_weight,
    up_weight,
    up_bias,
    down_weight,
):
    shards = (attend_weight, merge_weight, up_weight, down_weight, norm_gains, offsets, up_bias)
    gathered = (
        lax.all_gather(shards[0], "fsdp", axis=1, tiled=True),
        lax.all_gather(shards[1], "fsdp", axis=1, tiled=True),
        lax.all_gather(shards[2], "fsdp", axis=1, tiled=True),
        lax.all_gather(shards[3], "fsdp", axis=1, tiled=True),
        lax.all_gather(shards[4], "fsdp", axis=2, tiled=True),
        lax.all_gather(shards[5], "fsdp", axis=2, tiled=True),
        lax.all_gather(shards[6], "fsdp", axis=1, tiled=True),
    )
    weights = tuple((tensor[0] for tensor in gathered))
    is_first = lax.axis_index("section") == 0
    own_data = section_inputs[0]
    batches, clip_count, length, model_width = own_data.shape
    row_count = clip_count * length
    own_rows = own_data.reshape(batches, row_count, model_width)
    kept_state = []
    upper_rows = []
    received = jnp.zeros((row_count, model_width), jnp.bfloat16)
    for instant in range(batches + 1):
        entering = jnp.where(is_first, own_rows[min(instant, batches - 1)], received)
        result, saved_state = layer_forward(entering.astype(jnp.float32), weights, clip_count)
        kept_state.append(saved_state)
        rounded = result.astype(jnp.bfloat16)
        if instant >= 1:
            upper_rows.append(rounded)
        if instant < batches:
            received = from_behind(rounded, "section", 1)
    gathered = (
        lax.all_gather(shards[0], "fsdp", axis=1, tiled=True),
        lax.all_gather(shards[1], "fsdp", axis=1, tiled=True),
        lax.all_gather(shards[2], "fsdp", axis=1, tiled=True),
        lax.all_gather(shards[3], "fsdp", axis=1, tiled=True),
        lax.all_gather(shards[4], "fsdp", axis=2, tiled=True),
        lax.all_gather(shards[5], "fsdp", axis=2, tiled=True),
        lax.all_gather(shards[6], "fsdp", axis=1, tiled=True),
    )
    weights = tuple((tensor[0] for tensor in gathered))
    totals = (
        jnp.zeros(weights[0].shape, jnp.float32),
        jnp.zeros(weights[1].shape, jnp.float32),
        jnp.zeros(weights[2].shape, jnp.float32),
        jnp.zeros(weights[3].shape, jnp.float32),
        jnp.zeros(weights[4].shape, jnp.float32),
        jnp.zeros(weights[5].shape, jnp.float32),
        jnp.zeros(weights[6].shape, jnp.float32),
    )
    received_grad = jnp.zeros((row_count, model_width), jnp.bfloat16)
    lower_rows = []
    for instant in range(batches + 1):
        position = batches - 1 - instant
        if position >= 0:
            own_grad = own_rows[position]
        else:
            own_grad = jnp.zeros((row_count, model_width), jnp.bfloat16)
        cotangent = jnp.where(is_first, received_grad, own_grad).astype(jnp.float32)
        hidden_grad, param_terms = layer_backward(
            cotangent, kept_state[batches - instant], weights, clip_count
        )
        totals = jax.tree.map(jnp.add, totals, param_terms)
        rounded = hidden_grad.astype(jnp.bfloat16)
        if instant >= 1:
            lower_rows.append(rounded)
        if instant < batches:
            received_grad = from_behind(rounded, "section", -1)
    ordered_lower = lower_rows[::-1]
    combined = jnp.stack(
        [
            jnp.where(is_first, lower_part, upper_part)
            for lower_part, upper_part in zip(ordered_lower, upper_rows)
        ]
    )
    section_outputs = combined.reshape(1, batches, clip_count, length, model_width)
    reduced = (
        lax.psum_scatter(totals[0][None], "fsdp", scatter_dimension=1, tiled=True),
        lax.psum_scatter(totals[1][None], "fsdp", scatter_dimension=1, tiled=True),
        lax.psum_scatter(totals[2][None], "fsdp", scatter_dimension=1, tiled=True),
        lax.psum_scatter(totals[3][None], "fsdp", scatter_dimension=1, tiled=True),
        lax.psum_scatter(totals[4][None], "fsdp", scatter_dimension=2, tiled=True),
        lax.psum_scatter(totals[5][None], "fsdp", scatter_dimension=2, tiled=True),
        lax.psum_scatter(totals[6][None], "fsdp", scatter_dimension=1, tiled=True),
    )
    return (
        section_outputs,
        reduced[4],
        reduced[5],
        reduced[0],
        reduced[1],
        reduced[2],
        reduced[6],
        reduced[3],
    )


def body(
    section_inputs,
    norm_gains,
    offsets,
    attend_weight,
    merge_weight,
    up_weight,
    up_bias,
    down_weight,
):
    ways = lax.axis_size("fsdp")
    if ways % 4 or attend_weight.shape[1] % 16:
        return plain_body(
            section_inputs,
            norm_gains,
            offsets,
            attend_weight,
            merge_weight,
            up_weight,
            up_bias,
            down_weight,
        )
    batches, clips, length, width = section_inputs.shape[1:]
    own = section_inputs.reshape(batches, clips * length, width)
    results = train_step(
        own,
        attend_weight[0],
        merge_weight[0],
        up_weight[0],
        down_weight[0],
        norm_gains[0],
        offsets[0],
        up_bias,
        clips,
        ways,
        1,
    )
    section_outputs, gains, shifts, attend, merge, up, bias, down = results
    return (
        section_outputs.reshape(section_inputs.shape),
        gains[None],
        shifts.swapaxes(0, 1),
        attend[None],
        merge[None],
        up[None],
        bias,
        down[None],
    )


def solution(mesh):
    return jax.shard_map(
        body,
        mesh=mesh,
        in_specs=(
            P("section", None, "fsdp", None, None),
            P("section", None, "fsdp"),
            P("section", None, "fsdp"),
            P("section", "fsdp", None),
            P("section", "fsdp", None),
            P("section", "fsdp", None),
            P("section", "fsdp"),
            P("section", "fsdp", None),
        ),
        out_specs=(
            P("section", None, "fsdp", None, None),
            P("section", None, "fsdp"),
            P("section", None, "fsdp"),
            P("section", "fsdp", None),
            P("section", "fsdp", None),
            P("section", "fsdp", None),
            P("section", "fsdp"),
            P("section", "fsdp", None),
        ),
        check_vma=False,
    )
```

```python
import functools
import math

import jax
import jax.numpy as jnp
from jax import lax
from jax.experimental import pallas as pl
from jax.experimental.pallas import tpu as pltpu
from jax.sharding import PartitionSpec as P

MESH = pl.DeviceIdType.MESH

HEADS = 12
HEAD_DIM = 64
epsilon = 1e-05
BF, F32 = jnp.bfloat16, jnp.float32
NT = (((1,), (1,)), ((), ()))
TN = (((0,), (0,)), ((), ()))

SIDE, ACROSS, UP, DOWN = range(4)
LEVELS_FIRST, ACROSS_FIRST = 0, 1

class Sends:
    def __init__(self):
        self.items = []

    def start(self, copy, when):
        if when is None:
            copy.start()
        else:
            pl.when(when)(copy.start)
        self.items.append((copy, when))

    def drain(self):
        for copy, when in self.items:
            if when is None:
                copy.wait_send()
            else:
                pl.when(when)(copy.wait_send)


def matmul(left, right, dims=(((1,), (0,)), ((), ()))):
    return lax.dot_general(left, right, dims, preferred_element_type=F32)


def standard(features):
    centred = features - jnp.mean(features, axis=-1, keepdims=True)
    scale = lax.rsqrt(jnp.mean(centred * centred, axis=-1, keepdims=True) + epsilon)
    return centred * scale, scale


def gelu_and_slope(raised):
    share = 0.5 + 0.5 * lax.erf(raised * math.sqrt(0.5))
    bell = jnp.exp(raised * raised * -0.5) * (1.0 / math.sqrt(2.0 * math.pi))
    return raised * share, share + raised * bell


def norm_back(upper, normal, scale):
    shift = jnp.mean(upper, axis=-1, keepdims=True)
    slope = jnp.mean(upper * normal, axis=-1, keepdims=True)
    return (upper - shift - normal * slope) * scale


def column_sum(values):
    return jnp.sum(values, axis=0, keepdims=True)


def pair_parts(matrix):
    lane = lax.broadcasted_iota(jnp.int32, matrix.shape, 1)
    zero = jnp.zeros_like(matrix)
    first = lane < HEAD_DIM
    return jnp.concatenate([jnp.where(first, matrix, zero), jnp.where(first, zero, matrix)], axis=0)


def pair_join(stacked):
    rows = stacked.shape[0] // 2
    lane = lax.broadcasted_iota(jnp.int32, (rows, stacked.shape[1]), 1)
    return jnp.where(lane < HEAD_DIM, stacked[:rows], stacked[rows:])


def halves(scores):
    keys = scores.shape[1] // 2
    return scores[:, :keys], scores[:, keys:]


class Place:
    def __init__(self, levels):
        self.levels = levels
        self.section, self.mine = lax.axis_index("section"), lax.axis_index("fsdp")
        self.level = lax.div(self.mine, 4)
        self.row = lax.rem(lax.div(self.mine, 2), 2)
        self.core = lax.rem(self.mine, 2)
        self.has_up, self.has_down = self.level < levels - 1, self.level > 0
        self.targets = {SIDE: self.mine ^ 1, ACROSS: self.mine ^ 2, UP: self.mine + 4, DOWN: self.mine - 4}

    def block(self, level, row, core):
        return level * 4 + row * 2 + core

    def greet(self):
        barrier = pltpu.get_barrier_semaphore()

        def hello(section, target):
            pl.semaphore_signal(barrier, inc=1, device_id=(section, target), device_id_type=MESH)

        hello(1 - self.section, self.mine)
        hello(self.section, self.targets[SIDE])
        hello(self.section, self.targets[ACROSS])
        pl.when(self.has_down)(lambda: hello(self.section, self.targets[DOWN]))
        pl.when(self.has_up)(lambda: hello(self.section, self.targets[UP]))
        ends = (self.level == 0).astype(jnp.int32) + (self.level == self.levels - 1).astype(jnp.int32)
        pl.semaphore_wait(barrier, 5 - ends)


class Piece:
    def __init__(self, shard, ref, kind, start=0, size=None):
        self.shard, self.ref, self.plain = shard, ref, kind == "level"
        self.rows = None if size is None else pl.ds(start, size)

    def block(self, index):
        return self.ref.at[index] if self.rows is None else self.ref.at[index, self.rows]

    def span(self, count):
        return self.block(pl.ds(0, count))


class Gather:
    def __init__(self, place, pieces, send_sem, recv_sem, local_sem):
        self.place, self.pieces = place, pieces
        self.send_sem, self.recv_sem, self.local_sem = send_sem, recv_sem, local_sem
        self.side = 2 * place.levels

    def copy(self, source, target, out_sem, in_sem, way):
        return pltpu.make_async_remote_copy(
            src_ref=source,
            dst_ref=target,
            send_sem=out_sem,
            recv_sem=in_sem,
            device_id=(self.place.section, self.place.targets[way]),
            device_id_type=MESH,
        )

    def send(self, piece, level, row, way, own=False, when=None):
        held = self.pieces[piece]
        target = held.block(self.place.block(level, row, self.place.core))
        kind = {SIDE: 0, ACROSS: 1, UP: 2, DOWN: 2}[way]
        copy = self.copy(
            held.shard if own else target,
            target,
            self.send_sem.at[piece, kind],
            self.recv_sem.at[piece, self.side if way == SIDE else level * 2 + row],
            way,
        )
        if when is None:
            copy.start()
        else:
            pl.when(when)(copy.start)

    def arrived(self, piece, level, row, when=None):
        target = self.pieces[piece].block(self.place.block(level, row, self.place.core))
        index = level * 2 + row
        copy = self.copy(target, target, self.send_sem.at[piece, 0], self.recv_sem.at[piece, index], SIDE)
        if when is None:
            copy.wait_recv()
        else:
            pl.when(when)(copy.wait_recv)

    def local(self, piece):
        held = self.pieces[piece]
        return pltpu.make_async_copy(held.shard, held.block(self.place.mine), self.local_sem.at[piece])

    def start(self, piece):
        place = self.place
        self.send(piece, place.level, place.row, ACROSS, own=True)
        self.send(piece, place.level, place.row, UP, own=True, when=place.has_up)
        self.send(piece, place.level, place.row, DOWN, own=True, when=place.has_down)
        self.send(piece, place.level, place.row, SIDE, own=True)
        self.local(piece).start()

    def first_across(self, piece):
        place = self.place
        level, row = place.level, 1 - place.row
        self.arrived(piece, level, row)
        self.send(piece, level, row, UP, when=place.has_up)
        self.send(piece, level, row, DOWN, when=place.has_down)
        self.send(piece, level, row, SIDE)

    def from_levels(self, piece, distance):
        place = self.place
        plain = self.pieces[piece].plain
        for row in (place.row,) if plain else (place.row, 1 - place.row):
            for sign in (-1, 1):
                other = place.level + sign * distance
                here = other >= 0 if sign < 0 else other < place.levels
                onward = place.has_up if sign < 0 else place.has_down
                self.arrived(piece, other, row, here)
                if distance < place.levels - 1:
                    way = UP if sign < 0 else DOWN
                    self.send(piece, other, row, way, when=jnp.logical_and(here, onward))
                if plain:
                    self.send(piece, other, row, ACROSS, when=here)
                self.send(piece, other, row, SIDE, when=here)

    def from_across(self, piece, distance):
        place = self.place
        if not self.pieces[piece].plain:
            return
        for sign in (-1, 1) if distance else (1,):
            other = place.level + sign * distance
            here = None
            if distance:
                here = other >= 0 if sign < 0 else other < place.levels
            self.arrived(piece, other, 1 - place.row, here)
            self.send(piece, other, 1 - place.row, SIDE, when=here)

    def from_side(self, piece):
        self.local(piece).wait()
        span = self.pieces[piece].span(self.side)
        self.copy(span, span, self.send_sem.at[piece, 0], self.recv_sem.at[piece, self.side], SIDE).wait_recv()

    def drain(self, piece):
        place, held = self.place, self.pieces[piece]

        def sent(count, kind):
            span = held.span(count)
            return self.copy(span, span, self.send_sem.at[piece, kind], self.recv_sem.at[piece, 0], SIDE)

        rows = 1 if held.plain else 2
        sent(self.side, 0).wait_send()
        sent(place.levels if held.plain else 1, 1).wait_send()
        inner = jnp.logical_and(place.has_up, place.has_down)
        pl.when(inner)(sent(rows * (place.levels + 1), 2).wait_send)
        pl.when(jnp.logical_not(inner))(sent(rows, 2).wait_send)


class Chunk:
    def __init__(self, place, order, part, start, refs, sems):
        self.place, self.order, self.levels = place, order, place.levels
        self.whole, self.start = part, start
        self.from_side, self.from_across, self.from_chain = refs
        self.cols = self.from_side.shape[2]
        (
            self.side_out,
            self.side_in,
            self.across_out,
            self.across_in,
            self.chain_out,
            self.chain_in,
        ) = sems

    def part(self, block):
        return self.whole.at[block, :, pl.ds(self.start, self.cols)]

    def copy(self, block, target, out_sem, in_sem, way):
        return pltpu.make_async_remote_copy(
            src_ref=self.part(block),
            dst_ref=target,
            send_sem=out_sem,
            recv_sem=in_sem,
            device_id=(self.place.section, self.place.targets[way]),
            device_id_type=MESH,
        )

    def side(self, pair):
        block = pair * 2 + 1 - self.place.core
        return self.copy(
            block, self.from_side.at[pair], self.side_out, self.side_in.at[pair], SIDE
        )

    def across(self, level, slot):
        block = self.place.block(level, 1 - self.place.row, self.place.core)
        return self.copy(
            block,
            self.from_across.at[slot],
            self.across_out,
            self.across_in.at[slot],
            ACROSS,
        )

    def below_index(self, target, level):
        return target - level

    def above_index(self, target):
        return self.levels - target

    def up(self, row, slot, target):
        index = self.below_index(target, self.place.level + 1)
        return self.copy(
            self.place.block(target, row, self.place.core),
            self.from_chain.at[slot, index],
            self.chain_out.at[slot],
            self.chain_in.at[slot, index],
            UP,
        )

    def down(self, row, slot, target):
        index = self.above_index(target)
        return self.copy(
            self.place.block(target, row, self.place.core),
            self.from_chain.at[slot, index],
            self.chain_out.at[slot],
            self.chain_in.at[slot, index],
            DOWN,
        )

    def arrived(self, slot, index):
        target = self.from_chain.at[slot, index]
        pltpu.make_async_remote_copy(
            src_ref=target,
            dst_ref=target,
            send_sem=self.side_out,
            recv_sem=self.chain_in.at[slot, index],
            device_id=(self.place.section, self.place.targets[SIDE]),
            device_id_type=MESH,
        ).wait_recv()

    def add(self, block, term):
        part = self.part(block)
        part[...] = part[...] + term

    def send_side(self):
        @pl.loop(0, self.levels * 2)
        def _(pair):
            self.side(pair).start()

    def join_pair(self, level, row):
        pair = level * 2 + row
        self.side(pair).wait_recv()
        self.add(pair * 2 + self.place.core, self.from_side[pair])

    def level_at(self, index):
        return jnp.where(self.place.level < self.levels // 2, self.levels - 1 - index, index)

    def join_side(self):
        place = self.place
        for other in (True, False):
            row = 1 - place.row if other else place.row

            @pl.loop(0, self.levels)
            def _(index):
                level = self.level_at(index)
                self.join_pair(level, row)
                if other and self.order == ACROSS_FIRST:
                    self.across(level, level).start()

    def chain_open(self, row, slot, target):
        level, last = self.place.level, self.levels - 1
        pl.when(jnp.logical_and(level == 0, target > 0))(lambda: self.up(row, slot, target).start())
        pl.when(jnp.logical_and(level == last, target < last))(
            lambda: self.down(row, slot, target).start()
        )

    def join_across(self):
        place = self.place

        @pl.loop(0, self.levels)
        def _(index):
            level = self.level_at(index)
            self.across(level, level).wait_recv()
            self.add(place.block(level, place.row, place.core), self.from_across[level])
            self.chain_open(place.row, 0, level)

    def rows(self):
        row = self.place.row
        return ((0, row), (1, 1 - row)) if self.order == LEVELS_FIRST else ((0, row),)

    def chain_pass(self, distance):
        place, last = self.place, self.levels - 1
        for slot, row in self.rows():
            for target in range(last, distance, -1):

                @pl.when(place.level == distance)
                def _():
                    index = self.below_index(target, place.level)
                    self.arrived(slot, index)
                    self.add(place.block(target, row, place.core), self.from_chain[slot, index])
                    self.up(row, slot, target).start()

            for target in range(last - distance):

                @pl.when(place.level == last - distance)
                def _():
                    index = self.above_index(target)
                    self.arrived(slot, index)
                    self.add(place.block(target, row, place.core), self.from_chain[slot, index])
                    self.down(row, slot, target).start()

    def chain_end(self, out):
        place, last = self.place, self.levels - 1
        for slot, row in reversed(self.rows()):
            block = place.block(place.level, row, place.core)

            @pl.when(place.level > 0)
            def _():
                index = self.below_index(place.level, place.level)
                self.arrived(slot, index)
                self.add(block, self.from_chain[slot, index])

            @pl.when(place.level < last)
            def _():
                index = self.above_index(place.level)
                self.arrived(slot, index)
                self.add(block, self.from_chain[slot, index])

            if slot == 1:
                self.across(place.level, 0).start()
        if self.order == ACROSS_FIRST:
            out(self.part(place.mine)[...].astype(F32))

    def finish(self, out):
        if self.order == LEVELS_FIRST:
            self.across(self.place.level, 0).wait_recv()
            out(self.part(self.place.mine)[...].astype(F32) + self.from_across[0].astype(F32))

    def drain(self):
        def sent(span, out_sem):
            pltpu.make_async_remote_copy(
                src_ref=span,
                dst_ref=span,
                send_sem=out_sem,
                recv_sem=self.side_in.at[0],
                device_id=(self.place.section, self.place.targets[SIDE]),
                device_id_type=MESH,
            ).wait_send()

        sent(self.from_side, self.side_out)
        sent(self.from_across, self.across_out)
        for slot, _ in self.rows():
            sent(self.from_chain.at[slot, pl.ds(0, self.levels - 1)], self.chain_out.at[slot])


def chunk_scratch(levels, order, rows, cols, dtype, shared):
    block = (rows, cols)
    slots = 2 if order == LEVELS_FIRST else 1
    crossing = 1 if order == LEVELS_FIRST else levels
    dma = pltpu.SemaphoreType.DMA
    from_side = [] if shared else [pltpu.VMEM((levels * 2,) + block, dtype)]
    return from_side + [
        pltpu.VMEM((crossing,) + block, dtype),
        pltpu.VMEM((slots, levels + 1) + block, dtype),
        dma(()),
        dma((levels * 2,)),
        dma(()),
        dma((crossing,)),
        dma((slots,)),
        dma((slots, levels + 1)),
    ]


CHUNK_REFS = 8
STEP = 512


def pad_lanes(rows, lanes=128):
    missing = lanes - rows.shape[1]
    if not missing:
        return rows
    return jnp.concatenate([rows, jnp.zeros((rows.shape[0], missing), rows.dtype)], axis=1)


def tile_of(rows):
    missing = 8 - rows.shape[0]
    if not missing:
        return rows
    return jnp.concatenate([rows, jnp.zeros((missing, rows.shape[1]), rows.dtype)], axis=0)


def fold(line):
    pieces = [pad_lanes(line[:, at : at + 128]) for at in range(0, line.shape[1], 128)]
    return tile_of(jnp.concatenate(pieces, axis=0))


def unfold(rows, count):
    pieces = []
    for index in range(-(-count // 128)):
        pieces.append(rows[index : index + 1, : min(128, count - index * 128)])
    return jnp.concatenate(pieces, axis=1)


def relay_kernel(levels, clips, plan, *refs):
    own, attend_shard, merge_shard, up_shard, down_shard, gain_shard, shift_shard, bias_shard = refs[:8]
    out, gain_out, shift_out, attend_out, merge_out, up_out, bias_out, down_out = refs[8:16]
    (
        packed,
        vector_blocks,
        attend_blocks,
        merge_blocks,
        up_blocks,
        down_blocks,
        vectors,
        bias,
        vector_sum,
        bias_sum,
        entry,
        projected,
        probability,
        normed,
        attended,
        middle,
        normed_two,
        activated,
        slope,
        leaving,
        low_temp,
        temp,
        sum_temp,
        gather_send,
        gather_recv,
        gather_local,
        load_sem,
        send_sem,
        recv_sem,
        out_sem,
        free_sem,
        store_sem,
    ) = refs[16:48]
    chunk_refs = list(refs[48:])
    place = Place(levels)
    section, mine = place.section, place.mine
    batches, rows, width = own.shape
    wide = up_shard.shape[1]
    ways = levels * 4
    share, wide_share = width // ways, wide // ways
    length = rows // clips
    pairs = HEADS // 2
    total = batches * rows

    load_own = pltpu.make_async_copy(own, entry.at[0], load_sem)
    load_own.start()
    packed[0:8] = pad_lanes(
        jnp.concatenate([gain_shard[...], shift_shard[...]], axis=0).astype(F32)
    )
    packed[8:16] = fold(bias_shard[...].astype(F32))
    place.greet()

    half_share = wide_share // 2
    pieces = [
        Piece(packed, vector_blocks, "level"),
        Piece(attend_shard, attend_blocks, "level"),
        Piece(merge_shard, merge_blocks, "level"),
        Piece(up_shard, up_blocks, "level"),
        Piece(down_shard.at[pl.ds(0, half_share)], down_blocks, "level", 0, half_share),
        Piece(down_shard.at[pl.ds(half_share, half_share)], down_blocks, "across", half_share, half_share),
    ]
    gather = Gather(place, pieces, gather_send, gather_recv, gather_local)
    def flat(blocks):
        return blocks.reshape(-1, blocks.shape[-1])

    half = rows // 2 if clips % 2 == 0 else rows
    portions = rows // half

    def relay_part(batch, portion, slot=0):
        here = pl.ds(portion * half, half)
        return pltpu.make_async_remote_copy(
            src_ref=leaving.at[slot, here],
            dst_ref=entry.at[1, batch, here],
            send_sem=send_sem.at[batch, portion],
            recv_sem=recv_sem.at[batch, portion],
            device_id=(1 - section, mine),
            device_id_type=MESH,
        )

    class Relay:
        def __init__(self, batch, slot=0):
            self.copies = [relay_part(batch, portion, slot) for portion in range(portions)]

        def start(self):
            for copy in self.copies:
                copy.start()

        def wait_send(self):
            for copy in self.copies:
                copy.wait_send()

        def wait_recv(self):
            for copy in self.copies:
                copy.wait_recv()

    relay = Relay

    def keep(batch, slot=0):
        return pltpu.make_async_copy(leaving.at[slot], out.at[batch], out_sem.at[batch])

    vector_sum[...] = jnp.zeros_like(vector_sum)
    bias_sum[...] = jnp.zeros_like(bias_sum)
    fed, back = section, 1 - section

    def row(index):
        return vectors[index : index + 1, :]

    def chances(batch, start, pair):
        at = pl.multiple_of(batch * 4 * length + (pair % 2) * 2 * length, 128)
        first = start * (pairs // 2) + (pair // 2) * length
        return probability.at[pl.ds(first, length), pl.ds(at, 2 * length)]

    def attend_part(batch, start, size):
        here = pl.ds(start, size)
        normal, _ = standard(entry[fed, batch, here].astype(F32))
        normed[batch, here] = (normal * row(0) + row(2)).astype(BF)
        for part, shift in ((0, 4), (1, None), (2, 5)):
            at = slice(part * width, (part + 1) * width)
            value = matmul(normed[batch, here], flat(attend_blocks[:, :, at]))
            if shift is not None:
                value = value + row(shift)
            projected[batch, here, at] = value.astype(BF)
        for clip in range(size // length):
            span = pl.ds(start + clip * length, length)
            for pair in range(pairs):
                lanes = [slice(p * width + pair * 128, p * width + pair * 128 + 128) for p in range(3)]
                query = projected[batch, span, lanes[0]] * jnp.asarray(HEAD_DIM**-0.5, BF)
                key = pair_parts(projected[batch, span, lanes[1]])
                scores = matmul(query, key, NT)
                parts = []
                for half in halves(scores):
                    exponent = jnp.exp(half - jnp.max(half, axis=-1, keepdims=True))
                    parts.append(exponent * (1.0 / jnp.sum(exponent, axis=-1, keepdims=True)))
                weight = jnp.concatenate(parts, axis=1).astype(BF)
                chances(batch, start + clip * length, pair)[...] = weight
                value = pair_parts(projected[batch, span, lanes[2]])
                attended[batch, span, lanes[0]] = matmul(weight, value).astype(BF)
        joined = matmul(attended[batch, here], flat(merge_blocks[...])) + row(6)
        temp[here] = entry[fed, batch, here].astype(F32) + joined
        middle[batch, here] = temp[here].astype(BF)
        normal, _ = standard(temp[here])
        normed_two[batch, here] = (normal * row(1) + row(3)).astype(BF)

    def rise_part(batch, start, size):
        here = pl.ds(start, size)
        tile = 256
        for first in range(0, wide, tile):
            at = slice(first, first + tile)
            value, rate = gelu_and_slope(
                matmul(normed_two[batch, here], flat(up_blocks[:, :, at])) + bias[:, at]
            )
            activated[batch, here, at] = value.astype(BF)
            slope[batch, here, at] = rate.astype(BF)

    def fall_part(batch, start, size, slot):
        here = pl.ds(start, size)
        result = temp[here] + matmul(activated[batch, here], flat(down_blocks[...])) + row(7)
        leaving[slot, here] = result.astype(BF)

    def forward(batch, start, size, slot):
        attend_part(batch, start, size)
        rise_part(batch, start, size)
        fall_part(batch, start, size, slot)

    def backward(batch, start, size, slot):
        here = pl.ds(start, size)
        low = entry[back, batch, here]
        vector_sum[7:8] += column_sum(low.astype(F32))
        blocks = 4
        for block in range(0, ways, blocks):
            at = slice(block * wide_share, (block + blocks) * wide_share)
            rate = matmul(low, flat(down_blocks[block : block + blocks]), NT)
            rate = rate * slope[batch, here, at].astype(F32)
            bias_sum[:, at] += column_sum(rate)
            slope[batch, here, at] = rate.astype(BF)
        temp[here] = matmul(slope[batch, here], flat(up_blocks[...]), NT)
        normal, scale = standard(middle[batch, here].astype(F32))
        grad = temp[here]
        vector_sum[1:2] += column_sum(grad * normal)
        vector_sum[3:4] += column_sum(grad)
        grad = entry[back, batch, here].astype(F32) + norm_back(grad * row(1), normal, scale)
        sum_temp[here] = grad
        vector_sum[6:7] += column_sum(grad)
        middle[batch, here] = grad.astype(BF)
        low_temp[here] = matmul(middle[batch, here], flat(merge_blocks[...]), NT).astype(BF)
        for clip in range(size // length):
            span = pl.ds(start + clip * length, length)
            for pair in range(pairs):
                lanes = [slice(p * width + pair * 128, p * width + pair * 128 + 128) for p in range(3)]
                query = projected[batch, span, lanes[0]]
                key = pair_parts(projected[batch, span, lanes[1]])
                value = pair_parts(projected[batch, span, lanes[2]])
                upper = low_temp[span, lanes[0]]
                weight = chances(batch, start + clip * length, pair)[...]
                rise = matmul(upper, value, NT)
                value_grad = pair_join(matmul(weight, upper, TN))
                parts = []
                for part, heavy in zip(halves(rise), halves(weight)):
                    heavy = heavy.astype(F32)
                    mean = jnp.sum(part * heavy, axis=-1, keepdims=True)
                    parts.append(heavy * (part - mean) * HEAD_DIM**-0.5)
                change = jnp.concatenate(parts, axis=1).astype(BF)
                query_grad = matmul(change, key)
                key_grad = pair_join(matmul(change, query, TN))
                vector_sum[4:5, lanes[0]] += column_sum(query_grad)
                vector_sum[5:6, lanes[0]] += column_sum(value_grad)
                for at, piece in zip(lanes, (query_grad, key_grad, value_grad)):
                    projected[batch, span, at] = piece.astype(BF)
        temp[here] = matmul(projected[batch, here], flat(attend_blocks[...]), NT)
        normal, scale = standard(entry[fed, batch, here].astype(F32))
        grad = temp[here]
        vector_sum[0:1] += column_sum(grad * normal)
        vector_sum[2:3] += column_sum(grad)
        leaving[slot, here] = (sum_temp[here] + norm_back(grad * row(0), normal, scale)).astype(BF)

    count = len(pieces)
    early, late = range(3), range(4, count)
    for piece in range(count):
        gather.start(piece)
    gather.first_across(count - 1)
    for distance in range(1, levels - 1):
        for piece in range(count):
            gather.from_levels(piece, distance)
            gather.from_across(piece, distance - 1)
    for piece in range(4):
        gather.from_levels(piece, levels - 1)
        gather.from_across(piece, levels - 2)
    for piece in early:
        gather.from_across(piece, levels - 1)
    for piece in early:
        gather.from_side(piece)
    vectors[...] = jnp.concatenate([vector_blocks[block, 0:8, 0:share] for block in range(ways)], axis=1)
    bias[...] = jnp.concatenate(
        [unfold(vector_blocks[block, 8:16], wide_share) for block in range(ways)], axis=1
    )
    load_own.wait()
    for piece in late:
        gather.from_levels(piece, levels - 1)
        gather.from_across(piece, levels - 2)
    for piece in (3, *late):
        gather.from_across(piece, levels - 1)
    gather.from_side(3)
    for piece in late:
        gather.from_side(piece)
    for piece in range(count):
        gather.drain(piece)

    chunks = []
    part_refs = [vector_blocks, attend_blocks, merge_blocks, up_blocks, down_blocks]
    for which, start, order, _, cols, _, shared in plan:
        if shared is None:
            from_side = chunk_refs.pop(0)
        else:
            from_side = chunks[shared].from_side.at[:, :, pl.ds(0, cols)]
        held, chunk_refs = chunk_refs[:CHUNK_REFS], chunk_refs[CHUNK_REFS:]
        chunks.append(Chunk(place, order, part_refs[which], start, [from_side] + held[:2], held[2:]))
    down_a, down_b, up_a, up_b, attend_a, attend_b, merge, vector = chunks

    def down_gradient():
        def pair_at(index):
            late = lax.div(index, levels)
            level = down_a.level_at(lax.rem(index, levels))
            return level, jnp.where(late == 0, 1 - place.row, place.row), late == 0

        def multiply(index):
            level, row, _ = pair_at(index)
            pair = level * 2 + row
            at = pl.ds(pl.multiple_of(pair * 2 * wide_share, 128), 2 * wide_share)
            tile = flat(activated[:, :, at])
            product = matmul(tile, flat(entry[back]), TN).astype(BF)
            for core in range(2):
                down_blocks[pair * 2 + core] = product[core * wide_share : (core + 1) * wide_share]
            for chunk in (down_b, down_a):
                chunk.side(pair).start()

        def join(index):
            level, row, early = pair_at(index)
            down_b.join_pair(level, row)
            pl.when(early)(down_b.across(level, level).start)
            down_a.join_pair(level, row)
            down_a.chain_open(row, jnp.where(early, 1, 0), level)

        multiply(jnp.int32(0))

        @pl.loop(1, 2 * levels)
        def _(index):
            multiply(index)
            join(index - 1)

        join(jnp.int32(2 * levels - 1))

    stores = []

    def store(target, chunk, through=None, first=0):
        def put(value):
            if through is None:
                target[:, pl.ds(chunk.start, chunk.cols)] = value
                return
            done = 0
            while done < chunk.cols:
                column = chunk.start + done
                size = min(width - column % width, chunk.cols - done)
                at = (pl.ds(first + column // width * share, share), pl.ds(column % width, size))
                through[at] = value[:, done : done + size]
                copy = pltpu.make_async_copy(
                    through.at[at], target.at[:, pl.ds(column, size)], store_sem.at[len(stores)]
                )
                copy.start()
                stores.append(copy)
                done += size

        return put

    def turn(source, place_at):
        target = probability.at[pl.ds(0, width), pl.ds(place_at * total, total)]
        target[...] = flat(source[...]).T
        return target

    def columns(left, source, chunk, credit=None):
        step = STEP if chunk.cols % STEP == 0 else chunk.cols

        @pl.loop(0, chunk.cols // step)
        def _(index):
            at = pl.multiple_of(chunk.start + index * step, 128)
            product = matmul(left[...], flat(source[:, :, pl.ds(at, step)]))
            chunk.whole[:, :, pl.ds(at, step)] = product.astype(BF).reshape(ways, width // ways, step)

        if credit is not None:
            pl.semaphore_wait(free_sem.at[credit], 1)
        chunk.send_side()

    def release(index):
        pl.semaphore_signal(
            free_sem.at[index], inc=1, device_id=(section, place.targets[SIDE]), device_id_type=MESH
        )

    @pl.loop(0, portions)
    def _(portion):
        pl.when(section == 1)(relay_part(0, portion).wait_recv)
        forward(0, pl.multiple_of(portion * half, length), half, 0)
        pl.when(section == 0)(relay_part(0, portion).start)

    pl.when(section == 1)(keep(0).start)

    @pl.loop(1, 2 * batches)
    def _(step):
        is_forward = jnp.where(section == 0, step < batches, lax.rem(step, 2) == 0)
        batch = jnp.where(section == 0, lax.rem(step, batches), lax.div(step, 2))
        slot = jnp.where(section == 0, lax.rem(batch, 2), jnp.where(is_forward, 0, 1))

        def when(*conditions):
            return pl.when(functools.reduce(jnp.logical_and, conditions))

        @pl.when(is_forward)
        def _():
            pl.when(section == 1)(lambda: relay(batch).wait_recv())
            when(section == 0, batch >= 2)(lambda: relay(batch - 2).wait_send())
            pl.when(section == 1)(lambda: keep(batch - 1).wait())
            forward(batch, 0, rows, slot)
            pl.when(section == 0)(lambda: relay(batch, slot).start())
            pl.when(section == 1)(lambda: keep(batch, slot).start())

        @pl.when(jnp.logical_not(is_forward))
        def _():
            pl.when(section == 0)(lambda: relay(batch).wait_recv())
            when(section == 0, batch < 2)(lambda: relay(batch + batches - 2).wait_send())
            when(section == 0, batch >= 2)(lambda: keep(batch - 2).wait())
            when(section == 1, batch >= 1)(lambda: relay(batch - 1).wait_send())
            backward(batch, 0, rows, slot)
            pl.when(section == 1)(lambda: relay(batch, slot).start())
            pl.when(section == 0)(lambda: keep(batch, slot).start())

    down_gradient()

    for block in range(ways):
        vector_blocks[block, 0:8] = pad_lanes(vector_sum[:, block * share : (block + 1) * share])
        vector_blocks[block, 8:16] = fold(bias_sum[:, block * wide_share : (block + 1) * wide_share])
    vector.send_side()

    def store_vectors(value):
        gain_out[...] = value[0:2, :share]
        for index in range(6):
            shift_out[index] = value[2 + index : 3 + index, :share]
        bias_out[...] = unfold(value[8:16], wide_share)

    turned_up = turn(normed_two, 0)
    columns(turned_up, slope, up_a)
    up_a.join_side()
    release(0)
    columns(turned_up, slope, up_b)
    down_a.chain_pass(1)
    vector.join_side()
    down_b.join_across()
    turned_attend = turn(normed, 1)
    columns(turned_attend, projected, attend_a, 0)
    up_b.join_side()
    release(1)
    up_a.join_across()
    vector.join_across()
    down_a.chain_pass(2)
    down_b.chain_pass(1)
    attend_a.join_side()
    release(2)
    columns(turned_attend, projected, attend_b, 1)
    turned_merge = turn(attended, 0)
    columns(turned_merge, middle, merge, 2)
    attend_b.join_side()
    up_a.chain_pass(1)
    merge.join_side()
    up_b.join_across()
    up_a.chain_pass(2)
    down_b.chain_pass(2)
    vector.chain_pass(1)
    down_a.chain_end(None)
    up_b.chain_pass(1)
    up_b.chain_pass(2)
    vector.chain_pass(2)
    attend_a.join_across()
    attend_a.chain_pass(1)
    attend_b.join_across()
    up_b.chain_end(store(up_out, up_b, temp, 0))
    attend_b.chain_pass(1)
    down_b.chain_end(store(down_out, down_b))
    vector.chain_end(store_vectors)
    attend_a.chain_pass(2)
    attend_b.chain_pass(2)
    merge.join_across()
    merge.chain_pass(1)
    up_a.chain_end(store(up_out, up_a, temp, 0))
    attend_a.chain_end(store(attend_out, attend_a, sum_temp, 0))
    merge.chain_pass(2)
    down_a.finish(store(down_out, down_a))
    attend_b.chain_end(store(attend_out, attend_b, sum_temp, 0))
    merge.chain_end(store(merge_out, merge, sum_temp, 3 * share))
    for chunk in chunks:
        chunk.drain()

    for copy in stores:
        copy.wait()

    @pl.when(section == 0)
    def _():
        keep(batches - 2).wait()
        keep(batches - 1).wait()

    @pl.when(section == 1)
    def _():
        keep(batches - 1).wait()
        relay(batches - 1).wait_send()


def settle_kernel(*refs):
    count = (len(refs) - 2) // 3
    load_sem, store_sem = refs[-2:]
    sources, targets, held = refs[:count], refs[count : 2 * count], refs[2 * count : 3 * count]
    loads = [pltpu.make_async_copy(sources[i], held[i], load_sem.at[i]) for i in range(count)]
    stores = [pltpu.make_async_copy(held[i], targets[i], store_sem.at[i]) for i in range(count)]
    for copy in loads:
        copy.start()
    for load, store in zip(loads, stores):
        load.wait()
        store.start()
    for copy in stores:
        copy.wait()


def train_step(own, attend, merge, up, down, gains, shifts, bias, clips, ways, collective_id):
    levels = ways // 4
    batches, rows, width = own.shape
    wide = up.shape[1]
    share, wide_share = width // ways, wide // ways
    length = rows // clips
    plan = [
        (4, 0, LEVELS_FIRST, wide_share, width // 2, BF, None),
        (4, width // 2, ACROSS_FIRST, wide_share, width // 2, BF, None),
        (3, 0, ACROSS_FIRST, share, wide // 2, BF, None),
        (3, wide // 2, ACROSS_FIRST, share, wide // 2, BF, None),
        (1, 0, ACROSS_FIRST, share, 2 * width, BF, 2),
        (1, 2 * width, ACROSS_FIRST, share, width, BF, 3),
        (2, 0, ACROSS_FIRST, share, width, BF, 2),
        (0, 0, ACROSS_FIRST, 16, 128, F32, None),
    ]
    dma = pltpu.SemaphoreType.DMA
    vmem, anywhere = pl.BlockSpec(memory_space=pltpu.VMEM), pl.BlockSpec(memory_space=pl.ANY)

    def held(cols, dtype=BF):
        return pltpu.VMEM((batches, rows, cols), dtype)

    scratch = [
        pltpu.VMEM((16, 128), F32),
        pltpu.VMEM((ways, 16, 128), F32),
        pltpu.VMEM((ways, share, 3 * width), BF),
        pltpu.VMEM((ways, share, width), BF),
        pltpu.VMEM((ways, share, wide), BF),
        pltpu.VMEM((ways, wide_share, width), BF),
        pltpu.VMEM((8, width), F32),
        pltpu.VMEM((1, wide), F32),
        pltpu.VMEM((8, width), F32),
        pltpu.VMEM((1, wide), F32),
        pltpu.VMEM((2, batches, rows, width), BF),
        held(3 * width),
        pltpu.VMEM((clips * HEADS // 4 * length, batches * 4 * length), BF),
        held(width),
        held(width),
        held(width),
        held(width),
        held(wide),
        held(wide),
        pltpu.VMEM((2, rows, width), BF),
        pltpu.VMEM((rows, width), BF),
        pltpu.VMEM((rows, width), F32),
        pltpu.VMEM((rows, width), F32),
        dma((6, 3)),
        dma((6, 2 * levels + 1)),
        dma((6,)),
        dma(()),
        dma((batches, 2)),
        dma((batches, 2)),
        dma((batches,)),
        pltpu.SemaphoreType.REGULAR((3,)),
        dma((9,)),
    ]
    for _, _, order, chunk_rows, cols, dtype, shared in plan:
        scratch += chunk_scratch(levels, order, chunk_rows, cols, dtype, shared is not None)

    def grad(*shape):
        return jax.ShapeDtypeStruct(shape, F32)

    results = pl.pallas_call(
        functools.partial(relay_kernel, levels, clips, plan),
        out_shape=[
            jax.ShapeDtypeStruct(own.shape, BF),
            grad(2, share),
            grad(6, 1, share),
            grad(share, 3 * width),
            grad(share, width),
            grad(share, wide),
            grad(1, wide_share),
            grad(wide_share, width),
        ],
        in_specs=[anywhere] * 5 + [vmem] * 3,
        out_specs=[anywhere, vmem, vmem, anywhere, anywhere, anywhere, vmem, vmem],
        scratch_shapes=scratch,
        compiler_params=pltpu.CompilerParams(
            collective_id=collective_id, has_side_effects=True, vmem_limit_bytes=62 * 2**20
        ),
    )(own, attend, merge, up, down, gains, shifts, bias)
    return pl.pallas_call(
        settle_kernel,
        out_shape=[jax.ShapeDtypeStruct(result.shape, result.dtype) for result in results],
        in_specs=[anywhere] * len(results),
        out_specs=[anywhere] * len(results),
        scratch_shapes=[pltpu.VMEM(result.shape, result.dtype) for result in results]
        + [dma((len(results),))] * 2,
    )(*results)


def from_behind(block, axis, distance):
    devices = range(lax.axis_size(axis))
    route = [(i - distance, i) for i in devices if i - distance in devices]
    return lax.ppermute(block, axis, route)


def normalize(features, gain_row, offset):
    centred = features - jnp.mean(features, axis=-1, keepdims=True)
    spread = jnp.mean(centred * centred, axis=-1, keepdims=True)
    return centred * lax.rsqrt(spread + epsilon) * gain_row + offset


def gelu_exact(features):
    return jax.nn.gelu(features, approximate=False)


def split_heads(matrix, clip_count):
    return matrix.reshape(clip_count, matrix.shape[0] // clip_count, HEADS, HEAD_DIM)


def layer_forward(hidden, weights, clip_count):
    attend_weight, merge_weight, up_weight, down_weight, gain_rows, offset_rows, up_bias = weights
    gain_rows = gain_rows.astype(jnp.float32)
    offset_rows = offset_rows.astype(jnp.float32)
    row_count, model_width = hidden.shape
    score_scale = HEAD_DIM ** (-0.5)
    normed = normalize(hidden, gain_rows[0], offset_rows[0]).astype(jnp.bfloat16)
    projected = jnp.dot(normed, attend_weight, preferred_element_type=jnp.float32)
    query_heads = split_heads(
        (projected[:, :model_width] + offset_rows[2]).astype(jnp.bfloat16), clip_count
    )
    key_heads = split_heads(
        projected[:, model_width : 2 * model_width].astype(jnp.bfloat16), clip_count
    )
    value_heads = split_heads(
        (projected[:, 2 * model_width :] + offset_rows[3]).astype(jnp.bfloat16), clip_count
    )
    scores = (
        jnp.einsum("clhe,cmhe->chlm", query_heads, key_heads, preferred_element_type=jnp.float32)
        * score_scale
    )
    row_peak = jnp.max(scores, axis=-1, keepdims=True)
    exponent = jnp.exp(scores - row_peak)
    row_total = jnp.sum(exponent, axis=-1, keepdims=True)
    probability = (exponent / row_total).astype(jnp.bfloat16)
    log_total = (row_peak + jnp.log(row_total))[..., 0]
    attended = jnp.einsum(
        "chlm,cmhe->clhe", probability, value_heads, preferred_element_type=jnp.float32
    )
    attended = attended.reshape(row_count, model_width).astype(jnp.bfloat16)
    middle = (
        hidden
        + jnp.dot(attended, merge_weight, preferred_element_type=jnp.float32)
        + offset_rows[4]
    )
    normed_two = normalize(middle, gain_rows[1], offset_rows[1]).astype(jnp.bfloat16)
    raised = jnp.dot(normed_two, up_weight, preferred_element_type=jnp.float32) + up_bias.astype(
        jnp.float32
    )
    activated = gelu_exact(raised).astype(jnp.bfloat16)
    result = (
        middle
        + jnp.dot(activated, down_weight, preferred_element_type=jnp.float32)
        + offset_rows[5]
    )
    saved_state = (
        hidden,
        normed,
        query_heads,
        key_heads,
        value_heads,
        log_total,
        attended,
        middle,
        normed_two,
        raised,
        activated,
    )
    return (result, saved_state)


def layer_backward(out_grad, saved_state, weights, clip_count):
    attend_weight, merge_weight, up_weight, down_weight, gain_rows, offset_rows, up_bias = weights
    gain_rows = gain_rows.astype(jnp.float32)
    offset_rows = offset_rows.astype(jnp.float32)
    (
        hidden,
        normed,
        query_heads,
        key_heads,
        value_heads,
        log_total,
        attended,
        middle,
        normed_two,
        raised,
        activated,
    ) = saved_state
    row_count, model_width = hidden.shape
    score_scale = HEAD_DIM ** (-0.5)
    low_grad = out_grad.astype(jnp.bfloat16)
    down_term = jnp.einsum("tf,td->fd", activated, low_grad, preferred_element_type=jnp.float32)
    last_bias = jnp.sum(out_grad, axis=0)
    act_grad = jnp.einsum("td,fd->tf", low_grad, down_weight, preferred_element_type=jnp.float32)
    raised_grad = jax.vjp(gelu_exact, raised)[1](act_grad)[0]
    up_bias_term = jnp.sum(raised_grad, axis=0)
    raised_low = raised_grad.astype(jnp.bfloat16)
    up_term = jnp.einsum("td,tf->df", normed_two, raised_low, preferred_element_type=jnp.float32)
    normed_two_grad = jnp.einsum(
        "tf,df->td", raised_low, up_weight, preferred_element_type=jnp.float32
    )
    second_back = jax.vjp(normalize, middle, gain_rows[1], offset_rows[1])[1]
    middle_part, gain_two, offset_two = second_back(normed_two_grad)
    middle_grad = out_grad + middle_part
    merge_bias = jnp.sum(middle_grad, axis=0)
    middle_low = middle_grad.astype(jnp.bfloat16)
    merge_term = jnp.einsum("td,te->de", attended, middle_low, preferred_element_type=jnp.float32)
    attended_grad = jnp.einsum(
        "te,de->td", middle_low, merge_weight, preferred_element_type=jnp.float32
    )
    attended_grad = split_heads(attended_grad.astype(jnp.bfloat16), clip_count)
    scores = (
        jnp.einsum("clhe,cmhe->chlm", query_heads, key_heads, preferred_element_type=jnp.float32)
        * score_scale
    )
    probability = jnp.exp(scores - log_total[..., None])
    prob_grad = jnp.einsum(
        "clhe,cmhe->chlm", attended_grad, value_heads, preferred_element_type=jnp.float32
    )
    value_grad = jnp.einsum(
        "chlm,clhe->cmhe",
        probability.astype(jnp.bfloat16),
        attended_grad,
        preferred_element_type=jnp.float32,
    )
    score_grad = probability * (
        prob_grad - jnp.sum(prob_grad * probability, axis=-1, keepdims=True)
    )
    score_grad = score_grad.astype(jnp.bfloat16)
    query_grad = (
        jnp.einsum("chlm,cmhe->clhe", score_grad, key_heads, preferred_element_type=jnp.float32)
        * score_scale
    )
    key_grad = (
        jnp.einsum("chlm,clhe->cmhe", score_grad, query_heads, preferred_element_type=jnp.float32)
        * score_scale
    )
    query_grad = query_grad.reshape(row_count, model_width)
    key_grad = key_grad.reshape(row_count, model_width)
    value_grad = value_grad.reshape(row_count, model_width)
    query_bias = jnp.sum(query_grad, axis=0)
    value_bias = jnp.sum(value_grad, axis=0)
    joined_low = jnp.concatenate([query_grad, key_grad, value_grad], axis=1).astype(jnp.bfloat16)
    attend_term = jnp.einsum("td,te->de", normed, joined_low, preferred_element_type=jnp.float32)
    normed_grad = jnp.einsum(
        "te,de->td", joined_low, attend_weight, preferred_element_type=jnp.float32
    )
    first_back = jax.vjp(normalize, hidden, gain_rows[0], offset_rows[0])[1]
    hidden_part, gain_one, offset_one = first_back(normed_grad)
    hidden_grad = middle_grad + hidden_part
    gain_term = jnp.stack([gain_one, gain_two])
    offset_term = jnp.stack([offset_one, offset_two, query_bias, value_bias, merge_bias, last_bias])
    return (
        hidden_grad,
        (attend_term, merge_term, up_term, down_term, gain_term, offset_term, up_bias_term),
    )


def plain_body(
    section_inputs,
    norm_gains,
    offsets,
    attend_weight,
    merge_weight,
    up_weight,
    up_bias,
    down_weight,
):
    shards = (attend_weight, merge_weight, up_weight, down_weight, norm_gains, offsets, up_bias)
    gathered = (
        lax.all_gather(shards[0], "fsdp", axis=1, tiled=True),
        lax.all_gather(shards[1], "fsdp", axis=1, tiled=True),
        lax.all_gather(shards[2], "fsdp", axis=1, tiled=True),
        lax.all_gather(shards[3], "fsdp", axis=1, tiled=True),
        lax.all_gather(shards[4], "fsdp", axis=2, tiled=True),
        lax.all_gather(shards[5], "fsdp", axis=2, tiled=True),
        lax.all_gather(shards[6], "fsdp", axis=1, tiled=True),
    )
    weights = tuple((tensor[0] for tensor in gathered))
    is_first = lax.axis_index("section") == 0
    own_data = section_inputs[0]
    batches, clip_count, length, model_width = own_data.shape
    row_count = clip_count * length
    own_rows = own_data.reshape(batches, row_count, model_width)
    kept_state = []
    upper_rows = []
    received = jnp.zeros((row_count, model_width), jnp.bfloat16)
    for instant in range(batches + 1):
        entering = jnp.where(is_first, own_rows[min(instant, batches - 1)], received)
        result, saved_state = layer_forward(entering.astype(jnp.float32), weights, clip_count)
        kept_state.append(saved_state)
        rounded = result.astype(jnp.bfloat16)
        if instant >= 1:
            upper_rows.append(rounded)
        if instant < batches:
            received = from_behind(rounded, "section", 1)
    gathered = (
        lax.all_gather(shards[0], "fsdp", axis=1, tiled=True),
        lax.all_gather(shards[1], "fsdp", axis=1, tiled=True),
        lax.all_gather(shards[2], "fsdp", axis=1, tiled=True),
        lax.all_gather(shards[3], "fsdp", axis=1, tiled=True),
        lax.all_gather(shards[4], "fsdp", axis=2, tiled=True),
        lax.all_gather(shards[5], "fsdp", axis=2, tiled=True),
        lax.all_gather(shards[6], "fsdp", axis=1, tiled=True),
    )
    weights = tuple((tensor[0] for tensor in gathered))
    totals = (
        jnp.zeros(weights[0].shape, jnp.float32),
        jnp.zeros(weights[1].shape, jnp.float32),
        jnp.zeros(weights[2].shape, jnp.float32),
        jnp.zeros(weights[3].shape, jnp.float32),
        jnp.zeros(weights[4].shape, jnp.float32),
        jnp.zeros(weights[5].shape, jnp.float32),
        jnp.zeros(weights[6].shape, jnp.float32),
    )
    received_grad = jnp.zeros((row_count, model_width), jnp.bfloat16)
    lower_rows = []
    for instant in range(batches + 1):
        position = batches - 1 - instant
        if position >= 0:
            own_grad = own_rows[position]
        else:
            own_grad = jnp.zeros((row_count, model_width), jnp.bfloat16)
        cotangent = jnp.where(is_first, received_grad, own_grad).astype(jnp.float32)
        hidden_grad, param_terms = layer_backward(
            cotangent, kept_state[batches - instant], weights, clip_count
        )
        totals = jax.tree.map(jnp.add, totals, param_terms)
        rounded = hidden_grad.astype(jnp.bfloat16)
        if instant >= 1:
            lower_rows.append(rounded)
        if instant < batches:
            received_grad = from_behind(rounded, "section", -1)
    ordered_lower = lower_rows[::-1]
    combined = jnp.stack(
        [
            jnp.where(is_first, lower_part, upper_part)
            for lower_part, upper_part in zip(ordered_lower, upper_rows)
        ]
    )
    section_outputs = combined.reshape(1, batches, clip_count, length, model_width)
    reduced = (
        lax.psum_scatter(totals[0][None], "fsdp", scatter_dimension=1, tiled=True),
        lax.psum_scatter(totals[1][None], "fsdp", scatter_dimension=1, tiled=True),
        lax.psum_scatter(totals[2][None], "fsdp", scatter_dimension=1, tiled=True),
        lax.psum_scatter(totals[3][None], "fsdp", scatter_dimension=1, tiled=True),
        lax.psum_scatter(totals[4][None], "fsdp", scatter_dimension=2, tiled=True),
        lax.psum_scatter(totals[5][None], "fsdp", scatter_dimension=2, tiled=True),
        lax.psum_scatter(totals[6][None], "fsdp", scatter_dimension=1, tiled=True),
    )
    return (
        section_outputs,
        reduced[4],
        reduced[5],
        reduced[0],
        reduced[1],
        reduced[2],
        reduced[6],
        reduced[3],
    )


def body(
    section_inputs,
    norm_gains,
    offsets,
    attend_weight,
    merge_weight,
    up_weight,
    up_bias,
    down_weight,
):
    ways = lax.axis_size("fsdp")
    if ways % 4 or attend_weight.shape[1] % 16:
        return plain_body(
            section_inputs,
            norm_gains,
            offsets,
            attend_weight,
            merge_weight,
            up_weight,
            up_bias,
            down_weight,
        )
    batches, clips, length, width = section_inputs.shape[1:]
    own = section_inputs.reshape(batches, clips * length, width)
    results = train_step(
        own,
        attend_weight[0],
        merge_weight[0],
        up_weight[0],
        down_weight[0],
        norm_gains[0],
        offsets[0],
        up_bias,
        clips,
        ways,
        1,
    )
    section_outputs, gains, shifts, attend, merge, up, bias, down = results
    return (
        section_outputs.reshape(section_inputs.shape),
        gains[None],
        shifts.swapaxes(0, 1),
        attend[None],
        merge[None],
        up[None],
        bias,
        down[None],
    )


def solution(mesh):
    return jax.shard_map(
        body,
        mesh=mesh,
        in_specs=(
            P("section", None, "fsdp", None, None),
            P("section", None, "fsdp"),
            P("section", None, "fsdp"),
            P("section", "fsdp", None),
            P("section", "fsdp", None),
            P("section", "fsdp", None),
            P("section", "fsdp"),
            P("section", "fsdp", None),
        ),
        out_specs=(
            P("section", None, "fsdp", None, None),
            P("section", None, "fsdp"),
            P("section", None, "fsdp"),
            P("section", "fsdp", None),
            P("section", "fsdp", None),
            P("section", "fsdp", None),
            P("section", "fsdp"),
            P("section", "fsdp", None),
        ),
        check_vma=False,
    )
```

```python
import functools
import math

import jax
import jax.numpy as jnp
from jax import lax
from jax.experimental import pallas as pl
from jax.experimental.pallas import tpu as pltpu
from jax.sharding import PartitionSpec as P

MESH = pl.DeviceIdType.MESH

HEADS = 12
HEAD_DIM = 64
epsilon = 1e-05
BF, F32 = jnp.bfloat16, jnp.float32
NT = (((1,), (1,)), ((), ()))
TN = (((0,), (0,)), ((), ()))

SIDE, ACROSS, UP, DOWN = range(4)
LEVELS_FIRST, ACROSS_FIRST = 0, 1

class Sends:
    def __init__(self):
        self.items = []

    def start(self, copy, when):
        if when is None:
            copy.start()
        else:
            pl.when(when)(copy.start)
        self.items.append((copy, when))

    def drain(self):
        for copy, when in self.items:
            if when is None:
                copy.wait_send()
            else:
                pl.when(when)(copy.wait_send)


def matmul(left, right, dims=(((1,), (0,)), ((), ()))):
    return lax.dot_general(left, right, dims, preferred_element_type=F32)


def standard(features):
    centred = features - jnp.mean(features, axis=-1, keepdims=True)
    scale = lax.rsqrt(jnp.mean(centred * centred, axis=-1, keepdims=True) + epsilon)
    return centred * scale, scale


def gelu_and_slope(raised):
    share = 0.5 + 0.5 * lax.erf(raised * math.sqrt(0.5))
    bell = jnp.exp(raised * raised * -0.5) * (1.0 / math.sqrt(2.0 * math.pi))
    return raised * share, share + raised * bell


def norm_back(upper, normal, scale):
    shift = jnp.mean(upper, axis=-1, keepdims=True)
    slope = jnp.mean(upper * normal, axis=-1, keepdims=True)
    return (upper - shift - normal * slope) * scale


def column_sum(values):
    return jnp.sum(values, axis=0, keepdims=True)


def pair_parts(matrix):
    lane = lax.broadcasted_iota(jnp.int32, matrix.shape, 1)
    zero = jnp.zeros_like(matrix)
    first = lane < HEAD_DIM
    return jnp.concatenate([jnp.where(first, matrix, zero), jnp.where(first, zero, matrix)], axis=0)


def pair_join(stacked):
    rows = stacked.shape[0] // 2
    lane = lax.broadcasted_iota(jnp.int32, (rows, stacked.shape[1]), 1)
    return jnp.where(lane < HEAD_DIM, stacked[:rows], stacked[rows:])


def halves(scores):
    keys = scores.shape[1] // 2
    return scores[:, :keys], scores[:, keys:]


class Place:
    def __init__(self, levels):
        self.levels = levels
        self.section, self.mine = lax.axis_index("section"), lax.axis_index("fsdp")
        self.level = lax.div(self.mine, 4)
        self.row = lax.rem(lax.div(self.mine, 2), 2)
        self.core = lax.rem(self.mine, 2)
        self.has_up, self.has_down = self.level < levels - 1, self.level > 0
        self.targets = {SIDE: self.mine ^ 1, ACROSS: self.mine ^ 2, UP: self.mine + 4, DOWN: self.mine - 4}

    def block(self, level, row, core):
        return level * 4 + row * 2 + core

    def greet(self):
        barrier = pltpu.get_barrier_semaphore()

        def hello(section, target):
            pl.semaphore_signal(barrier, inc=1, device_id=(section, target), device_id_type=MESH)

        hello(1 - self.section, self.mine)
        hello(self.section, self.targets[SIDE])
        hello(self.section, self.targets[ACROSS])
        pl.when(self.has_down)(lambda: hello(self.section, self.targets[DOWN]))
        pl.when(self.has_up)(lambda: hello(self.section, self.targets[UP]))
        ends = (self.level == 0).astype(jnp.int32) + (self.level == self.levels - 1).astype(jnp.int32)
        pl.semaphore_wait(barrier, 5 - ends)


class Piece:
    def __init__(self, shard, ref, kind, start=0, size=None):
        self.shard, self.ref, self.plain = shard, ref, kind == "level"
        self.rows = None if size is None else pl.ds(start, size)

    def block(self, index):
        return self.ref.at[index] if self.rows is None else self.ref.at[index, self.rows]

    def span(self, count):
        return self.block(pl.ds(0, count))


class Gather:
    def __init__(self, place, pieces, send_sem, recv_sem, local_sem):
        self.place, self.pieces = place, pieces
        self.send_sem, self.recv_sem, self.local_sem = send_sem, recv_sem, local_sem
        self.side = 2 * place.levels

    def copy(self, source, target, out_sem, in_sem, way):
        return pltpu.make_async_remote_copy(
            src_ref=source,
            dst_ref=target,
            send_sem=out_sem,
            recv_sem=in_sem,
            device_id=(self.place.section, self.place.targets[way]),
            device_id_type=MESH,
        )

    def send(self, piece, level, row, way, own=False, when=None):
        held = self.pieces[piece]
        target = held.block(self.place.block(level, row, self.place.core))
        kind = {SIDE: 0, ACROSS: 1, UP: 2, DOWN: 2}[way]
        copy = self.copy(
            held.shard if own else target,
            target,
            self.send_sem.at[piece, kind],
            self.recv_sem.at[piece, self.side if way == SIDE else level * 2 + row],
            way,
        )
        if when is None:
            copy.start()
        else:
            pl.when(when)(copy.start)

    def arrived(self, piece, level, row, when=None):
        target = self.pieces[piece].block(self.place.block(level, row, self.place.core))
        index = level * 2 + row
        copy = self.copy(target, target, self.send_sem.at[piece, 0], self.recv_sem.at[piece, index], SIDE)
        if when is None:
            copy.wait_recv()
        else:
            pl.when(when)(copy.wait_recv)

    def local(self, piece):
        held = self.pieces[piece]
        return pltpu.make_async_copy(held.shard, held.block(self.place.mine), self.local_sem.at[piece])

    def start(self, piece):
        place = self.place
        self.send(piece, place.level, place.row, ACROSS, own=True)
        self.send(piece, place.level, place.row, UP, own=True, when=place.has_up)
        self.send(piece, place.level, place.row, DOWN, own=True, when=place.has_down)
        self.send(piece, place.level, place.row, SIDE, own=True)
        self.local(piece).start()

    def first_across(self, piece):
        place = self.place
        level, row = place.level, 1 - place.row
        self.arrived(piece, level, row)
        self.send(piece, level, row, UP, when=place.has_up)
        self.send(piece, level, row, DOWN, when=place.has_down)
        self.send(piece, level, row, SIDE)

    def from_levels(self, piece, distance):
        place = self.place
        plain = self.pieces[piece].plain
        for row in (place.row,) if plain else (place.row, 1 - place.row):
            for sign in (-1, 1):
                other = place.level + sign * distance
                here = other >= 0 if sign < 0 else other < place.levels
                onward = place.has_up if sign < 0 else place.has_down
                self.arrived(piece, other, row, here)
                if distance < place.levels - 1:
                    way = UP if sign < 0 else DOWN
                    self.send(piece, other, row, way, when=jnp.logical_and(here, onward))
                if plain:
                    self.send(piece, other, row, ACROSS, when=here)
                self.send(piece, other, row, SIDE, when=here)

    def from_across(self, piece, distance):
        place = self.place
        if not self.pieces[piece].plain:
            return
        for sign in (-1, 1) if distance else (1,):
            other = place.level + sign * distance
            here = None
            if distance:
                here = other >= 0 if sign < 0 else other < place.levels
            self.arrived(piece, other, 1 - place.row, here)
            self.send(piece, other, 1 - place.row, SIDE, when=here)

    def from_side(self, piece):
        self.local(piece).wait()
        span = self.pieces[piece].span(self.side)
        self.copy(span, span, self.send_sem.at[piece, 0], self.recv_sem.at[piece, self.side], SIDE).wait_recv()

    def drain(self, piece):
        place, held = self.place, self.pieces[piece]

        def sent(count, kind):
            span = held.span(count)
            return self.copy(span, span, self.send_sem.at[piece, kind], self.recv_sem.at[piece, 0], SIDE)

        rows = 1 if held.plain else 2
        sent(self.side, 0).wait_send()
        sent(place.levels if held.plain else 1, 1).wait_send()
        inner = jnp.logical_and(place.has_up, place.has_down)
        pl.when(inner)(sent(rows * (place.levels + 1), 2).wait_send)
        pl.when(jnp.logical_not(inner))(sent(rows, 2).wait_send)


class Chunk:
    def __init__(self, place, order, part, start, refs, sems):
        self.place, self.order, self.levels = place, order, place.levels
        self.whole, self.start = part, start
        self.from_side, self.from_across, self.from_chain = refs
        self.cols = self.from_side.shape[2]
        (
            self.side_out,
            self.side_in,
            self.across_out,
            self.across_in,
            self.chain_out,
            self.chain_in,
        ) = sems

    def part(self, block):
        return self.whole.at[block, :, pl.ds(self.start, self.cols)]

    def copy(self, block, target, out_sem, in_sem, way):
        return pltpu.make_async_remote_copy(
            src_ref=self.part(block),
            dst_ref=target,
            send_sem=out_sem,
            recv_sem=in_sem,
            device_id=(self.place.section, self.place.targets[way]),
            device_id_type=MESH,
        )

    def side(self, pair):
        block = pair * 2 + 1 - self.place.core
        return self.copy(
            block, self.from_side.at[pair], self.side_out, self.side_in.at[pair], SIDE
        )

    def across(self, level, slot):
        block = self.place.block(level, 1 - self.place.row, self.place.core)
        return self.copy(
            block,
            self.from_across.at[slot],
            self.across_out,
            self.across_in.at[slot],
            ACROSS,
        )

    def below_index(self, target, level):
        return target - level

    def above_index(self, target):
        return self.levels - target

    def up(self, row, slot, target):
        index = self.below_index(target, self.place.level + 1)
        return self.copy(
            self.place.block(target, row, self.place.core),
            self.from_chain.at[slot, index],
            self.chain_out.at[slot],
            self.chain_in.at[slot, index],
            UP,
        )

    def down(self, row, slot, target):
        index = self.above_index(target)
        return self.copy(
            self.place.block(target, row, self.place.core),
            self.from_chain.at[slot, index],
            self.chain_out.at[slot],
            self.chain_in.at[slot, index],
            DOWN,
        )

    def arrived(self, slot, index):
        target = self.from_chain.at[slot, index]
        pltpu.make_async_remote_copy(
            src_ref=target,
            dst_ref=target,
            send_sem=self.side_out,
            recv_sem=self.chain_in.at[slot, index],
            device_id=(self.place.section, self.place.targets[SIDE]),
            device_id_type=MESH,
        ).wait_recv()

    def add(self, block, term):
        part = self.part(block)
        part[...] = part[...] + term

    def send_side(self):
        @pl.loop(0, self.levels * 2)
        def _(pair):
            self.side(pair).start()

    def join_pair(self, level, row):
        pair = level * 2 + row
        self.side(pair).wait_recv()
        self.add(pair * 2 + self.place.core, self.from_side[pair])

    def level_at(self, index):
        return jnp.where(self.place.level < self.levels // 2, self.levels - 1 - index, index)

    def join_side(self):
        place = self.place
        for other in (True, False):
            row = 1 - place.row if other else place.row

            @pl.loop(0, self.levels)
            def _(index):
                level = self.level_at(index)
                self.join_pair(level, row)
                if other and self.order == ACROSS_FIRST:
                    self.across(level, level).start()

    def chain_open(self, row, slot, target):
        level, last = self.place.level, self.levels - 1
        pl.when(jnp.logical_and(level == 0, target > 0))(lambda: self.up(row, slot, target).start())
        pl.when(jnp.logical_and(level == last, target < last))(
            lambda: self.down(row, slot, target).start()
        )

    def join_across(self):
        place = self.place

        @pl.loop(0, self.levels)
        def _(index):
            level = self.level_at(index)
            self.across(level, level).wait_recv()
            self.add(place.block(level, place.row, place.core), self.from_across[level])
            self.chain_open(place.row, 0, level)

    def rows(self):
        row = self.place.row
        return ((0, row), (1, 1 - row)) if self.order == LEVELS_FIRST else ((0, row),)

    def chain_pass(self, distance):
        place, last = self.place, self.levels - 1
        for slot, row in self.rows():
            for target in range(last, distance, -1):

                @pl.when(place.level == distance)
                def _():
                    index = self.below_index(target, place.level)
                    self.arrived(slot, index)
                    self.add(place.block(target, row, place.core), self.from_chain[slot, index])
                    self.up(row, slot, target).start()

            for target in range(last - distance):

                @pl.when(place.level == last - distance)
                def _():
                    index = self.above_index(target)
                    self.arrived(slot, index)
                    self.add(place.block(target, row, place.core), self.from_chain[slot, index])
                    self.down(row, slot, target).start()

    def chain_end(self, out):
        place, last = self.place, self.levels - 1
        for slot, row in reversed(self.rows()):
            block = place.block(place.level, row, place.core)

            @pl.when(place.level > 0)
            def _():
                index = self.below_index(place.level, place.level)
                self.arrived(slot, index)
                self.add(block, self.from_chain[slot, index])

            @pl.when(place.level < last)
            def _():
                index = self.above_index(place.level)
                self.arrived(slot, index)
                self.add(block, self.from_chain[slot, index])

            if slot == 1:
                self.across(place.level, 0).start()
        if self.order == ACROSS_FIRST:
            out(self.part(place.mine)[...].astype(F32))

    def finish(self, out):
        if self.order == LEVELS_FIRST:
            self.across(self.place.level, 0).wait_recv()
            out(self.part(self.place.mine)[...].astype(F32) + self.from_across[0].astype(F32))

    def drain(self):
        def sent(span, out_sem):
            pltpu.make_async_remote_copy(
                src_ref=span,
                dst_ref=span,
                send_sem=out_sem,
                recv_sem=self.side_in.at[0],
                device_id=(self.place.section, self.place.targets[SIDE]),
                device_id_type=MESH,
            ).wait_send()

        sent(self.from_side, self.side_out)
        sent(self.from_across, self.across_out)
        for slot, _ in self.rows():
            sent(self.from_chain.at[slot, pl.ds(0, self.levels - 1)], self.chain_out.at[slot])


def chunk_scratch(levels, order, rows, cols, dtype, shared):
    block = (rows, cols)
    slots = 2 if order == LEVELS_FIRST else 1
    crossing = 1 if order == LEVELS_FIRST else levels
    dma = pltpu.SemaphoreType.DMA
    from_side = [] if shared else [pltpu.VMEM((levels * 2,) + block, dtype)]
    return from_side + [
        pltpu.VMEM((crossing,) + block, dtype),
        pltpu.VMEM((slots, levels + 1) + block, dtype),
        dma(()),
        dma((levels * 2,)),
        dma(()),
        dma((crossing,)),
        dma((slots,)),
        dma((slots, levels + 1)),
    ]


CHUNK_REFS = 8
STEP = 512


def pad_lanes(rows, lanes=128):
    missing = lanes - rows.shape[1]
    if not missing:
        return rows
    return jnp.concatenate([rows, jnp.zeros((rows.shape[0], missing), rows.dtype)], axis=1)


def tile_of(rows):
    missing = 8 - rows.shape[0]
    if not missing:
        return rows
    return jnp.concatenate([rows, jnp.zeros((missing, rows.shape[1]), rows.dtype)], axis=0)


def fold(line):
    pieces = [pad_lanes(line[:, at : at + 128]) for at in range(0, line.shape[1], 128)]
    return tile_of(jnp.concatenate(pieces, axis=0))


def unfold(rows, count):
    pieces = []
    for index in range(-(-count // 128)):
        pieces.append(rows[index : index + 1, : min(128, count - index * 128)])
    return jnp.concatenate(pieces, axis=1)


FOUR_LEVEL_STEPS = (
    (0, 1, 1), (4, 2, 0), (2, 2, 0), (4, 1, 1), (0, 1, 2), (2, 1, 1),
    (5, 0, 0), (1, 1, 1), (2, 1, 2), (0, 2, 0), (3, 1, 1), (4, 2, 1),
    (1, 1, 2), (3, 1, 2), (0, 1, 3), (0, 2, 1), (1, 1, 3), (5, 1, 1),
    (3, 2, 0), (1, 2, 0), (1, 2, 1), (3, 1, 3), (4, 1, 2), (0, 2, 2),
    (5, 1, 2), (3, 2, 1), (2, 1, 3), (4, 1, 3), (1, 2, 2), (0, 2, 3),
    (2, 2, 1), (2, 2, 2), (3, 2, 2), (1, 2, 3), (2, 2, 3), (3, 2, 3),
    (4, 2, 2), (5, 1, 3), (4, 2, 3),
)


def gather_steps(levels, count):
    if levels == 4 and count == 6:
        return FOUR_LEVEL_STEPS
    steps = [(count - 1, 0, 0)]
    for distance in range(1, levels):
        for piece in range(count):
            steps += [(piece, 1, distance), (piece, 2, distance - 1)]
    return steps + [(piece, 2, levels - 1) for piece in range(count)]


def relay_kernel(levels, clips, plan, *refs):
    own, attend_shard, merge_shard, up_shard, down_shard, gain_shard, shift_shard, bias_shard = refs[:8]
    out, gain_out, shift_out, attend_out, merge_out, up_out, bias_out, down_out = refs[8:16]
    (
        packed,
        vector_blocks,
        attend_blocks,
        merge_blocks,
        up_blocks,
        down_blocks,
        vectors,
        bias,
        vector_sum,
        bias_sum,
        entry,
        projected,
        probability,
        normed,
        attended,
        middle,
        normed_two,
        activated,
        slope,
        leaving,
        low_temp,
        temp,
        sum_temp,
        gather_send,
        gather_recv,
        gather_local,
        load_sem,
        send_sem,
        recv_sem,
        out_sem,
        free_sem,
        store_sem,
    ) = refs[16:48]
    chunk_refs = list(refs[48:])
    place = Place(levels)
    section, mine = place.section, place.mine
    batches, rows, width = own.shape
    wide = up_shard.shape[1]
    ways = levels * 4
    share, wide_share = width // ways, wide // ways
    length = rows // clips
    pairs = HEADS // 2
    total = batches * rows

    load_own = pltpu.make_async_copy(own, entry.at[0], load_sem)
    load_own.start()
    packed[0:8] = pad_lanes(
        jnp.concatenate([gain_shard[...], shift_shard[...]], axis=0).astype(F32)
    )
    packed[8:16] = fold(bias_shard[...].astype(F32))
    place.greet()

    half_share = wide_share // 2
    pieces = [
        Piece(packed, vector_blocks, "level"),
        Piece(attend_shard, attend_blocks, "level"),
        Piece(merge_shard, merge_blocks, "level"),
        Piece(up_shard, up_blocks, "level"),
        Piece(down_shard.at[pl.ds(0, half_share)], down_blocks, "level", 0, half_share),
        Piece(down_shard.at[pl.ds(half_share, half_share)], down_blocks, "across", half_share, half_share),
    ]
    gather = Gather(place, pieces, gather_send, gather_recv, gather_local)
    def flat(blocks):
        return blocks.reshape(-1, blocks.shape[-1])

    half = rows // 2 if clips % 2 == 0 else rows
    portions = rows // half

    def relay_part(batch, portion, slot=0):
        here = pl.ds(portion * half, half)
        return pltpu.make_async_remote_copy(
            src_ref=leaving.at[slot, here],
            dst_ref=entry.at[1, batch, here],
            send_sem=send_sem.at[batch, portion],
            recv_sem=recv_sem.at[batch, portion],
            device_id=(1 - section, mine),
            device_id_type=MESH,
        )

    class Relay:
        def __init__(self, batch, slot=0):
            self.copies = [relay_part(batch, portion, slot) for portion in range(portions)]

        def start(self):
            for copy in self.copies:
                copy.start()

        def wait_send(self):
            for copy in self.copies:
                copy.wait_send()

        def wait_recv(self):
            for copy in self.copies:
                copy.wait_recv()

    relay = Relay

    def keep(batch, slot=0):
        return pltpu.make_async_copy(leaving.at[slot], out.at[batch], out_sem.at[batch])

    vector_sum[...] = jnp.zeros_like(vector_sum)
    bias_sum[...] = jnp.zeros_like(bias_sum)
    fed, back = section, 1 - section

    def row(index):
        return vectors[index : index + 1, :]

    def chances(batch, start, pair):
        at = pl.multiple_of(batch * 4 * length + (pair % 2) * 2 * length, 128)
        first = start * (pairs // 2) + (pair // 2) * length
        return probability.at[pl.ds(first, length), pl.ds(at, 2 * length)]

    def attend_part(batch, start, size):
        here = pl.ds(start, size)
        normal, _ = standard(entry[fed, batch, here].astype(F32))
        normed[batch, here] = (normal * row(0) + row(2)).astype(BF)
        for part, shift in ((0, 4), (1, None), (2, 5)):
            at = slice(part * width, (part + 1) * width)
            value = matmul(normed[batch, here], flat(attend_blocks[:, :, at]))
            if shift is not None:
                value = value + row(shift)
            projected[batch, here, at] = value.astype(BF)
        for clip in range(size // length):
            span = pl.ds(start + clip * length, length)
            for pair in range(pairs):
                lanes = [slice(p * width + pair * 128, p * width + pair * 128 + 128) for p in range(3)]
                query = projected[batch, span, lanes[0]] * jnp.asarray(HEAD_DIM**-0.5, BF)
                key = pair_parts(projected[batch, span, lanes[1]])
                scores = matmul(query, key, NT)
                parts = []
                for half in halves(scores):
                    exponent = jnp.exp(half - jnp.max(half, axis=-1, keepdims=True))
                    parts.append(exponent * (1.0 / jnp.sum(exponent, axis=-1, keepdims=True)))
                weight = jnp.concatenate(parts, axis=1).astype(BF)
                chances(batch, start + clip * length, pair)[...] = weight
                value = pair_parts(projected[batch, span, lanes[2]])
                attended[batch, span, lanes[0]] = matmul(weight, value).astype(BF)
        joined = matmul(attended[batch, here], flat(merge_blocks[...])) + row(6)
        temp[here] = entry[fed, batch, here].astype(F32) + joined
        middle[batch, here] = temp[here].astype(BF)
        normal, _ = standard(temp[here])
        normed_two[batch, here] = (normal * row(1) + row(3)).astype(BF)

    def rise_part(batch, start, size):
        here = pl.ds(start, size)
        tile = 256
        for first in range(0, wide, tile):
            at = slice(first, first + tile)
            value, rate = gelu_and_slope(
                matmul(normed_two[batch, here], flat(up_blocks[:, :, at])) + bias[:, at]
            )
            activated[batch, here, at] = value.astype(BF)
            slope[batch, here, at] = rate.astype(BF)

    def fall_part(batch, start, size, slot):
        here = pl.ds(start, size)
        result = temp[here] + matmul(activated[batch, here], flat(down_blocks[...])) + row(7)
        leaving[slot, here] = result.astype(BF)

    def forward(batch, start, size, slot):
        attend_part(batch, start, size)
        rise_part(batch, start, size)
        fall_part(batch, start, size, slot)

    def backward(batch, start, size, slot):
        here = pl.ds(start, size)
        low = entry[back, batch, here]
        vector_sum[7:8] += column_sum(low.astype(F32))
        blocks = 4
        for block in range(0, ways, blocks):
            at = slice(block * wide_share, (block + blocks) * wide_share)
            rate = matmul(low, flat(down_blocks[block : block + blocks]), NT)
            rate = rate * slope[batch, here, at].astype(F32)
            bias_sum[:, at] += column_sum(rate)
            slope[batch, here, at] = rate.astype(BF)
        temp[here] = matmul(slope[batch, here], flat(up_blocks[...]), NT)
        normal, scale = standard(middle[batch, here].astype(F32))
        grad = temp[here]
        vector_sum[1:2] += column_sum(grad * normal)
        vector_sum[3:4] += column_sum(grad)
        grad = entry[back, batch, here].astype(F32) + norm_back(grad * row(1), normal, scale)
        sum_temp[here] = grad
        vector_sum[6:7] += column_sum(grad)
        middle[batch, here] = grad.astype(BF)
        low_temp[here] = matmul(middle[batch, here], flat(merge_blocks[...]), NT).astype(BF)
        for clip in range(size // length):
            span = pl.ds(start + clip * length, length)
            for pair in range(pairs):
                lanes = [slice(p * width + pair * 128, p * width + pair * 128 + 128) for p in range(3)]
                query = projected[batch, span, lanes[0]]
                key = pair_parts(projected[batch, span, lanes[1]])
                value = pair_parts(projected[batch, span, lanes[2]])
                upper = low_temp[span, lanes[0]]
                weight = chances(batch, start + clip * length, pair)[...]
                rise = matmul(upper, value, NT)
                value_grad = pair_join(matmul(weight, upper, TN))
                parts = []
                for part, heavy in zip(halves(rise), halves(weight)):
                    heavy = heavy.astype(F32)
                    mean = jnp.sum(part * heavy, axis=-1, keepdims=True)
                    parts.append(heavy * (part - mean) * HEAD_DIM**-0.5)
                change = jnp.concatenate(parts, axis=1).astype(BF)
                query_grad = matmul(change, key)
                key_grad = pair_join(matmul(change, query, TN))
                vector_sum[4:5, lanes[0]] += column_sum(query_grad)
                vector_sum[5:6, lanes[0]] += column_sum(value_grad)
                for at, piece in zip(lanes, (query_grad, key_grad, value_grad)):
                    projected[batch, span, at] = piece.astype(BF)
        temp[here] = matmul(projected[batch, here], flat(attend_blocks[...]), NT)
        normal, scale = standard(entry[fed, batch, here].astype(F32))
        grad = temp[here]
        vector_sum[0:1] += column_sum(grad * normal)
        vector_sum[2:3] += column_sum(grad)
        leaving[slot, here] = (sum_temp[here] + norm_back(grad * row(0), normal, scale)).astype(BF)

    count = len(pieces)
    for piece in range(count):
        gather.start(piece)
    for piece, what, distance in gather_steps(levels, count):
        if what == 0:
            gather.first_across(piece)
        elif what == 1:
            gather.from_levels(piece, distance)
        else:
            gather.from_across(piece, distance)
    for piece in range(count):
        gather.from_side(piece)
    vectors[...] = jnp.concatenate([vector_blocks[block, 0:8, 0:share] for block in range(ways)], axis=1)
    bias[...] = jnp.concatenate(
        [unfold(vector_blocks[block, 8:16], wide_share) for block in range(ways)], axis=1
    )
    load_own.wait()
    for piece in range(count):
        gather.drain(piece)

    chunks = []
    part_refs = [vector_blocks, attend_blocks, merge_blocks, up_blocks, down_blocks]
    for which, start, order, _, cols, _, shared in plan:
        if shared is None:
            from_side = chunk_refs.pop(0)
        else:
            from_side = chunks[shared].from_side.at[:, :, pl.ds(0, cols)]
        held, chunk_refs = chunk_refs[:CHUNK_REFS], chunk_refs[CHUNK_REFS:]
        chunks.append(Chunk(place, order, part_refs[which], start, [from_side] + held[:2], held[2:]))
    down_a, down_b, up_a, up_b, attend_a, attend_b, merge, vector = chunks

    def down_gradient():
        def pair_at(index):
            late = lax.div(index, levels)
            level = down_a.level_at(lax.rem(index, levels))
            return level, jnp.where(late == 0, 1 - place.row, place.row), late == 0

        def multiply(index):
            level, row, _ = pair_at(index)
            pair = level * 2 + row
            at = pl.ds(pl.multiple_of(pair * 2 * wide_share, 128), 2 * wide_share)
            tile = flat(activated[:, :, at])
            product = matmul(tile, flat(entry[back]), TN).astype(BF)
            for core in range(2):
                down_blocks[pair * 2 + core] = product[core * wide_share : (core + 1) * wide_share]
            for chunk in (down_b, down_a):
                chunk.side(pair).start()

        def join(index):
            level, row, early = pair_at(index)
            down_b.join_pair(level, row)
            pl.when(early)(down_b.across(level, level).start)
            down_a.join_pair(level, row)
            down_a.chain_open(row, jnp.where(early, 1, 0), level)

        multiply(jnp.int32(0))

        @pl.loop(1, 2 * levels)
        def _(index):
            multiply(index)
            join(index - 1)

        join(jnp.int32(2 * levels - 1))

    stores = []

    def store(target, chunk, through=None, first=0):
        def put(value):
            if through is None:
                target[:, pl.ds(chunk.start, chunk.cols)] = value
                return
            done = 0
            while done < chunk.cols:
                column = chunk.start + done
                size = min(width - column % width, chunk.cols - done)
                at = (pl.ds(first + column // width * share, share), pl.ds(column % width, size))
                through[at] = value[:, done : done + size]
                copy = pltpu.make_async_copy(
                    through.at[at], target.at[:, pl.ds(column, size)], store_sem.at[len(stores)]
                )
                copy.start()
                stores.append(copy)
                done += size

        return put

    def turn(source, place_at):
        target = probability.at[pl.ds(0, width), pl.ds(place_at * total, total)]
        target[...] = flat(source[...]).T
        return target

    def columns(left, source, chunk, credit=None):
        step = STEP if chunk.cols % STEP == 0 else chunk.cols

        @pl.loop(0, chunk.cols // step)
        def _(index):
            at = pl.multiple_of(chunk.start + index * step, 128)
            product = matmul(left[...], flat(source[:, :, pl.ds(at, step)]))
            chunk.whole[:, :, pl.ds(at, step)] = product.astype(BF).reshape(ways, width // ways, step)

        if credit is not None:
            pl.semaphore_wait(free_sem.at[credit], 1)
        chunk.send_side()

    def release(index):
        pl.semaphore_signal(
            free_sem.at[index], inc=1, device_id=(section, place.targets[SIDE]), device_id_type=MESH
        )

    @pl.loop(0, portions)
    def _(portion):
        pl.when(section == 1)(relay_part(0, portion).wait_recv)
        forward(0, pl.multiple_of(portion * half, length), half, 0)
        pl.when(section == 0)(relay_part(0, portion).start)

    pl.when(section == 1)(keep(0).start)

    @pl.loop(1, 2 * batches)
    def _(step):
        is_forward = jnp.where(section == 0, step < batches, lax.rem(step, 2) == 0)
        batch = jnp.where(section == 0, lax.rem(step, batches), lax.div(step, 2))
        slot = jnp.where(section == 0, lax.rem(batch, 2), jnp.where(is_forward, 0, 1))

        def when(*conditions):
            return pl.when(functools.reduce(jnp.logical_and, conditions))

        @pl.when(is_forward)
        def _():
            pl.when(section == 1)(lambda: relay(batch).wait_recv())
            when(section == 0, batch >= 2)(lambda: relay(batch - 2).wait_send())
            pl.when(section == 1)(lambda: keep(batch - 1).wait())
            forward(batch, 0, rows, slot)
            pl.when(section == 0)(lambda: relay(batch, slot).start())
            pl.when(section == 1)(lambda: keep(batch, slot).start())

        @pl.when(jnp.logical_not(is_forward))
        def _():
            pl.when(section == 0)(lambda: relay(batch).wait_recv())
            when(section == 0, batch < 2)(lambda: relay(batch + batches - 2).wait_send())
            when(section == 0, batch >= 2)(lambda: keep(batch - 2).wait())
            when(section == 1, batch >= 1)(lambda: relay(batch - 1).wait_send())
            backward(batch, 0, rows, slot)
            pl.when(section == 1)(lambda: relay(batch, slot).start())
            pl.when(section == 0)(lambda: keep(batch, slot).start())

    down_gradient()

    for block in range(ways):
        vector_blocks[block, 0:8] = pad_lanes(vector_sum[:, block * share : (block + 1) * share])
        vector_blocks[block, 8:16] = fold(bias_sum[:, block * wide_share : (block + 1) * wide_share])
    vector.send_side()

    def store_vectors(value):
        gain_out[...] = value[0:2, :share]
        for index in range(6):
            shift_out[index] = value[2 + index : 3 + index, :share]
        bias_out[...] = unfold(value[8:16], wide_share)

    turned_up = turn(normed_two, 0)
    columns(turned_up, slope, up_a)
    up_a.join_side()
    release(0)
    columns(turned_up, slope, up_b)
    down_a.chain_pass(1)
    vector.join_side()
    down_b.join_across()
    turned_attend = turn(normed, 1)
    columns(turned_attend, projected, attend_a, 0)
    up_b.join_side()
    release(1)
    up_a.join_across()
    vector.join_across()
    down_a.chain_pass(2)
    down_b.chain_pass(1)
    attend_a.join_side()
    release(2)
    columns(turned_attend, projected, attend_b, 1)
    turned_merge = turn(attended, 0)
    columns(turned_merge, middle, merge, 2)
    attend_b.join_side()
    up_a.chain_pass(1)
    merge.join_side()
    up_b.join_across()
    up_a.chain_pass(2)
    down_b.chain_pass(2)
    vector.chain_pass(1)
    down_a.chain_end(None)
    up_b.chain_pass(1)
    up_b.chain_pass(2)
    vector.chain_pass(2)
    attend_a.join_across()
    attend_a.chain_pass(1)
    attend_b.join_across()
    up_b.chain_end(store(up_out, up_b, temp, 0))
    attend_b.chain_pass(1)
    down_b.chain_end(store(down_out, down_b))
    vector.chain_end(store_vectors)
    attend_a.chain_pass(2)
    attend_b.chain_pass(2)
    merge.join_across()
    merge.chain_pass(1)
    up_a.chain_end(store(up_out, up_a, temp, 0))
    attend_a.chain_end(store(attend_out, attend_a, sum_temp, 0))
    merge.chain_pass(2)
    down_a.finish(store(down_out, down_a))
    attend_b.chain_end(store(attend_out, attend_b, sum_temp, 0))
    merge.chain_end(store(merge_out, merge, sum_temp, 3 * share))
    for chunk in chunks:
        chunk.drain()

    for copy in stores:
        copy.wait()

    @pl.when(section == 0)
    def _():
        keep(batches - 2).wait()
        keep(batches - 1).wait()

    @pl.when(section == 1)
    def _():
        keep(batches - 1).wait()
        relay(batches - 1).wait_send()


def settle_kernel(*refs):
    count = (len(refs) - 2) // 3
    load_sem, store_sem = refs[-2:]
    sources, targets, held = refs[:count], refs[count : 2 * count], refs[2 * count : 3 * count]
    loads = [pltpu.make_async_copy(sources[i], held[i], load_sem.at[i]) for i in range(count)]
    stores = [pltpu.make_async_copy(held[i], targets[i], store_sem.at[i]) for i in range(count)]
    for copy in loads:
        copy.start()
    for load, store in zip(loads, stores):
        load.wait()
        store.start()
    for copy in stores:
        copy.wait()


def train_step(own, attend, merge, up, down, gains, shifts, bias, clips, ways, collective_id):
    levels = ways // 4
    batches, rows, width = own.shape
    wide = up.shape[1]
    share, wide_share = width // ways, wide // ways
    length = rows // clips
    plan = [
        (4, 0, LEVELS_FIRST, wide_share, width // 2, BF, None),
        (4, width // 2, ACROSS_FIRST, wide_share, width // 2, BF, None),
        (3, 0, ACROSS_FIRST, share, wide // 2, BF, None),
        (3, wide // 2, ACROSS_FIRST, share, wide // 2, BF, None),
        (1, 0, ACROSS_FIRST, share, 2 * width, BF, 2),
        (1, 2 * width, ACROSS_FIRST, share, width, BF, 3),
        (2, 0, ACROSS_FIRST, share, width, BF, 2),
        (0, 0, ACROSS_FIRST, 16, 128, F32, None),
    ]
    dma = pltpu.SemaphoreType.DMA
    vmem, anywhere = pl.BlockSpec(memory_space=pltpu.VMEM), pl.BlockSpec(memory_space=pl.ANY)

    def held(cols, dtype=BF):
        return pltpu.VMEM((batches, rows, cols), dtype)

    scratch = [
        pltpu.VMEM((16, 128), F32),
        pltpu.VMEM((ways, 16, 128), F32),
        pltpu.VMEM((ways, share, 3 * width), BF),
        pltpu.VMEM((ways, share, width), BF),
        pltpu.VMEM((ways, share, wide), BF),
        pltpu.VMEM((ways, wide_share, width), BF),
        pltpu.VMEM((8, width), F32),
        pltpu.VMEM((1, wide), F32),
        pltpu.VMEM((8, width), F32),
        pltpu.VMEM((1, wide), F32),
        pltpu.VMEM((2, batches, rows, width), BF),
        held(3 * width),
        pltpu.VMEM((clips * HEADS // 4 * length, batches * 4 * length), BF),
        held(width),
        held(width),
        held(width),
        held(width),
        held(wide),
        held(wide),
        pltpu.VMEM((2, rows, width), BF),
        pltpu.VMEM((rows, width), BF),
        pltpu.VMEM((rows, width), F32),
        pltpu.VMEM((rows, width), F32),
        dma((6, 3)),
        dma((6, 2 * levels + 1)),
        dma((6,)),
        dma(()),
        dma((batches, 2)),
        dma((batches, 2)),
        dma((batches,)),
        pltpu.SemaphoreType.REGULAR((3,)),
        dma((9,)),
    ]
    for _, _, order, chunk_rows, cols, dtype, shared in plan:
        scratch += chunk_scratch(levels, order, chunk_rows, cols, dtype, shared is not None)

    def grad(*shape):
        return jax.ShapeDtypeStruct(shape, F32)

    results = pl.pallas_call(
        functools.partial(relay_kernel, levels, clips, plan),
        out_shape=[
            jax.ShapeDtypeStruct(own.shape, BF),
            grad(2, share),
            grad(6, 1, share),
            grad(share, 3 * width),
            grad(share, width),
            grad(share, wide),
            grad(1, wide_share),
            grad(wide_share, width),
        ],
        in_specs=[anywhere] * 5 + [vmem] * 3,
        out_specs=[anywhere, vmem, vmem, anywhere, anywhere, anywhere, vmem, vmem],
        scratch_shapes=scratch,
        compiler_params=pltpu.CompilerParams(
            collective_id=collective_id, has_side_effects=True, vmem_limit_bytes=62 * 2**20
        ),
    )(own, attend, merge, up, down, gains, shifts, bias)
    return pl.pallas_call(
        settle_kernel,
        out_shape=[jax.ShapeDtypeStruct(result.shape, result.dtype) for result in results],
        in_specs=[anywhere] * len(results),
        out_specs=[anywhere] * len(results),
        scratch_shapes=[pltpu.VMEM(result.shape, result.dtype) for result in results]
        + [dma((len(results),))] * 2,
    )(*results)


def from_behind(block, axis, distance):
    devices = range(lax.axis_size(axis))
    route = [(i - distance, i) for i in devices if i - distance in devices]
    return lax.ppermute(block, axis, route)


def normalize(features, gain_row, offset):
    centred = features - jnp.mean(features, axis=-1, keepdims=True)
    spread = jnp.mean(centred * centred, axis=-1, keepdims=True)
    return centred * lax.rsqrt(spread + epsilon) * gain_row + offset


def gelu_exact(features):
    return jax.nn.gelu(features, approximate=False)


def split_heads(matrix, clip_count):
    return matrix.reshape(clip_count, matrix.shape[0] // clip_count, HEADS, HEAD_DIM)


def layer_forward(hidden, weights, clip_count):
    attend_weight, merge_weight, up_weight, down_weight, gain_rows, offset_rows, up_bias = weights
    gain_rows = gain_rows.astype(jnp.float32)
    offset_rows = offset_rows.astype(jnp.float32)
    row_count, model_width = hidden.shape
    score_scale = HEAD_DIM ** (-0.5)
    normed = normalize(hidden, gain_rows[0], offset_rows[0]).astype(jnp.bfloat16)
    projected = jnp.dot(normed, attend_weight, preferred_element_type=jnp.float32)
    query_heads = split_heads(
        (projected[:, :model_width] + offset_rows[2]).astype(jnp.bfloat16), clip_count
    )
    key_heads = split_heads(
        projected[:, model_width : 2 * model_width].astype(jnp.bfloat16), clip_count
    )
    value_heads = split_heads(
        (projected[:, 2 * model_width :] + offset_rows[3]).astype(jnp.bfloat16), clip_count
    )
    scores = (
        jnp.einsum("clhe,cmhe->chlm", query_heads, key_heads, preferred_element_type=jnp.float32)
        * score_scale
    )
    row_peak = jnp.max(scores, axis=-1, keepdims=True)
    exponent = jnp.exp(scores - row_peak)
    row_total = jnp.sum(exponent, axis=-1, keepdims=True)
    probability = (exponent / row_total).astype(jnp.bfloat16)
    log_total = (row_peak + jnp.log(row_total))[..., 0]
    attended = jnp.einsum(
        "chlm,cmhe->clhe", probability, value_heads, preferred_element_type=jnp.float32
    )
    attended = attended.reshape(row_count, model_width).astype(jnp.bfloat16)
    middle = (
        hidden
        + jnp.dot(attended, merge_weight, preferred_element_type=jnp.float32)
        + offset_rows[4]
    )
    normed_two = normalize(middle, gain_rows[1], offset_rows[1]).astype(jnp.bfloat16)
    raised = jnp.dot(normed_two, up_weight, preferred_element_type=jnp.float32) + up_bias.astype(
        jnp.float32
    )
    activated = gelu_exact(raised).astype(jnp.bfloat16)
    result = (
        middle
        + jnp.dot(activated, down_weight, preferred_element_type=jnp.float32)
        + offset_rows[5]
    )
    saved_state = (
        hidden,
        normed,
        query_heads,
        key_heads,
        value_heads,
        log_total,
        attended,
        middle,
        normed_two,
        raised,
        activated,
    )
    return (result, saved_state)


def layer_backward(out_grad, saved_state, weights, clip_count):
    attend_weight, merge_weight, up_weight, down_weight, gain_rows, offset_rows, up_bias = weights
    gain_rows = gain_rows.astype(jnp.float32)
    offset_rows = offset_rows.astype(jnp.float32)
    (
        hidden,
        normed,
        query_heads,
        key_heads,
        value_heads,
        log_total,
        attended,
        middle,
        normed_two,
        raised,
        activated,
    ) = saved_state
    row_count, model_width = hidden.shape
    score_scale = HEAD_DIM ** (-0.5)
    low_grad = out_grad.astype(jnp.bfloat16)
    down_term = jnp.einsum("tf,td->fd", activated, low_grad, preferred_element_type=jnp.float32)
    last_bias = jnp.sum(out_grad, axis=0)
    act_grad = jnp.einsum("td,fd->tf", low_grad, down_weight, preferred_element_type=jnp.float32)
    raised_grad = jax.vjp(gelu_exact, raised)[1](act_grad)[0]
    up_bias_term = jnp.sum(raised_grad, axis=0)
    raised_low = raised_grad.astype(jnp.bfloat16)
    up_term = jnp.einsum("td,tf->df", normed_two, raised_low, preferred_element_type=jnp.float32)
    normed_two_grad = jnp.einsum(
        "tf,df->td", raised_low, up_weight, preferred_element_type=jnp.float32
    )
    second_back = jax.vjp(normalize, middle, gain_rows[1], offset_rows[1])[1]
    middle_part, gain_two, offset_two = second_back(normed_two_grad)
    middle_grad = out_grad + middle_part
    merge_bias = jnp.sum(middle_grad, axis=0)
    middle_low = middle_grad.astype(jnp.bfloat16)
    merge_term = jnp.einsum("td,te->de", attended, middle_low, preferred_element_type=jnp.float32)
    attended_grad = jnp.einsum(
        "te,de->td", middle_low, merge_weight, preferred_element_type=jnp.float32
    )
    attended_grad = split_heads(attended_grad.astype(jnp.bfloat16), clip_count)
    scores = (
        jnp.einsum("clhe,cmhe->chlm", query_heads, key_heads, preferred_element_type=jnp.float32)
        * score_scale
    )
    probability = jnp.exp(scores - log_total[..., None])
    prob_grad = jnp.einsum(
        "clhe,cmhe->chlm", attended_grad, value_heads, preferred_element_type=jnp.float32
    )
    value_grad = jnp.einsum(
        "chlm,clhe->cmhe",
        probability.astype(jnp.bfloat16),
        attended_grad,
        preferred_element_type=jnp.float32,
    )
    score_grad = probability * (
        prob_grad - jnp.sum(prob_grad * probability, axis=-1, keepdims=True)
    )
    score_grad = score_grad.astype(jnp.bfloat16)
    query_grad = (
        jnp.einsum("chlm,cmhe->clhe", score_grad, key_heads, preferred_element_type=jnp.float32)
        * score_scale
    )
    key_grad = (
        jnp.einsum("chlm,clhe->cmhe", score_grad, query_heads, preferred_element_type=jnp.float32)
        * score_scale
    )
    query_grad = query_grad.reshape(row_count, model_width)
    key_grad = key_grad.reshape(row_count, model_width)
    value_grad = value_grad.reshape(row_count, model_width)
    query_bias = jnp.sum(query_grad, axis=0)
    value_bias = jnp.sum(value_grad, axis=0)
    joined_low = jnp.concatenate([query_grad, key_grad, value_grad], axis=1).astype(jnp.bfloat16)
    attend_term = jnp.einsum("td,te->de", normed, joined_low, preferred_element_type=jnp.float32)
    normed_grad = jnp.einsum(
        "te,de->td", joined_low, attend_weight, preferred_element_type=jnp.float32
    )
    first_back = jax.vjp(normalize, hidden, gain_rows[0], offset_rows[0])[1]
    hidden_part, gain_one, offset_one = first_back(normed_grad)
    hidden_grad = middle_grad + hidden_part
    gain_term = jnp.stack([gain_one, gain_two])
    offset_term = jnp.stack([offset_one, offset_two, query_bias, value_bias, merge_bias, last_bias])
    return (
        hidden_grad,
        (attend_term, merge_term, up_term, down_term, gain_term, offset_term, up_bias_term),
    )


def plain_body(
    section_inputs,
    norm_gains,
    offsets,
    attend_weight,
    merge_weight,
    up_weight,
    up_bias,
    down_weight,
):
    shards = (attend_weight, merge_weight, up_weight, down_weight, norm_gains, offsets, up_bias)
    gathered = (
        lax.all_gather(shards[0], "fsdp", axis=1, tiled=True),
        lax.all_gather(shards[1], "fsdp", axis=1, tiled=True),
        lax.all_gather(shards[2], "fsdp", axis=1, tiled=True),
        lax.all_gather(shards[3], "fsdp", axis=1, tiled=True),
        lax.all_gather(shards[4], "fsdp", axis=2, tiled=True),
        lax.all_gather(shards[5], "fsdp", axis=2, tiled=True),
        lax.all_gather(shards[6], "fsdp", axis=1, tiled=True),
    )
    weights = tuple((tensor[0] for tensor in gathered))
    is_first = lax.axis_index("section") == 0
    own_data = section_inputs[0]
    batches, clip_count, length, model_width = own_data.shape
    row_count = clip_count * length
    own_rows = own_data.reshape(batches, row_count, model_width)
    kept_state = []
    upper_rows = []
    received = jnp.zeros((row_count, model_width), jnp.bfloat16)
    for instant in range(batches + 1):
        entering = jnp.where(is_first, own_rows[min(instant, batches - 1)], received)
        result, saved_state = layer_forward(entering.astype(jnp.float32), weights, clip_count)
        kept_state.append(saved_state)
        rounded = result.astype(jnp.bfloat16)
        if instant >= 1:
            upper_rows.append(rounded)
        if instant < batches:
            received = from_behind(rounded, "section", 1)
    gathered = (
        lax.all_gather(shards[0], "fsdp", axis=1, tiled=True),
        lax.all_gather(shards[1], "fsdp", axis=1, tiled=True),
        lax.all_gather(shards[2], "fsdp", axis=1, tiled=True),
        lax.all_gather(shards[3], "fsdp", axis=1, tiled=True),
        lax.all_gather(shards[4], "fsdp", axis=2, tiled=True),
        lax.all_gather(shards[5], "fsdp", axis=2, tiled=True),
        lax.all_gather(shards[6], "fsdp", axis=1, tiled=True),
    )
    weights = tuple((tensor[0] for tensor in gathered))
    totals = (
        jnp.zeros(weights[0].shape, jnp.float32),
        jnp.zeros(weights[1].shape, jnp.float32),
        jnp.zeros(weights[2].shape, jnp.float32),
        jnp.zeros(weights[3].shape, jnp.float32),
        jnp.zeros(weights[4].shape, jnp.float32),
        jnp.zeros(weights[5].shape, jnp.float32),
        jnp.zeros(weights[6].shape, jnp.float32),
    )
    received_grad = jnp.zeros((row_count, model_width), jnp.bfloat16)
    lower_rows = []
    for instant in range(batches + 1):
        position = batches - 1 - instant
        if position >= 0:
            own_grad = own_rows[position]
        else:
            own_grad = jnp.zeros((row_count, model_width), jnp.bfloat16)
        cotangent = jnp.where(is_first, received_grad, own_grad).astype(jnp.float32)
        hidden_grad, param_terms = layer_backward(
            cotangent, kept_state[batches - instant], weights, clip_count
        )
        totals = jax.tree.map(jnp.add, totals, param_terms)
        rounded = hidden_grad.astype(jnp.bfloat16)
        if instant >= 1:
            lower_rows.append(rounded)
        if instant < batches:
            received_grad = from_behind(rounded, "section", -1)
    ordered_lower = lower_rows[::-1]
    combined = jnp.stack(
        [
            jnp.where(is_first, lower_part, upper_part)
            for lower_part, upper_part in zip(ordered_lower, upper_rows)
        ]
    )
    section_outputs = combined.reshape(1, batches, clip_count, length, model_width)
    reduced = (
        lax.psum_scatter(totals[0][None], "fsdp", scatter_dimension=1, tiled=True),
        lax.psum_scatter(totals[1][None], "fsdp", scatter_dimension=1, tiled=True),
        lax.psum_scatter(totals[2][None], "fsdp", scatter_dimension=1, tiled=True),
        lax.psum_scatter(totals[3][None], "fsdp", scatter_dimension=1, tiled=True),
        lax.psum_scatter(totals[4][None], "fsdp", scatter_dimension=2, tiled=True),
        lax.psum_scatter(totals[5][None], "fsdp", scatter_dimension=2, tiled=True),
        lax.psum_scatter(totals[6][None], "fsdp", scatter_dimension=1, tiled=True),
    )
    return (
        section_outputs,
        reduced[4],
        reduced[5],
        reduced[0],
        reduced[1],
        reduced[2],
        reduced[6],
        reduced[3],
    )


def body(
    section_inputs,
    norm_gains,
    offsets,
    attend_weight,
    merge_weight,
    up_weight,
    up_bias,
    down_weight,
):
    ways = lax.axis_size("fsdp")
    if ways % 4 or attend_weight.shape[1] % 16:
        return plain_body(
            section_inputs,
            norm_gains,
            offsets,
            attend_weight,
            merge_weight,
            up_weight,
            up_bias,
            down_weight,
        )
    batches, clips, length, width = section_inputs.shape[1:]
    own = section_inputs.reshape(batches, clips * length, width)
    results = train_step(
        own,
        attend_weight[0],
        merge_weight[0],
        up_weight[0],
        down_weight[0],
        norm_gains[0],
        offsets[0],
        up_bias,
        clips,
        ways,
        1,
    )
    section_outputs, gains, shifts, attend, merge, up, bias, down = results
    return (
        section_outputs.reshape(section_inputs.shape),
        gains[None],
        shifts.swapaxes(0, 1),
        attend[None],
        merge[None],
        up[None],
        bias,
        down[None],
    )


def solution(mesh):
    return jax.shard_map(
        body,
        mesh=mesh,
        in_specs=(
            P("section", None, "fsdp", None, None),
            P("section", None, "fsdp"),
            P("section", None, "fsdp"),
            P("section", "fsdp", None),
            P("section", "fsdp", None),
            P("section", "fsdp", None),
            P("section", "fsdp"),
            P("section", "fsdp", None),
        ),
        out_specs=(
            P("section", None, "fsdp", None, None),
            P("section", None, "fsdp"),
            P("section", None, "fsdp"),
            P("section", "fsdp", None),
            P("section", "fsdp", None),
            P("section", "fsdp", None),
            P("section", "fsdp"),
            P("section", "fsdp", None),
        ),
        check_vma=False,
    )
```

```python
import functools
import math

import jax
import jax.numpy as jnp
from jax import lax
from jax.experimental import pallas as pl
from jax.experimental.pallas import tpu as pltpu
from jax.sharding import PartitionSpec as P

MESH = pl.DeviceIdType.MESH

HEADS = 12
HEAD_DIM = 64
epsilon = 1e-05
BF, F32 = jnp.bfloat16, jnp.float32
NT = (((1,), (1,)), ((), ()))
TN = (((0,), (0,)), ((), ()))

SIDE, ACROSS, UP, DOWN = range(4)
LEVELS_FIRST, ACROSS_FIRST = 0, 1

class Sends:
    def __init__(self):
        self.items = []

    def start(self, copy, when):
        if when is None:
            copy.start()
        else:
            pl.when(when)(copy.start)
        self.items.append((copy, when))

    def drain(self):
        for copy, when in self.items:
            if when is None:
                copy.wait_send()
            else:
                pl.when(when)(copy.wait_send)


def matmul(left, right, dims=(((1,), (0,)), ((), ()))):
    return lax.dot_general(left, right, dims, preferred_element_type=F32)


def standard(features):
    centred = features - jnp.mean(features, axis=-1, keepdims=True)
    scale = lax.rsqrt(jnp.mean(centred * centred, axis=-1, keepdims=True) + epsilon)
    return centred * scale, scale


def gelu_and_slope(raised):
    share = 0.5 + 0.5 * lax.erf(raised * math.sqrt(0.5))
    bell = jnp.exp(raised * raised * -0.5) * (1.0 / math.sqrt(2.0 * math.pi))
    return raised * share, share + raised * bell


def norm_back(upper, normal, scale):
    shift = jnp.mean(upper, axis=-1, keepdims=True)
    slope = jnp.mean(upper * normal, axis=-1, keepdims=True)
    return (upper - shift - normal * slope) * scale


def column_sum(values):
    return jnp.sum(values, axis=0, keepdims=True)


def pair_parts(matrix):
    lane = lax.broadcasted_iota(jnp.int32, matrix.shape, 1)
    zero = jnp.zeros_like(matrix)
    first = lane < HEAD_DIM
    return jnp.concatenate([jnp.where(first, matrix, zero), jnp.where(first, zero, matrix)], axis=0)


def pair_join(stacked):
    rows = stacked.shape[0] // 2
    lane = lax.broadcasted_iota(jnp.int32, (rows, stacked.shape[1]), 1)
    return jnp.where(lane < HEAD_DIM, stacked[:rows], stacked[rows:])


def halves(scores):
    keys = scores.shape[1] // 2
    return scores[:, :keys], scores[:, keys:]


class Place:
    def __init__(self, levels):
        self.levels = levels
        self.section, self.mine = lax.axis_index("section"), lax.axis_index("fsdp")
        self.level = lax.div(self.mine, 4)
        self.row = lax.rem(lax.div(self.mine, 2), 2)
        self.core = lax.rem(self.mine, 2)
        self.has_up, self.has_down = self.level < levels - 1, self.level > 0
        self.targets = {SIDE: self.mine ^ 1, ACROSS: self.mine ^ 2, UP: self.mine + 4, DOWN: self.mine - 4}

    def block(self, level, row, core):
        return level * 4 + row * 2 + core

    def greet(self):
        barrier = pltpu.get_barrier_semaphore()

        def hello(section, target):
            pl.semaphore_signal(barrier, inc=1, device_id=(section, target), device_id_type=MESH)

        hello(1 - self.section, self.mine)
        hello(self.section, self.targets[SIDE])
        hello(self.section, self.targets[ACROSS])
        pl.when(self.has_down)(lambda: hello(self.section, self.targets[DOWN]))
        pl.when(self.has_up)(lambda: hello(self.section, self.targets[UP]))
    def greeted(self):
        barrier = pltpu.get_barrier_semaphore()
        ends = (self.level == 0).astype(jnp.int32) + (self.level == self.levels - 1).astype(jnp.int32)
        pl.semaphore_wait(barrier, 5 - ends)


class Piece:
    def __init__(self, shard, ref, kind, start=0, size=None):
        self.shard, self.ref, self.plain = shard, ref, kind == "level"
        self.rows = None if size is None else pl.ds(start, size)

    def block(self, index):
        return self.ref.at[index] if self.rows is None else self.ref.at[index, self.rows]

    def span(self, count):
        return self.block(pl.ds(0, count))


class Gather:
    def __init__(self, place, pieces, send_sem, recv_sem, local_sem):
        self.place, self.pieces = place, pieces
        self.send_sem, self.recv_sem, self.local_sem = send_sem, recv_sem, local_sem
        self.side = 2 * place.levels

    def copy(self, source, target, out_sem, in_sem, way):
        return pltpu.make_async_remote_copy(
            src_ref=source,
            dst_ref=target,
            send_sem=out_sem,
            recv_sem=in_sem,
            device_id=(self.place.section, self.place.targets[way]),
            device_id_type=MESH,
        )

    def send(self, piece, level, row, way, own=False, when=None):
        held = self.pieces[piece]
        target = held.block(self.place.block(level, row, self.place.core))
        kind = {SIDE: 0, ACROSS: 1, UP: 2, DOWN: 2}[way]
        copy = self.copy(
            held.shard if own else target,
            target,
            self.send_sem.at[piece, kind],
            self.recv_sem.at[piece, self.side if way == SIDE else level * 2 + row],
            way,
        )
        if when is None:
            copy.start()
        else:
            pl.when(when)(copy.start)

    def arrived(self, piece, level, row, when=None):
        target = self.pieces[piece].block(self.place.block(level, row, self.place.core))
        index = level * 2 + row
        copy = self.copy(target, target, self.send_sem.at[piece, 0], self.recv_sem.at[piece, index], SIDE)
        if when is None:
            copy.wait_recv()
        else:
            pl.when(when)(copy.wait_recv)

    def local(self, piece):
        held = self.pieces[piece]
        return pltpu.make_async_copy(held.shard, held.block(self.place.mine), self.local_sem.at[piece])

    def start(self, piece):
        place = self.place
        self.send(piece, place.level, place.row, ACROSS, own=True)
        self.send(piece, place.level, place.row, UP, own=True, when=place.has_up)
        self.send(piece, place.level, place.row, DOWN, own=True, when=place.has_down)
        self.send(piece, place.level, place.row, SIDE, own=True)
        self.local(piece).start()

    def first_across(self, piece):
        place = self.place
        level, row = place.level, 1 - place.row
        self.arrived(piece, level, row)
        self.send(piece, level, row, UP, when=place.has_up)
        self.send(piece, level, row, DOWN, when=place.has_down)
        self.send(piece, level, row, SIDE)

    def from_levels(self, piece, distance):
        place = self.place
        plain = self.pieces[piece].plain
        for row in (place.row,) if plain else (place.row, 1 - place.row):
            for sign in (-1, 1):
                other = place.level + sign * distance
                here = other >= 0 if sign < 0 else other < place.levels
                onward = place.has_up if sign < 0 else place.has_down
                self.arrived(piece, other, row, here)
                if distance < place.levels - 1:
                    way = UP if sign < 0 else DOWN
                    self.send(piece, other, row, way, when=jnp.logical_and(here, onward))
                if plain:
                    self.send(piece, other, row, ACROSS, when=here)
                self.send(piece, other, row, SIDE, when=here)

    def from_across(self, piece, distance):
        place = self.place
        if not self.pieces[piece].plain:
            return
        for sign in (-1, 1) if distance else (1,):
            other = place.level + sign * distance
            here = None
            if distance:
                here = other >= 0 if sign < 0 else other < place.levels
            self.arrived(piece, other, 1 - place.row, here)
            self.send(piece, other, 1 - place.row, SIDE, when=here)

    def from_side(self, piece):
        self.local(piece).wait()
        span = self.pieces[piece].span(self.side)
        self.copy(span, span, self.send_sem.at[piece, 0], self.recv_sem.at[piece, self.side], SIDE).wait_recv()

    def drain(self, piece):
        place, held = self.place, self.pieces[piece]

        def sent(count, kind):
            span = held.span(count)
            return self.copy(span, span, self.send_sem.at[piece, kind], self.recv_sem.at[piece, 0], SIDE)

        rows = 1 if held.plain else 2
        sent(self.side, 0).wait_send()
        sent(place.levels if held.plain else 1, 1).wait_send()
        inner = jnp.logical_and(place.has_up, place.has_down)
        pl.when(inner)(sent(rows * (place.levels + 1), 2).wait_send)
        pl.when(jnp.logical_not(inner))(sent(rows, 2).wait_send)


class Chunk:
    def __init__(self, place, order, part, start, refs, sems):
        self.place, self.order, self.levels = place, order, place.levels
        self.whole, self.start = part, start
        self.from_side, self.from_across, self.from_chain = refs
        self.cols = self.from_side.shape[2]
        (
            self.side_out,
            self.side_in,
            self.across_out,
            self.across_in,
            self.chain_out,
            self.chain_in,
        ) = sems

    def part(self, block):
        return self.whole.at[block, :, pl.ds(self.start, self.cols)]

    def copy(self, block, target, out_sem, in_sem, way):
        return pltpu.make_async_remote_copy(
            src_ref=self.part(block),
            dst_ref=target,
            send_sem=out_sem,
            recv_sem=in_sem,
            device_id=(self.place.section, self.place.targets[way]),
            device_id_type=MESH,
        )

    def side(self, pair):
        block = pair * 2 + 1 - self.place.core
        return self.copy(
            block, self.from_side.at[pair], self.side_out, self.side_in.at[pair], SIDE
        )

    def across(self, level, slot):
        block = self.place.block(level, 1 - self.place.row, self.place.core)
        return self.copy(
            block,
            self.from_across.at[slot],
            self.across_out,
            self.across_in.at[slot],
            ACROSS,
        )

    def below_index(self, target, level):
        return target - level

    def above_index(self, target):
        return self.levels - target

    def up(self, row, slot, target):
        index = self.below_index(target, self.place.level + 1)
        return self.copy(
            self.place.block(target, row, self.place.core),
            self.from_chain.at[slot, index],
            self.chain_out.at[slot],
            self.chain_in.at[slot, index],
            UP,
        )

    def down(self, row, slot, target):
        index = self.above_index(target)
        return self.copy(
            self.place.block(target, row, self.place.core),
            self.from_chain.at[slot, index],
            self.chain_out.at[slot],
            self.chain_in.at[slot, index],
            DOWN,
        )

    def arrived(self, slot, index):
        target = self.from_chain.at[slot, index]
        pltpu.make_async_remote_copy(
            src_ref=target,
            dst_ref=target,
            send_sem=self.side_out,
            recv_sem=self.chain_in.at[slot, index],
            device_id=(self.place.section, self.place.targets[SIDE]),
            device_id_type=MESH,
        ).wait_recv()

    def add(self, block, term):
        part = self.part(block)
        part[...] = part[...] + term

    def send_side(self):
        @pl.loop(0, self.levels * 2)
        def _(pair):
            self.side(pair).start()

    def join_pair(self, level, row):
        pair = level * 2 + row
        self.side(pair).wait_recv()
        self.add(pair * 2 + self.place.core, self.from_side[pair])

    def level_at(self, index):
        return jnp.where(self.place.level < self.levels // 2, self.levels - 1 - index, index)

    def join_side(self):
        place = self.place
        for other in (True, False):
            row = 1 - place.row if other else place.row

            @pl.loop(0, self.levels)
            def _(index):
                level = self.level_at(index)
                self.join_pair(level, row)
                if other and self.order == ACROSS_FIRST:
                    self.across(level, level).start()

    def chain_open(self, row, slot, target):
        level, last = self.place.level, self.levels - 1
        pl.when(jnp.logical_and(level == 0, target > 0))(lambda: self.up(row, slot, target).start())
        pl.when(jnp.logical_and(level == last, target < last))(
            lambda: self.down(row, slot, target).start()
        )

    def join_across(self):
        place = self.place

        @pl.loop(0, self.levels)
        def _(index):
            level = self.level_at(index)
            self.across(level, level).wait_recv()
            self.add(place.block(level, place.row, place.core), self.from_across[level])
            self.chain_open(place.row, 0, level)

    def rows(self):
        row = self.place.row
        return ((0, row), (1, 1 - row)) if self.order == LEVELS_FIRST else ((0, row),)

    def chain_pass(self, distance):
        place, last = self.place, self.levels - 1
        for slot, row in self.rows():
            for target in range(last, distance, -1):

                @pl.when(place.level == distance)
                def _():
                    index = self.below_index(target, place.level)
                    self.arrived(slot, index)
                    self.add(place.block(target, row, place.core), self.from_chain[slot, index])
                    self.up(row, slot, target).start()

            for target in range(last - distance):

                @pl.when(place.level == last - distance)
                def _():
                    index = self.above_index(target)
                    self.arrived(slot, index)
                    self.add(place.block(target, row, place.core), self.from_chain[slot, index])
                    self.down(row, slot, target).start()

    def chain_end(self, out):
        place, last = self.place, self.levels - 1
        for slot, row in reversed(self.rows()):
            block = place.block(place.level, row, place.core)

            @pl.when(place.level > 0)
            def _():
                index = self.below_index(place.level, place.level)
                self.arrived(slot, index)
                self.add(block, self.from_chain[slot, index])

            @pl.when(place.level < last)
            def _():
                index = self.above_index(place.level)
                self.arrived(slot, index)
                self.add(block, self.from_chain[slot, index])

            if slot == 1:
                self.across(place.level, 0).start()
        if self.order == ACROSS_FIRST:
            out(self.part(place.mine)[...].astype(F32))

    def finish(self, out):
        if self.order == LEVELS_FIRST:
            self.across(self.place.level, 0).wait_recv()
            out(self.part(self.place.mine)[...].astype(F32) + self.from_across[0].astype(F32))

    def drain(self):
        def sent(span, out_sem):
            pltpu.make_async_remote_copy(
                src_ref=span,
                dst_ref=span,
                send_sem=out_sem,
                recv_sem=self.side_in.at[0],
                device_id=(self.place.section, self.place.targets[SIDE]),
                device_id_type=MESH,
            ).wait_send()

        sent(self.from_side, self.side_out)
        sent(self.from_across, self.across_out)
        for slot, _ in self.rows():
            sent(self.from_chain.at[slot, pl.ds(0, self.levels - 1)], self.chain_out.at[slot])


def chunk_scratch(levels, order, rows, cols, dtype, shared):
    block = (rows, cols)
    slots = 2 if order == LEVELS_FIRST else 1
    crossing = 1 if order == LEVELS_FIRST else levels
    dma = pltpu.SemaphoreType.DMA
    from_side = [] if shared else [pltpu.VMEM((levels * 2,) + block, dtype)]
    return from_side + [
        pltpu.VMEM((crossing,) + block, dtype),
        pltpu.VMEM((slots, levels + 1) + block, dtype),
        dma(()),
        dma((levels * 2,)),
        dma(()),
        dma((crossing,)),
        dma((slots,)),
        dma((slots, levels + 1)),
    ]


CHUNK_REFS = 8
STEP = 512


def pad_lanes(rows, lanes=128):
    missing = lanes - rows.shape[1]
    if not missing:
        return rows
    return jnp.concatenate([rows, jnp.zeros((rows.shape[0], missing), rows.dtype)], axis=1)


def tile_of(rows):
    missing = 8 - rows.shape[0]
    if not missing:
        return rows
    return jnp.concatenate([rows, jnp.zeros((missing, rows.shape[1]), rows.dtype)], axis=0)


def fold(line):
    pieces = [pad_lanes(line[:, at : at + 128]) for at in range(0, line.shape[1], 128)]
    return tile_of(jnp.concatenate(pieces, axis=0))


def unfold(rows, count):
    pieces = []
    for index in range(-(-count // 128)):
        pieces.append(rows[index : index + 1, : min(128, count - index * 128)])
    return jnp.concatenate(pieces, axis=1)


FOUR_LEVEL_STEPS = (
    (0, 1, 1), (4, 2, 0), (2, 2, 0), (4, 1, 1), (0, 1, 2), (2, 1, 1),
    (5, 0, 0), (1, 1, 1), (2, 1, 2), (0, 2, 0), (3, 1, 1), (4, 2, 1),
    (1, 1, 2), (3, 1, 2), (0, 1, 3), (0, 2, 1), (1, 1, 3), (5, 1, 1),
    (3, 2, 0), (1, 2, 0), (1, 2, 1), (3, 1, 3), (4, 1, 2), (0, 2, 2),
    (5, 1, 2), (3, 2, 1), (2, 1, 3), (4, 1, 3), (1, 2, 2), (0, 2, 3),
    (2, 2, 1), (2, 2, 2), (3, 2, 2), (1, 2, 3), (2, 2, 3), (3, 2, 3),
    (4, 2, 2), (5, 1, 3), (4, 2, 3),
)


def gather_steps(levels, count):
    if levels == 4 and count == 6:
        return FOUR_LEVEL_STEPS
    steps = [(count - 1, 0, 0)]
    for distance in range(1, levels):
        for piece in range(count):
            steps += [(piece, 1, distance), (piece, 2, distance - 1)]
    return steps + [(piece, 2, levels - 1) for piece in range(count)]


def relay_kernel(levels, clips, plan, *refs):
    own, attend_shard, merge_shard, up_shard, down_shard, gain_shard, shift_shard, bias_shard = refs[:8]
    out, gain_out, shift_out, attend_out, merge_out, up_out, bias_out, down_out = refs[8:16]
    (
        packed,
        vector_blocks,
        attend_blocks,
        merge_blocks,
        up_blocks,
        down_blocks,
        vectors,
        bias,
        vector_sum,
        bias_sum,
        entry,
        projected,
        probability,
        normed,
        attended,
        middle,
        normed_two,
        activated,
        slope,
        leaving,
        low_temp,
        temp,
        sum_temp,
        gather_send,
        gather_recv,
        gather_local,
        load_sem,
        send_sem,
        recv_sem,
        out_sem,
        free_sem,
        store_sem,
    ) = refs[16:48]
    chunk_refs = list(refs[48:])
    place = Place(levels)
    section, mine = place.section, place.mine
    batches, rows, width = own.shape
    wide = up_shard.shape[1]
    ways = levels * 4
    share, wide_share = width // ways, wide // ways
    length = rows // clips
    pairs = HEADS // 2
    total = batches * rows

    place.greet()
    load_own = pltpu.make_async_copy(own, entry.at[0], load_sem)
    load_own.start()
    packed[0:8] = pad_lanes(
        jnp.concatenate([gain_shard[...], shift_shard[...]], axis=0).astype(F32)
    )
    packed[8:16] = fold(bias_shard[...].astype(F32))
    place.greeted()

    half_share = wide_share // 2
    pieces = [
        Piece(packed, vector_blocks, "level"),
        Piece(attend_shard, attend_blocks, "level"),
        Piece(merge_shard, merge_blocks, "level"),
        Piece(up_shard, up_blocks, "level"),
        Piece(down_shard.at[pl.ds(0, half_share)], down_blocks, "level", 0, half_share),
        Piece(down_shard.at[pl.ds(half_share, half_share)], down_blocks, "across", half_share, half_share),
    ]
    gather = Gather(place, pieces, gather_send, gather_recv, gather_local)
    def flat(blocks):
        return blocks.reshape(-1, blocks.shape[-1])

    half = rows // 2 if clips % 2 == 0 else rows
    portions = rows // half

    def relay_part(batch, portion, slot=0):
        here = pl.ds(portion * half, half)
        return pltpu.make_async_remote_copy(
            src_ref=leaving.at[slot, here],
            dst_ref=entry.at[1, batch, here],
            send_sem=send_sem.at[batch, portion],
            recv_sem=recv_sem.at[batch, portion],
            device_id=(1 - section, mine),
            device_id_type=MESH,
        )

    class Relay:
        def __init__(self, batch, slot=0):
            self.copies = [relay_part(batch, portion, slot) for portion in range(portions)]

        def start(self):
            for copy in self.copies:
                copy.start()

        def wait_send(self):
            for copy in self.copies:
                copy.wait_send()

        def wait_recv(self):
            for copy in self.copies:
                copy.wait_recv()

    relay = Relay

    def keep(batch, slot=0):
        return pltpu.make_async_copy(leaving.at[slot], out.at[batch], out_sem.at[batch])

    vector_sum[...] = jnp.zeros_like(vector_sum)
    bias_sum[...] = jnp.zeros_like(bias_sum)
    fed, back = section, 1 - section

    def row(index):
        return vectors[index : index + 1, :]

    def chances(batch, start, pair):
        at = pl.multiple_of(batch * 4 * length + (pair % 2) * 2 * length, 128)
        first = start * (pairs // 2) + (pair // 2) * length
        return probability.at[pl.ds(first, length), pl.ds(at, 2 * length)]

    def attend_part(batch, start, size):
        here = pl.ds(start, size)
        normal, _ = standard(entry[fed, batch, here].astype(F32))
        normed[batch, here] = (normal * row(0) + row(2)).astype(BF)
        for part, shift in ((0, 4), (1, None), (2, 5)):
            at = slice(part * width, (part + 1) * width)
            value = matmul(normed[batch, here], flat(attend_blocks[:, :, at]))
            if shift is not None:
                value = value + row(shift)
            projected[batch, here, at] = value.astype(BF)
        for clip in range(size // length):
            span = pl.ds(start + clip * length, length)
            for pair in range(pairs):
                lanes = [slice(p * width + pair * 128, p * width + pair * 128 + 128) for p in range(3)]
                query = projected[batch, span, lanes[0]] * jnp.asarray(HEAD_DIM**-0.5, BF)
                key = pair_parts(projected[batch, span, lanes[1]])
                scores = matmul(query, key, NT)
                parts = []
                for half in halves(scores):
                    exponent = jnp.exp(half - jnp.max(half, axis=-1, keepdims=True))
                    parts.append(exponent * (1.0 / jnp.sum(exponent, axis=-1, keepdims=True)))
                weight = jnp.concatenate(parts, axis=1).astype(BF)
                chances(batch, start + clip * length, pair)[...] = weight
                value = pair_parts(projected[batch, span, lanes[2]])
                attended[batch, span, lanes[0]] = matmul(weight, value).astype(BF)
        joined = matmul(attended[batch, here], flat(merge_blocks[...])) + row(6)
        temp[here] = entry[fed, batch, here].astype(F32) + joined
        middle[batch, here] = temp[here].astype(BF)
        normal, _ = standard(temp[here])
        normed_two[batch, here] = (normal * row(1) + row(3)).astype(BF)

    def rise_part(batch, start, size):
        here = pl.ds(start, size)
        tile = 256
        for first in range(0, wide, tile):
            at = slice(first, first + tile)
            value, rate = gelu_and_slope(
                matmul(normed_two[batch, here], flat(up_blocks[:, :, at])) + bias[:, at]
            )
            activated[batch, here, at] = value.astype(BF)
            slope[batch, here, at] = rate.astype(BF)

    def fall_part(batch, start, size, slot):
        here = pl.ds(start, size)
        result = temp[here] + matmul(activated[batch, here], flat(down_blocks[...])) + row(7)
        leaving[slot, here] = result.astype(BF)

    def forward(batch, start, size, slot):
        attend_part(batch, start, size)
        rise_part(batch, start, size)
        fall_part(batch, start, size, slot)

    def backward(batch, start, size, slot):
        here = pl.ds(start, size)
        low = entry[back, batch, here]
        vector_sum[7:8] += column_sum(low.astype(F32))
        blocks = 4
        for block in range(0, ways, blocks):
            at = slice(block * wide_share, (block + blocks) * wide_share)
            rate = matmul(low, flat(down_blocks[block : block + blocks]), NT)
            rate = rate * slope[batch, here, at].astype(F32)
            bias_sum[:, at] += column_sum(rate)
            slope[batch, here, at] = rate.astype(BF)
        temp[here] = matmul(slope[batch, here], flat(up_blocks[...]), NT)
        normal, scale = standard(middle[batch, here].astype(F32))
        grad = temp[here]
        vector_sum[1:2] += column_sum(grad * normal)
        vector_sum[3:4] += column_sum(grad)
        grad = entry[back, batch, here].astype(F32) + norm_back(grad * row(1), normal, scale)
        sum_temp[here] = grad
        vector_sum[6:7] += column_sum(grad)
        middle[batch, here] = grad.astype(BF)
        low_temp[here] = matmul(middle[batch, here], flat(merge_blocks[...]), NT).astype(BF)
        for clip in range(size // length):
            span = pl.ds(start + clip * length, length)
            for pair in range(pairs):
                lanes = [slice(p * width + pair * 128, p * width + pair * 128 + 128) for p in range(3)]
                query = projected[batch, span, lanes[0]]
                key = pair_parts(projected[batch, span, lanes[1]])
                value = pair_parts(projected[batch, span, lanes[2]])
                upper = low_temp[span, lanes[0]]
                weight = chances(batch, start + clip * length, pair)[...]
                rise = matmul(upper, value, NT)
                value_grad = pair_join(matmul(weight, upper, TN))
                parts = []
                for part, heavy in zip(halves(rise), halves(weight)):
                    heavy = heavy.astype(F32)
                    mean = jnp.sum(part * heavy, axis=-1, keepdims=True)
                    parts.append(heavy * (part - mean) * HEAD_DIM**-0.5)
                change = jnp.concatenate(parts, axis=1).astype(BF)
                query_grad = matmul(change, key)
                key_grad = pair_join(matmul(change, query, TN))
                vector_sum[4:5, lanes[0]] += column_sum(query_grad)
                vector_sum[5:6, lanes[0]] += column_sum(value_grad)
                for at, piece in zip(lanes, (query_grad, key_grad, value_grad)):
                    projected[batch, span, at] = piece.astype(BF)
        temp[here] = matmul(projected[batch, here], flat(attend_blocks[...]), NT)
        normal, scale = standard(entry[fed, batch, here].astype(F32))
        grad = temp[here]
        vector_sum[0:1] += column_sum(grad * normal)
        vector_sum[2:3] += column_sum(grad)
        leaving[slot, here] = (sum_temp[here] + norm_back(grad * row(0), normal, scale)).astype(BF)

    count = len(pieces)
    for piece in range(count):
        gather.start(piece)
    for piece, what, distance in gather_steps(levels, count):
        if what == 0:
            gather.first_across(piece)
        elif what == 1:
            gather.from_levels(piece, distance)
        else:
            gather.from_across(piece, distance)
    for piece in range(count):
        gather.from_side(piece)
    vectors[...] = jnp.concatenate([vector_blocks[block, 0:8, 0:share] for block in range(ways)], axis=1)
    bias[...] = jnp.concatenate(
        [unfold(vector_blocks[block, 8:16], wide_share) for block in range(ways)], axis=1
    )
    load_own.wait()
    for piece in range(count):
        gather.drain(piece)

    chunks = []
    part_refs = [vector_blocks, attend_blocks, merge_blocks, up_blocks, down_blocks]
    for which, start, order, _, cols, _, shared in plan:
        if shared is None:
            from_side = chunk_refs.pop(0)
        else:
            from_side = chunks[shared].from_side.at[:, :, pl.ds(0, cols)]
        held, chunk_refs = chunk_refs[:CHUNK_REFS], chunk_refs[CHUNK_REFS:]
        chunks.append(Chunk(place, order, part_refs[which], start, [from_side] + held[:2], held[2:]))
    down_a, down_b, up_a, up_b, attend_a, attend_b, merge, vector = chunks

    def down_gradient():
        def pair_at(index):
            late = lax.div(index, levels)
            level = down_a.level_at(lax.rem(index, levels))
            return level, jnp.where(late == 0, 1 - place.row, place.row), late == 0

        def multiply(index):
            level, row, _ = pair_at(index)
            pair = level * 2 + row
            at = pl.ds(pl.multiple_of(pair * 2 * wide_share, 128), 2 * wide_share)
            tile = flat(activated[:, :, at])
            product = matmul(tile, flat(entry[back]), TN).astype(BF)
            for core in range(2):
                down_blocks[pair * 2 + core] = product[core * wide_share : (core + 1) * wide_share]
            for chunk in (down_b, down_a):
                chunk.side(pair).start()

        def join(index):
            level, row, early = pair_at(index)
            down_b.join_pair(level, row)
            pl.when(early)(down_b.across(level, level).start)
            down_a.join_pair(level, row)
            down_a.chain_open(row, jnp.where(early, 1, 0), level)

        multiply(jnp.int32(0))

        @pl.loop(1, 2 * levels)
        def _(index):
            multiply(index)
            join(index - 1)

        join(jnp.int32(2 * levels - 1))

    stores = []

    def store(target, chunk, through=None, first=0):
        def put(value):
            if through is None:
                target[:, pl.ds(chunk.start, chunk.cols)] = value
                return
            done = 0
            while done < chunk.cols:
                column = chunk.start + done
                size = min(width - column % width, chunk.cols - done)
                at = (pl.ds(first + column // width * share, share), pl.ds(column % width, size))
                through[at] = value[:, done : done + size]
                copy = pltpu.make_async_copy(
                    through.at[at], target.at[:, pl.ds(column, size)], store_sem.at[len(stores)]
                )
                copy.start()
                stores.append(copy)
                done += size

        return put

    def turn(source, place_at):
        target = probability.at[pl.ds(0, width), pl.ds(place_at * total, total)]
        target[...] = flat(source[...]).T
        return target

    def columns(left, source, chunk, credit=None):
        step = STEP if chunk.cols % STEP == 0 else chunk.cols

        @pl.loop(0, chunk.cols // step)
        def _(index):
            at = pl.multiple_of(chunk.start + index * step, 128)
            product = matmul(left[...], flat(source[:, :, pl.ds(at, step)]))
            chunk.whole[:, :, pl.ds(at, step)] = product.astype(BF).reshape(ways, width // ways, step)

        if credit is not None:
            pl.semaphore_wait(free_sem.at[credit], 1)
        chunk.send_side()

    def release(index):
        pl.semaphore_signal(
            free_sem.at[index], inc=1, device_id=(section, place.targets[SIDE]), device_id_type=MESH
        )

    @pl.loop(0, portions)
    def _(portion):
        pl.when(section == 1)(relay_part(0, portion).wait_recv)
        forward(0, pl.multiple_of(portion * half, length), half, 0)
        pl.when(section == 0)(relay_part(0, portion).start)

    pl.when(section == 1)(keep(0).start)

    @pl.loop(1, 2 * batches)
    def _(step):
        is_forward = jnp.where(section == 0, step < batches, lax.rem(step, 2) == 0)
        batch = jnp.where(section == 0, lax.rem(step, batches), lax.div(step, 2))
        slot = jnp.where(section == 0, lax.rem(batch, 2), jnp.where(is_forward, 0, 1))

        def when(*conditions):
            return pl.when(functools.reduce(jnp.logical_and, conditions))

        @pl.when(is_forward)
        def _():
            pl.when(section == 1)(lambda: relay(batch).wait_recv())
            when(section == 0, batch >= 2)(lambda: relay(batch - 2).wait_send())
            pl.when(section == 1)(lambda: keep(batch - 1).wait())
            forward(batch, 0, rows, slot)
            pl.when(section == 0)(lambda: relay(batch, slot).start())
            pl.when(section == 1)(lambda: keep(batch, slot).start())

        @pl.when(jnp.logical_not(is_forward))
        def _():
            pl.when(section == 0)(lambda: relay(batch).wait_recv())
            when(section == 0, batch < 2)(lambda: relay(batch + batches - 2).wait_send())
            when(section == 0, batch >= 2)(lambda: keep(batch - 2).wait())
            when(section == 1, batch >= 1)(lambda: relay(batch - 1).wait_send())
            backward(batch, 0, rows, slot)
            pl.when(section == 1)(lambda: relay(batch, slot).start())
            pl.when(section == 0)(lambda: keep(batch, slot).start())

    down_gradient()

    for block in range(ways):
        vector_blocks[block, 0:8] = pad_lanes(vector_sum[:, block * share : (block + 1) * share])
        vector_blocks[block, 8:16] = fold(bias_sum[:, block * wide_share : (block + 1) * wide_share])
    vector.send_side()

    def store_vectors(value):
        gain_out[...] = value[0:2, :share]
        for index in range(6):
            shift_out[index] = value[2 + index : 3 + index, :share]
        bias_out[...] = unfold(value[8:16], wide_share)

    turned_up = turn(normed_two, 0)
    columns(turned_up, slope, up_a)
    up_a.join_side()
    release(0)
    columns(turned_up, slope, up_b)
    down_a.chain_pass(1)
    vector.join_side()
    down_b.join_across()
    turned_attend = turn(normed, 1)
    columns(turned_attend, projected, attend_a, 0)
    up_b.join_side()
    release(1)
    up_a.join_across()
    vector.join_across()
    down_a.chain_pass(2)
    down_b.chain_pass(1)
    attend_a.join_side()
    release(2)
    columns(turned_attend, projected, attend_b, 1)
    turned_merge = turn(attended, 0)
    columns(turned_merge, middle, merge, 2)
    attend_b.join_side()
    up_a.chain_pass(1)
    merge.join_side()
    up_b.join_across()
    up_a.chain_pass(2)
    down_b.chain_pass(2)
    vector.chain_pass(1)
    down_a.chain_end(None)
    up_b.chain_pass(1)
    up_b.chain_pass(2)
    vector.chain_pass(2)
    attend_a.join_across()
    attend_a.chain_pass(1)
    attend_b.join_across()
    up_b.chain_end(store(up_out, up_b, temp, 0))
    attend_b.chain_pass(1)
    down_b.chain_end(store(down_out, down_b))
    vector.chain_end(store_vectors)
    attend_a.chain_pass(2)
    attend_b.chain_pass(2)
    merge.join_across()
    merge.chain_pass(1)
    up_a.chain_end(store(up_out, up_a, temp, 0))
    attend_a.chain_end(store(attend_out, attend_a, sum_temp, 0))
    merge.chain_pass(2)
    down_a.finish(store(down_out, down_a))
    attend_b.chain_end(store(attend_out, attend_b, sum_temp, 0))
    merge.chain_end(store(merge_out, merge, sum_temp, 3 * share))
    for chunk in chunks:
        chunk.drain()

    for copy in stores:
        copy.wait()

    @pl.when(section == 0)
    def _():
        keep(batches - 2).wait()
        keep(batches - 1).wait()

    @pl.when(section == 1)
    def _():
        keep(batches - 1).wait()
        relay(batches - 1).wait_send()


def settle_kernel(*refs):
    count = (len(refs) - 2) // 3
    load_sem, store_sem = refs[-2:]
    sources, targets, held = refs[:count], refs[count : 2 * count], refs[2 * count : 3 * count]
    loads = [pltpu.make_async_copy(sources[i], held[i], load_sem.at[i]) for i in range(count)]
    stores = [pltpu.make_async_copy(held[i], targets[i], store_sem.at[i]) for i in range(count)]
    for copy in loads:
        copy.start()
    for load, store in zip(loads, stores):
        load.wait()
        store.start()
    for copy in stores:
        copy.wait()


def train_step(own, attend, merge, up, down, gains, shifts, bias, clips, ways, collective_id):
    levels = ways // 4
    batches, rows, width = own.shape
    wide = up.shape[1]
    share, wide_share = width // ways, wide // ways
    length = rows // clips
    plan = [
        (4, 0, LEVELS_FIRST, wide_share, width // 2, BF, None),
        (4, width // 2, ACROSS_FIRST, wide_share, width // 2, BF, None),
        (3, 0, ACROSS_FIRST, share, wide // 2, BF, None),
        (3, wide // 2, ACROSS_FIRST, share, wide // 2, BF, None),
        (1, 0, ACROSS_FIRST, share, 2 * width, BF, 2),
        (1, 2 * width, ACROSS_FIRST, share, width, BF, 3),
        (2, 0, ACROSS_FIRST, share, width, BF, 2),
        (0, 0, ACROSS_FIRST, 16, 128, F32, None),
    ]
    dma = pltpu.SemaphoreType.DMA
    vmem, anywhere = pl.BlockSpec(memory_space=pltpu.VMEM), pl.BlockSpec(memory_space=pl.ANY)

    def held(cols, dtype=BF):
        return pltpu.VMEM((batches, rows, cols), dtype)

    scratch = [
        pltpu.VMEM((16, 128), F32),
        pltpu.VMEM((ways, 16, 128), F32),
        pltpu.VMEM((ways, share, 3 * width), BF),
        pltpu.VMEM((ways, share, width), BF),
        pltpu.VMEM((ways, share, wide), BF),
        pltpu.VMEM((ways, wide_share, width), BF),
        pltpu.VMEM((8, width), F32),
        pltpu.VMEM((1, wide), F32),
        pltpu.VMEM((8, width), F32),
        pltpu.VMEM((1, wide), F32),
        pltpu.VMEM((2, batches, rows, width), BF),
        held(3 * width),
        pltpu.VMEM((clips * HEADS // 4 * length, batches * 4 * length), BF),
        held(width),
        held(width),
        held(width),
        held(width),
        held(wide),
        held(wide),
        pltpu.VMEM((2, rows, width), BF),
        pltpu.VMEM((rows, width), BF),
        pltpu.VMEM((rows, width), F32),
        pltpu.VMEM((rows, width), F32),
        dma((6, 3)),
        dma((6, 2 * levels + 1)),
        dma((6,)),
        dma(()),
        dma((batches, 2)),
        dma((batches, 2)),
        dma((batches,)),
        pltpu.SemaphoreType.REGULAR((3,)),
        dma((9,)),
    ]
    for _, _, order, chunk_rows, cols, dtype, shared in plan:
        scratch += chunk_scratch(levels, order, chunk_rows, cols, dtype, shared is not None)

    def grad(*shape):
        return jax.ShapeDtypeStruct(shape, F32)

    results = pl.pallas_call(
        functools.partial(relay_kernel, levels, clips, plan),
        out_shape=[
            jax.ShapeDtypeStruct(own.shape, BF),
            grad(2, share),
            grad(6, 1, share),
            grad(share, 3 * width),
            grad(share, width),
            grad(share, wide),
            grad(1, wide_share),
            grad(wide_share, width),
        ],
        in_specs=[anywhere] * 5 + [vmem] * 3,
        out_specs=[anywhere, vmem, vmem, anywhere, anywhere, anywhere, vmem, vmem],
        scratch_shapes=scratch,
        compiler_params=pltpu.CompilerParams(
            collective_id=collective_id, has_side_effects=True, vmem_limit_bytes=62 * 2**20
        ),
    )(own, attend, merge, up, down, gains, shifts, bias)
    return pl.pallas_call(
        settle_kernel,
        out_shape=[jax.ShapeDtypeStruct(result.shape, result.dtype) for result in results],
        in_specs=[anywhere] * len(results),
        out_specs=[anywhere] * len(results),
        scratch_shapes=[pltpu.VMEM(result.shape, result.dtype) for result in results]
        + [dma((len(results),))] * 2,
    )(*results)


def from_behind(block, axis, distance):
    devices = range(lax.axis_size(axis))
    route = [(i - distance, i) for i in devices if i - distance in devices]
    return lax.ppermute(block, axis, route)


def normalize(features, gain_row, offset):
    centred = features - jnp.mean(features, axis=-1, keepdims=True)
    spread = jnp.mean(centred * centred, axis=-1, keepdims=True)
    return centred * lax.rsqrt(spread + epsilon) * gain_row + offset


def gelu_exact(features):
    return jax.nn.gelu(features, approximate=False)


def split_heads(matrix, clip_count):
    return matrix.reshape(clip_count, matrix.shape[0] // clip_count, HEADS, HEAD_DIM)


def layer_forward(hidden, weights, clip_count):
    attend_weight, merge_weight, up_weight, down_weight, gain_rows, offset_rows, up_bias = weights
    gain_rows = gain_rows.astype(jnp.float32)
    offset_rows = offset_rows.astype(jnp.float32)
    row_count, model_width = hidden.shape
    score_scale = HEAD_DIM ** (-0.5)
    normed = normalize(hidden, gain_rows[0], offset_rows[0]).astype(jnp.bfloat16)
    projected = jnp.dot(normed, attend_weight, preferred_element_type=jnp.float32)
    query_heads = split_heads(
        (projected[:, :model_width] + offset_rows[2]).astype(jnp.bfloat16), clip_count
    )
    key_heads = split_heads(
        projected[:, model_width : 2 * model_width].astype(jnp.bfloat16), clip_count
    )
    value_heads = split_heads(
        (projected[:, 2 * model_width :] + offset_rows[3]).astype(jnp.bfloat16), clip_count
    )
    scores = (
        jnp.einsum("clhe,cmhe->chlm", query_heads, key_heads, preferred_element_type=jnp.float32)
        * score_scale
    )
    row_peak = jnp.max(scores, axis=-1, keepdims=True)
    exponent = jnp.exp(scores - row_peak)
    row_total = jnp.sum(exponent, axis=-1, keepdims=True)
    probability = (exponent / row_total).astype(jnp.bfloat16)
    log_total = (row_peak + jnp.log(row_total))[..., 0]
    attended = jnp.einsum(
        "chlm,cmhe->clhe", probability, value_heads, preferred_element_type=jnp.float32
    )
    attended = attended.reshape(row_count, model_width).astype(jnp.bfloat16)
    middle = (
        hidden
        + jnp.dot(attended, merge_weight, preferred_element_type=jnp.float32)
        + offset_rows[4]
    )
    normed_two = normalize(middle, gain_rows[1], offset_rows[1]).astype(jnp.bfloat16)
    raised = jnp.dot(normed_two, up_weight, preferred_element_type=jnp.float32) + up_bias.astype(
        jnp.float32
    )
    activated = gelu_exact(raised).astype(jnp.bfloat16)
    result = (
        middle
        + jnp.dot(activated, down_weight, preferred_element_type=jnp.float32)
        + offset_rows[5]
    )
    saved_state = (
        hidden,
        normed,
        query_heads,
        key_heads,
        value_heads,
        log_total,
        attended,
        middle,
        normed_two,
        raised,
        activated,
    )
    return (result, saved_state)


def layer_backward(out_grad, saved_state, weights, clip_count):
    attend_weight, merge_weight, up_weight, down_weight, gain_rows, offset_rows, up_bias = weights
    gain_rows = gain_rows.astype(jnp.float32)
    offset_rows = offset_rows.astype(jnp.float32)
    (
        hidden,
        normed,
        query_heads,
        key_heads,
        value_heads,
        log_total,
        attended,
        middle,
        normed_two,
        raised,
        activated,
    ) = saved_state
    row_count, model_width = hidden.shape
    score_scale = HEAD_DIM ** (-0.5)
    low_grad = out_grad.astype(jnp.bfloat16)
    down_term = jnp.einsum("tf,td->fd", activated, low_grad, preferred_element_type=jnp.float32)
    last_bias = jnp.sum(out_grad, axis=0)
    act_grad = jnp.einsum("td,fd->tf", low_grad, down_weight, preferred_element_type=jnp.float32)
    raised_grad = jax.vjp(gelu_exact, raised)[1](act_grad)[0]
    up_bias_term = jnp.sum(raised_grad, axis=0)
    raised_low = raised_grad.astype(jnp.bfloat16)
    up_term = jnp.einsum("td,tf->df", normed_two, raised_low, preferred_element_type=jnp.float32)
    normed_two_grad = jnp.einsum(
        "tf,df->td", raised_low, up_weight, preferred_element_type=jnp.float32
    )
    second_back = jax.vjp(normalize, middle, gain_rows[1], offset_rows[1])[1]
    middle_part, gain_two, offset_two = second_back(normed_two_grad)
    middle_grad = out_grad + middle_part
    merge_bias = jnp.sum(middle_grad, axis=0)
    middle_low = middle_grad.astype(jnp.bfloat16)
    merge_term = jnp.einsum("td,te->de", attended, middle_low, preferred_element_type=jnp.float32)
    attended_grad = jnp.einsum(
        "te,de->td", middle_low, merge_weight, preferred_element_type=jnp.float32
    )
    attended_grad = split_heads(attended_grad.astype(jnp.bfloat16), clip_count)
    scores = (
        jnp.einsum("clhe,cmhe->chlm", query_heads, key_heads, preferred_element_type=jnp.float32)
        * score_scale
    )
    probability = jnp.exp(scores - log_total[..., None])
    prob_grad = jnp.einsum(
        "clhe,cmhe->chlm", attended_grad, value_heads, preferred_element_type=jnp.float32
    )
    value_grad = jnp.einsum(
        "chlm,clhe->cmhe",
        probability.astype(jnp.bfloat16),
        attended_grad,
        preferred_element_type=jnp.float32,
    )
    score_grad = probability * (
        prob_grad - jnp.sum(prob_grad * probability, axis=-1, keepdims=True)
    )
    score_grad = score_grad.astype(jnp.bfloat16)
    query_grad = (
        jnp.einsum("chlm,cmhe->clhe", score_grad, key_heads, preferred_element_type=jnp.float32)
        * score_scale
    )
    key_grad = (
        jnp.einsum("chlm,clhe->cmhe", score_grad, query_heads, preferred_element_type=jnp.float32)
        * score_scale
    )
    query_grad = query_grad.reshape(row_count, model_width)
    key_grad = key_grad.reshape(row_count, model_width)
    value_grad = value_grad.reshape(row_count, model_width)
    query_bias = jnp.sum(query_grad, axis=0)
    value_bias = jnp.sum(value_grad, axis=0)
    joined_low = jnp.concatenate([query_grad, key_grad, value_grad], axis=1).astype(jnp.bfloat16)
    attend_term = jnp.einsum("td,te->de", normed, joined_low, preferred_element_type=jnp.float32)
    normed_grad = jnp.einsum(
        "te,de->td", joined_low, attend_weight, preferred_element_type=jnp.float32
    )
    first_back = jax.vjp(normalize, hidden, gain_rows[0], offset_rows[0])[1]
    hidden_part, gain_one, offset_one = first_back(normed_grad)
    hidden_grad = middle_grad + hidden_part
    gain_term = jnp.stack([gain_one, gain_two])
    offset_term = jnp.stack([offset_one, offset_two, query_bias, value_bias, merge_bias, last_bias])
    return (
        hidden_grad,
        (attend_term, merge_term, up_term, down_term, gain_term, offset_term, up_bias_term),
    )


def plain_body(
    section_inputs,
    norm_gains,
    offsets,
    attend_weight,
    merge_weight,
    up_weight,
    up_bias,
    down_weight,
):
    shards = (attend_weight, merge_weight, up_weight, down_weight, norm_gains, offsets, up_bias)
    gathered = (
        lax.all_gather(shards[0], "fsdp", axis=1, tiled=True),
        lax.all_gather(shards[1], "fsdp", axis=1, tiled=True),
        lax.all_gather(shards[2], "fsdp", axis=1, tiled=True),
        lax.all_gather(shards[3], "fsdp", axis=1, tiled=True),
        lax.all_gather(shards[4], "fsdp", axis=2, tiled=True),
        lax.all_gather(shards[5], "fsdp", axis=2, tiled=True),
        lax.all_gather(shards[6], "fsdp", axis=1, tiled=True),
    )
    weights = tuple((tensor[0] for tensor in gathered))
    is_first = lax.axis_index("section") == 0
    own_data = section_inputs[0]
    batches, clip_count, length, model_width = own_data.shape
    row_count = clip_count * length
    own_rows = own_data.reshape(batches, row_count, model_width)
    kept_state = []
    upper_rows = []
    received = jnp.zeros((row_count, model_width), jnp.bfloat16)
    for instant in range(batches + 1):
        entering = jnp.where(is_first, own_rows[min(instant, batches - 1)], received)
        result, saved_state = layer_forward(entering.astype(jnp.float32), weights, clip_count)
        kept_state.append(saved_state)
        rounded = result.astype(jnp.bfloat16)
        if instant >= 1:
            upper_rows.append(rounded)
        if instant < batches:
            received = from_behind(rounded, "section", 1)
    gathered = (
        lax.all_gather(shards[0], "fsdp", axis=1, tiled=True),
        lax.all_gather(shards[1], "fsdp", axis=1, tiled=True),
        lax.all_gather(shards[2], "fsdp", axis=1, tiled=True),
        lax.all_gather(shards[3], "fsdp", axis=1, tiled=True),
        lax.all_gather(shards[4], "fsdp", axis=2, tiled=True),
        lax.all_gather(shards[5], "fsdp", axis=2, tiled=True),
        lax.all_gather(shards[6], "fsdp", axis=1, tiled=True),
    )
    weights = tuple((tensor[0] for tensor in gathered))
    totals = (
        jnp.zeros(weights[0].shape, jnp.float32),
        jnp.zeros(weights[1].shape, jnp.float32),
        jnp.zeros(weights[2].shape, jnp.float32),
        jnp.zeros(weights[3].shape, jnp.float32),
        jnp.zeros(weights[4].shape, jnp.float32),
        jnp.zeros(weights[5].shape, jnp.float32),
        jnp.zeros(weights[6].shape, jnp.float32),
    )
    received_grad = jnp.zeros((row_count, model_width), jnp.bfloat16)
    lower_rows = []
    for instant in range(batches + 1):
        position = batches - 1 - instant
        if position >= 0:
            own_grad = own_rows[position]
        else:
            own_grad = jnp.zeros((row_count, model_width), jnp.bfloat16)
        cotangent = jnp.where(is_first, received_grad, own_grad).astype(jnp.float32)
        hidden_grad, param_terms = layer_backward(
            cotangent, kept_state[batches - instant], weights, clip_count
        )
        totals = jax.tree.map(jnp.add, totals, param_terms)
        rounded = hidden_grad.astype(jnp.bfloat16)
        if instant >= 1:
            lower_rows.append(rounded)
        if instant < batches:
            received_grad = from_behind(rounded, "section", -1)
    ordered_lower = lower_rows[::-1]
    combined = jnp.stack(
        [
            jnp.where(is_first, lower_part, upper_part)
            for lower_part, upper_part in zip(ordered_lower, upper_rows)
        ]
    )
    section_outputs = combined.reshape(1, batches, clip_count, length, model_width)
    reduced = (
        lax.psum_scatter(totals[0][None], "fsdp", scatter_dimension=1, tiled=True),
        lax.psum_scatter(totals[1][None], "fsdp", scatter_dimension=1, tiled=True),
        lax.psum_scatter(totals[2][None], "fsdp", scatter_dimension=1, tiled=True),
        lax.psum_scatter(totals[3][None], "fsdp", scatter_dimension=1, tiled=True),
        lax.psum_scatter(totals[4][None], "fsdp", scatter_dimension=2, tiled=True),
        lax.psum_scatter(totals[5][None], "fsdp", scatter_dimension=2, tiled=True),
        lax.psum_scatter(totals[6][None], "fsdp", scatter_dimension=1, tiled=True),
    )
    return (
        section_outputs,
        reduced[4],
        reduced[5],
        reduced[0],
        reduced[1],
        reduced[2],
        reduced[6],
        reduced[3],
    )


def body(
    section_inputs,
    norm_gains,
    offsets,
    attend_weight,
    merge_weight,
    up_weight,
    up_bias,
    down_weight,
):
    ways = lax.axis_size("fsdp")
    if ways % 4 or attend_weight.shape[1] % 16:
        return plain_body(
            section_inputs,
            norm_gains,
            offsets,
            attend_weight,
            merge_weight,
            up_weight,
            up_bias,
            down_weight,
        )
    batches, clips, length, width = section_inputs.shape[1:]
    own = section_inputs.reshape(batches, clips * length, width)
    results = train_step(
        own,
        attend_weight[0],
        merge_weight[0],
        up_weight[0],
        down_weight[0],
        norm_gains[0],
        offsets[0],
        up_bias,
        clips,
        ways,
        1,
    )
    section_outputs, gains, shifts, attend, merge, up, bias, down = results
    return (
        section_outputs.reshape(section_inputs.shape),
        gains[None],
        shifts.swapaxes(0, 1),
        attend[None],
        merge[None],
        up[None],
        bias,
        down[None],
    )


def solution(mesh):
    return jax.shard_map(
        body,
        mesh=mesh,
        in_specs=(
            P("section", None, "fsdp", None, None),
            P("section", None, "fsdp"),
            P("section", None, "fsdp"),
            P("section", "fsdp", None),
            P("section", "fsdp", None),
            P("section", "fsdp", None),
            P("section", "fsdp"),
            P("section", "fsdp", None),
        ),
        out_specs=(
            P("section", None, "fsdp", None, None),
            P("section", None, "fsdp"),
            P("section", None, "fsdp"),
            P("section", "fsdp", None),
            P("section", "fsdp", None),
            P("section", "fsdp", None),
            P("section", "fsdp"),
            P("section", "fsdp", None),
        ),
        check_vma=False,
    )
```
